128 devices in a mesh: lat: 8 (over x, core), lon: 16 (over y, z).
Axes of the slice: x: 4, y: 4, z: 4, core: 2. Of those that a mesh axis runs over, the one named last changes fastest.
Arguments:
- model_state: bfloat16 [256, 2048, 256], P('lat', 'lon'), may hold values from -6 to 6
- tangent_slope: bfloat16 [256, 2048, 256], P('lat', 'lon'), may hold values from 0.19921875 to 1.1953125
- conv_weight: bfloat16 [3, 3, 256, 256], replicated, may hold values from -0.125 to 0.125
- weight_in: bfloat16 [256, 512], replicated, may hold values from -0.375 to 0.375
- bias_in: float32 [512], replicated, may hold values from -3 to 3
- weight_mid: bfloat16 [512, 512], replicated, may hold values from -0.25 to 0.25
- bias_mid: float32 [512], replicated, may hold values from -3 to 3
- weight_out: bfloat16 [512, 384], replicated, may hold values from -0.25 to 0.25
- bias_out: float32 [384], replicated, may hold values from -3 to 3
- obs_tile: int32 [65536, 1], P(('lat', 'lon')), may hold values from 0 to 127; in each aligned block of 512 rows (0 to 511, 512 to 1023, ...) at most 8 rows name the same one
- obs_cell: int32 [65536], P(('lat', 'lon')), may hold values from 0 to 3966, as said below
- obs_frac: float32 [65536, 2], P(('lat', 'lon')), may hold values from 0 to 1
- radiance: bfloat16 [65536, 384], P(('lat', 'lon')), may hold values from -6 to 6
- inv_error: float32 [384], replicated, may hold values from 0.5 to 2
Outputs:
- departures: float32 [65536, 384], P(('lat', 'lon'))
- gradient: float32 [256, 2048, 256], P('lat', 'lon')
The draws below stay inside these ranges and needn't reach their ends.
Inputs may be any that keep to these rules, and one draw needn't show every extreme that they name: `obs_tile`: among the rows of one device, at most 8 name the same tile. `obs_cell`: row k // 128 is at most 30 and column k % 128 at most 126.
All inputs are finite; a program needn't handle non-finite values.
Results may differ from the reference program's by a relative error of at most 0.0078.
Values may be sent and summed in bfloat16 or wider, within the bound.
No kernel may reach another device: no remote copies, remote signals or barrier semaphores. Data moves between devices by JAX's collectives and lax.ppermute only.
A program may use at most 64 MiB of HBM per device.

```python
import math
import jax
import jax.numpy as jnp
import numpy as np
from jax import lax

CLAT = 32
CLON = 128
C = 256
HID = 512
NCHAN = 384
OBS_DEV = 512
CAP = 8
NLAT = 256
MERIDIAN_TOTAL = 2048
NOBS = 65536
N_LON = 16
DEVICES = 128


def draw_obs_cell(key, part):
    key = jax.random.fold_in(key, 7)
    first_key, second_key = jax.random.split(key)
    lat_row = jax.random.randint(first_key, (NOBS,), 0, CLAT - 1)
    lon_col = jax.random.randint(second_key, (NOBS,), 0, CLON - 1)
    cell_ids = lat_row * CLON + lon_col
    cell_ids = cell_ids.at[0].set((CLAT - 2) * CLON + CLON - 2).at[1].set(0)
    return cell_ids.astype(jnp.int32)


def steps_of(rng, extent, shards, smallest, top_value):
    def one(axis_at, shards_of):
        heights = jax.random.uniform(jax.random.fold_in(jax.random.fold_in(rng, 6), axis_at), (shards_of,), jnp.float32, smallest / len(shards), top_value / len(shards))
        return jnp.repeat(jnp.exp(heights), extent[axis_at] // shards_of).reshape((-1,) + (1,) * (len(extent) - axis_at - 1))

    gain = one(*shards[0])
    for cut in shards[1:]:
        gain = gain * one(*cut)
    return gain


def shared_out(rng, own, number, rows, count, top, limit, slope):
    ranking = jax.random.permutation(rng, count)
    heavy_load, ordinary = shares(count, rows * top, limit, slope, True), shares(count, rows * top, limit, slope, False)
    places = jnp.arange(count)

    def named(tallies, offset_by):
        used = int((tallies > 0).sum())
        fixed = max(1, used // 4)
        passed = fixed + (places - fixed + offset_by * (used - fixed)) % max(1, count - fixed)
        return jnp.zeros((count,), jnp.int32).at[ranking[jnp.where(places < fixed, places, passed)]].set(jnp.asarray(tallies, jnp.int32))

    tallies = jnp.where(number % 4 == 0, named(heavy_load, number // 4), named(ordinary, number - number // 4 - 1))
    mixed = jax.random.permutation(jax.random.fold_in(own, 3), count)
    source_of, sink = mixed[0:count // 2 * 2:2], mixed[1:count // 2 * 2:2]
    margin = jnp.minimum(tallies[source_of] - 1, limit - tallies[sink]) // 2
    margin = jnp.where((source_of == ranking[0]) | (sink == ranking[0]) | (tallies[sink] == 0), 0, jnp.maximum(margin, 0))
    passed = jax.random.randint(jax.random.fold_in(own, 4), (count // 2,), 0, 1 << 20) % (margin + 1)
    tallies = tallies.at[source_of].add(-passed).at[sink].add(passed)
    members = jnp.searchsorted(jnp.cumsum(tallies), jnp.arange(rows * top), side="right").astype(jnp.int32)
    listing = members.reshape(top, rows).T
    listing = listing[jax.random.permutation(jax.random.fold_in(own, 1), rows)]
    offset_by = jax.random.randint(jax.random.fold_in(own, 2), (rows, 1), 0, top)
    return jnp.take_along_axis(listing, (jnp.arange(top)[None, :] + offset_by) % top, axis=1)


def shares(count, total, reach, skew, full):
    weights = [(1 << 20) // math.isqrt(grade ** skew) + 1 for grade in range(1, count + 1)]
    largest = reach if full else min(reach, max(-(-total // count), total * weights[0] // sum(weights)))
    least = 1 if total - largest >= count - 1 else 0
    counts, spare = [largest] + [least] * (count - 1), total - largest - least * (count - 1)
    while spare > 0:
        free = [i for i in range(1, count) if counts[i] < largest] or [i for i in range(1, count) if counts[i] < reach]
        whole, remaining = sum([weights[i] for i in free]), spare
        for i in free:
            extra = min(reach - counts[i], max(1, remaining * weights[i] // whole), spare)
            counts[i] = counts[i] + extra
            spare = spare - extra
    return np.array(counts)


def bell_draw(rng, extent, scale, reach, pieces=(), dtype=jnp.bfloat16):
    values = scale * jax.random.normal(rng, extent, jnp.float32)
    if pieces:
        values = values * steps_of(rng, extent, pieces, -0.22, 0.18)
    return jnp.clip(values, -reach, reach).astype(dtype)


def setup_inputs(seed: int = 0) -> dict:
    key_list = jax.random.split(jax.random.key(seed), 15)
    model_state = bell_draw(key_list[0], (NLAT, MERIDIAN_TOTAL, C), 1.0, 6.0, ((0, 8), (1, 16)))
    tangent_slope = jnp.clip(0.19921875 + 0.99609375 * jax.random.uniform(key_list[1], (NLAT, MERIDIAN_TOTAL, C), jnp.float32) ** steps_of(key_list[1], (NLAT, MERIDIAN_TOTAL, C), ((0, 8), (1, 16)), -0.2, 0.2), 0.19921875, 1.1953125).astype(jnp.bfloat16)
    conv_weight = bell_draw(key_list[2], (3, 3, C, C), (9 * C) ** -0.5, 0.125)
    weight_in = bell_draw(key_list[3], (C, HID), C ** -0.5, 0.375)
    bias_in = bell_draw(key_list[4], (HID,), 0.5, 3.0, (), jnp.float32)
    weight_mid = bell_draw(key_list[5], (HID, HID), HID ** -0.5, 0.25)
    bias_mid = bell_draw(key_list[6], (HID,), 0.5, 3.0, (), jnp.float32)
    weight_out = bell_draw(key_list[7], (HID, NCHAN), HID ** -0.5, 0.25)
    bias_out = bell_draw(key_list[8], (NCHAN,), 0.5, 3.0, (), jnp.float32)
    obs_tile_keys = jax.random.split(jax.random.fold_in(key_list[9], 1), NOBS // OBS_DEV)
    obs_tile_turns = jax.random.permutation(jax.random.fold_in(key_list[9], 3), NOBS // OBS_DEV)
    obs_tile = jax.vmap(lambda own, number: shared_out(jax.random.fold_in(key_list[9], 2), own, number, OBS_DEV, DEVICES, 1, CAP, 2))(obs_tile_keys, obs_tile_turns).reshape((NOBS, 1))
    obs_cell = draw_obs_cell(jax.random.fold_in(key_list[14], 71), 0)
    obs_frac = jnp.clip(1.0 * jax.random.uniform(key_list[11], (NOBS, 2), jnp.float32) ** steps_of(key_list[11], (NOBS, 2), ((0, 128),), -0.2, 0.2), 0.0, 1.0)
    radiance = bell_draw(key_list[12], (NOBS, NCHAN), 1.0, 6.0, ((0, 128),))
    inv_error = jnp.clip(jnp.exp(jax.random.uniform(key_list[13], (NCHAN,), jnp.float32, math.log(0.5), math.log(2.0))), 0.5, 2.0)
    return {"model_state": model_state, "tangent_slope": tangent_slope, "conv_weight": conv_weight, "weight_in": weight_in, "bias_in": bias_in, "weight_mid": weight_mid, "bias_mid": bias_mid, "weight_out": weight_out, "bias_out": bias_out, "obs_tile": obs_tile, "obs_cell": obs_cell, "obs_frac": obs_frac, "radiance": radiance, "inv_error": inv_error}


def convolve(padded, conv_weight, mirror):
    lat_cells = padded.shape[0] - 2
    meridian_columns = padded.shape[1] - 2
    channels = padded.shape[2]
    summed = jnp.zeros((lat_cells * meridian_columns, conv_weight.shape[3]), jnp.float32)
    for row_step in range(3):
        for col_step in range(3):
            if mirror:
                window = padded[2 - row_step:2 - row_step + lat_cells, 2 - col_step:2 - col_step + meridian_columns]
                kernel = conv_weight[row_step, col_step].T
            else:
                window = padded[row_step:row_step + lat_cells, col_step:col_step + meridian_columns]
                kernel = conv_weight[row_step, col_step]
            summed = summed + jnp.dot(window.reshape(lat_cells * meridian_columns, channels), kernel, preferred_element_type=jnp.float32)
    return summed


def extend_grid(field):
    wrapped = jnp.concatenate([field[:, -1:], field, field[:, :1]], axis=1)
    return jnp.pad(wrapped, ((1, 1), (0, 0), (0, 0)))


def corner_weights(fraction):
    lat_part = fraction[:, 0:1]
    lon_part = fraction[:, 1:2]
    return jnp.concatenate([(1.0 - lat_part) * (1.0 - lon_part), (1.0 - lat_part) * lon_part,
                            lat_part * (1.0 - lon_part), lat_part * lon_part], axis=1).astype(jnp.bfloat16)


def quad_blend_sample(grid_flat, cell_ids, coefficient_matrix, width):
    mesh_vertex = jnp.where(cell_ids >= 0, cell_ids, 0)
    summed = jnp.zeros((cell_ids.shape[0], grid_flat.shape[1]), jnp.float32)
    for number, offset in enumerate((0, 1, width, width + 1)):
        summed = summed + coefficient_matrix[:, number:number + 1].astype(jnp.float32) * grid_flat[mesh_vertex + offset].astype(jnp.float32)
    return summed.astype(jnp.bfloat16)


def spread_back(adjoint, cell_ids, coefficient_matrix, width, number_cells):
    mesh_vertex = jnp.where(cell_ids >= 0, cell_ids, 0)
    values = adjoint.astype(jnp.float32)
    result = jnp.zeros((number_cells, adjoint.shape[1]), jnp.float32)
    for number, offset in enumerate((0, 1, width, width + 1)):
        result = result.at[mesh_vertex + offset].add(coefficient_matrix[:, number:number + 1].astype(jnp.float32) * values)
    return result


def silu_slope(pre):
    sigma = jax.nn.sigmoid(pre)
    return sigma * (1.0 + pre * (1.0 - sigma))


def observe(columns, observed, weight_in, bias_in, weight_mid, bias_mid, weight_out, bias_out, inv_error):
    pre_first = jnp.dot(columns, weight_in, preferred_element_type=jnp.float32) + bias_in
    act_first = jax.nn.silu(pre_first).astype(jnp.bfloat16)
    pre_second = jnp.dot(act_first, weight_mid, preferred_element_type=jnp.float32) + bias_mid
    act_second = jax.nn.silu(pre_second).astype(jnp.bfloat16)
    evolved = jnp.dot(act_second, weight_out, preferred_element_type=jnp.float32) + bias_out
    departures = (evolved - observed.astype(jnp.float32)) * inv_error
    scaled = (departures * inv_error).astype(jnp.bfloat16)
    back_second = (jnp.dot(scaled, weight_out.T, preferred_element_type=jnp.float32) * silu_slope(pre_second)).astype(jnp.bfloat16)
    back_first = (jnp.dot(back_second, weight_mid.T, preferred_element_type=jnp.float32) * silu_slope(pre_first)).astype(jnp.bfloat16)
    adjoint = jnp.dot(back_first, weight_in.T, preferred_element_type=jnp.float32).astype(jnp.bfloat16)
    return departures, adjoint


def reference(model_state, tangent_slope, conv_weight, weight_in, bias_in, weight_mid, bias_mid, weight_out, bias_out,
              obs_tile, obs_cell, obs_frac, radiance, inv_error):
    spectral_band_jacobian = convolve(extend_grid(model_state), conv_weight, False)
    linear_atmosphere_vector = model_state.reshape(NLAT * MERIDIAN_TOTAL, C).astype(jnp.float32)
    linear_derivative_entries = tangent_slope.reshape(NLAT * MERIDIAN_TOTAL, C).astype(jnp.float32)
    background_prediction = (linear_atmosphere_vector + linear_derivative_entries * spectral_band_jacobian).astype(jnp.bfloat16)
    owner_tile = obs_tile[:, 0]
    lat_index = owner_tile // N_LON
    lon_index = owner_tile % N_LON
    mesh_vertex = (lat_index * CLAT + obs_cell // CLON) * MERIDIAN_TOTAL + lon_index * CLON + obs_cell % CLON
    coefficient_matrix = corner_weights(obs_frac)
    found_mesh_sites = quad_blend_sample(background_prediction, mesh_vertex.astype(jnp.int32), coefficient_matrix, MERIDIAN_TOTAL)

    def one_block(pair):
        return observe(pair[0], pair[1], weight_in, bias_in, weight_mid, bias_mid, weight_out, bias_out, inv_error)

    departures, adjoint = lax.map(one_block, (found_mesh_sites.reshape(DEVICES, OBS_DEV, C), radiance.reshape(DEVICES, OBS_DEV, NCHAN)))
    departures = departures.reshape(NOBS, NCHAN)
    adjoint = adjoint.reshape(NOBS, C)
    gathered = spread_back(adjoint, mesh_vertex.astype(jnp.int32), coefficient_matrix, MERIDIAN_TOTAL, NLAT * MERIDIAN_TOTAL)
    pulled = (linear_derivative_entries * gathered).astype(jnp.bfloat16).reshape(NLAT, MERIDIAN_TOTAL, C)
    backward = convolve(extend_grid(pulled), conv_weight, True)
    gradient = (gathered + backward).reshape(NLAT, MERIDIAN_TOTAL, C)
    return departures, gradient
```

```python
import functools

import jax
import jax.numpy as jnp
from jax import lax
from jax.experimental import pallas as pl
from jax.experimental.pallas import tpu as pltpu
from jax.sharding import PartitionSpec as P

F32 = jnp.float32
BF16 = jnp.bfloat16
META = 128
FIELDS = 6
VMEM_LIMIT = 40 * 1024 * 1024


def dot_nt(left, right):
    return lax.dot_general(left, right, (((1,), (1,)), ((), ())), preferred_element_type=F32)


def dot_nn(left, right):
    return jnp.dot(left, right, preferred_element_type=F32)


def iota(shape, dim):
    return lax.broadcasted_iota(jnp.int32, shape, dim)


def kernel_call(body, outs, scratch=(), flops=0, moved=0, name=None):
    return pl.pallas_call(
        body,
        out_shape=outs,
        scratch_shapes=list(scratch),
        name=name,
        compiler_params=pltpu.CompilerParams(vmem_limit_bytes=VMEM_LIMIT),
        cost_estimate=pl.CostEstimate(flops=flops, bytes_accessed=moved, transcendentals=0),
    )


def dispatch_kernel(capacity, tile_ref, cell_ref, frac_ref, radiance_ref, box_ref, slot_ref):
    slots, width = box_ref.shape
    devices = slots // capacity
    count = tile_ref.shape[1]
    channels = width - META
    tile = tile_ref[...]
    match = (iota((devices, count), 0) == tile).astype(F32)
    earlier = (iota((count, count), 0) < iota((count, count), 1)).astype(F32).astype(BF16)
    before = dot_nn(match.astype(BF16), earlier)
    position = jnp.sum(before * match, axis=0, keepdims=True)
    slot = tile * capacity + position.astype(jnp.int32)
    slot_ref[...] = slot
    place = (iota((slots, count), 0) == slot).astype(F32).astype(BF16)
    box_ref[:, :channels] = dot_nn(place, radiance_ref[...]).astype(BF16)
    cell = cell_ref[...]
    low, side = frac_ref[0:1, :], frac_ref[1:2, :]
    fields = (
        (cell >> 7).astype(F32),
        (cell & 127).astype(F32),
        (1.0 - low) * (1.0 - side),
        (1.0 - low) * side,
        low * (1.0 - side),
        low * side,
    )
    number = iota((META, count), 0)
    meta = jnp.zeros((META, count), F32)
    for index, field in enumerate(fields):
        meta = jnp.where(number == index, field, meta)
    box_ref[:, channels:] = dot_nt(place, meta.astype(BF16)).astype(BF16)


def fill_row(shifted, row, center, left, right):
    columns = center.shape[0]
    place = iota(center.shape, 0)
    where = pl.ds(row * columns, columns)
    shifted[1, where, :] = center.astype(BF16)
    shifted[0, where, :] = jnp.where(place == 0, left, pltpu.roll(center, 1, 0)).astype(BF16)
    shifted[2, where, :] = jnp.where(
        place == columns - 1, right, pltpu.roll(center, columns - 1, 0)
    ).astype(BF16)


def fill(shifted, field_ref, left_ref, right_ref, north_ref, south_ref):
    rows, columns, _ = field_ref.shape
    left = left_ref[...].astype(F32)
    right = right_ref[...].astype(F32)
    for row in range(rows):
        fill_row(
            shifted,
            row + 1,
            field_ref[row].astype(F32),
            left[row : row + 1],
            right[row : row + 1],
        )
    for row, edge_ref in ((0, north_ref), (rows + 1, south_ref)):
        corners = edge_ref[columns : columns + 16, :].astype(F32)
        fill_row(
            shifted, row, edge_ref[:columns, :].astype(F32), corners[0:1], corners[1:2]
        )


def convolve_rows(shifted, weight_ref, start, count, columns, mirror):
    total = None
    for row_step in range(3):
        for col_step in range(3):
            window = shifted[
                col_step, pl.ds(pl.multiple_of(start + row_step * columns, columns), count), :
            ]
            if mirror:
                term = dot_nt(window, weight_ref[2 - row_step, 2 - col_step])
            else:
                term = dot_nn(window, weight_ref[row_step, col_step])
            total = term if total is None else total + term
    return total


CHUNK = 512


def forecast_kernel(
    state_ref, slope_ref, left_ref, right_ref, north_ref, south_ref, weight_ref, out_ref, shifted
):
    rows, columns, channels = state_ref.shape
    fill(shifted, state_ref, left_ref, right_ref, north_ref, south_ref)
    per = CHUNK // columns

    def step(index, carry):
        start = index * CHUNK
        response = convolve_rows(shifted, weight_ref, start, CHUNK, columns, False)
        which = pl.ds(index * per, per)
        state = state_ref[which].reshape(CHUNK, channels).astype(F32)
        slope = slope_ref[which].reshape(CHUNK, channels).astype(F32)
        out_ref[pl.ds(pl.multiple_of(start, CHUNK), CHUNK), :] = (
            state + slope * response
        ).astype(BF16)
        return carry

    lax.fori_loop(0, rows * columns // CHUNK, step, 0)


def gradient_kernel(
    pulled_ref, spread_ref, left_ref, right_ref, north_ref, south_ref, weight_ref, out_ref, shifted
):
    rows, columns, channels = pulled_ref.shape
    fill(shifted, pulled_ref, left_ref, right_ref, north_ref, south_ref)

    def step(index, carry):
        start = index * CHUNK
        response = convolve_rows(shifted, weight_ref, start, CHUNK, columns, True)
        which = pl.ds(pl.multiple_of(start, CHUNK), CHUNK)
        out_ref[which, :] = spread_ref[which, :] + response
        return carry

    lax.fori_loop(0, rows * columns // CHUNK, step, 0)


def sigmoid(value):
    return 0.5 + 0.5 * jnp.tanh(0.5 * value)


def sample_kernel(
    columns,
    box_ref,
    grid_ref,
    weight_in_ref,
    bias_in_ref,
    weight_mid_ref,
    bias_mid_ref,
    weight_out_ref,
    bias_out_ref,
    inv_error_ref,
    departures_ref,
    scaled_ref,
    slope_first_ref,
    slope_second_ref,
    sampled,
):
    slots, width = box_ref.shape
    cells = grid_ref.shape[0]
    channels = width - META
    pick = (iota((META, FIELDS * columns), 0) == iota((META, FIELDS * columns), 1) // columns)
    wide = dot_nn(box_ref[:, channels:], pick.astype(F32).astype(BF16))
    row, column, w00, w01, w10, w11 = (
        wide[:, index * columns : (index + 1) * columns] for index in range(FIELDS)
    )
    lane = iota((slots, columns), 1).astype(F32)
    here, beside = lane == column, lane == column + 1.0
    upper = (jnp.where(here, w00, 0.0) + jnp.where(beside, w01, 0.0)).astype(BF16)
    lower = (jnp.where(here, w10, 0.0) + jnp.where(beside, w11, 0.0)).astype(BF16)
    row_low = row.astype(BF16)
    row_high = (row + 1.0).astype(BF16)
    zero = jnp.zeros((slots, columns), BF16)
    per = 8
    for block in range(cells // columns // per):
        parts = []
        for index in range(per):
            at = jnp.asarray(block * per + index, BF16)
            parts.append(jnp.where(row_low == at, upper, jnp.where(row_high == at, lower, zero)))
        first = block * per * columns
        term = dot_nn(
            jnp.concatenate(parts, axis=1), grid_ref[first : first + per * columns, :]
        )
        if block == 0:
            sampled[...] = term
        else:
            sampled[...] += term
    inv_error = inv_error_ref[...]
    step = 256
    for start in range(0, slots, step):
        rows = slice(start, start + step)
        pre_first = dot_nn(sampled[rows, :].astype(BF16), weight_in_ref[...]) + bias_in_ref[...]
        gate = sigmoid(pre_first)
        act = pre_first * gate
        slope_first_ref[rows, :] = gate + act * (1.0 - gate)
        pre_second = dot_nn(act.astype(BF16), weight_mid_ref[...]) + bias_mid_ref[...]
        gate = sigmoid(pre_second)
        act = pre_second * gate
        slope_second_ref[rows, :] = gate + act * (1.0 - gate)
        evolved = dot_nn(act.astype(BF16), weight_out_ref[...]) + bias_out_ref[...]
        departures = (evolved - box_ref[rows, :channels].astype(F32)) * inv_error
        departures_ref[rows, :] = departures.astype(BF16)
        scaled_ref[rows, :] = (departures * inv_error).astype(BF16)


def spread_kernel(
    columns,
    box_ref,
    scaled_ref,
    slope_first_ref,
    slope_second_ref,
    weight_in_ref,
    weight_mid_ref,
    weight_out_ref,
    tangent_ref,
    spread_ref,
    pulled_ref,
    west_ref,
    east_ref,
    adjoint,
):
    slots, width = box_ref.shape
    cells = spread_ref.shape[0]
    channels = width - META
    step = 256
    for start in range(0, slots, step):
        rows = slice(start, start + step)
        back = (dot_nt(scaled_ref[rows, :], weight_out_ref[...]) * slope_second_ref[rows, :]).astype(BF16)
        back = (dot_nt(back, weight_mid_ref[...]) * slope_first_ref[rows, :]).astype(BF16)
        adjoint[rows, :] = dot_nt(back, weight_in_ref[...]).astype(BF16)
    pick = (iota((16, META), 0) == iota((16, META), 1)).astype(F32).astype(BF16)
    turned = dot_nt(pick, box_ref[:, channels:])
    row, column, w00, w01, w10, w11 = (turned[index : index + 1, :] for index in range(FIELDS))
    place = iota((columns, slots), 0).astype(F32)
    here, beside = place == column, place == column + 1.0
    upper = (jnp.where(here, w00, 0.0) + jnp.where(beside, w01, 0.0)).astype(BF16)
    lower = (jnp.where(here, w10, 0.0) + jnp.where(beside, w11, 0.0)).astype(BF16)
    row_low = jnp.broadcast_to(row, (columns, slots)).astype(BF16)
    row_high = jnp.broadcast_to(row + 1.0, (columns, slots)).astype(BF16)
    zero = jnp.zeros((columns, slots), BF16)
    per = 4
    for block in range(cells // columns // per):
        parts = []
        for index in range(per):
            at = jnp.asarray(block * per + index, BF16)
            parts.append(jnp.where(row_low == at, upper, jnp.where(row_high == at, lower, zero)))
        first = block * per * columns
        which = slice(first, first + per * columns)
        spread = dot_nn(jnp.concatenate(parts, axis=0), adjoint[...])
        spread_ref[which, :] = spread
        pulled = tangent_ref[which, :].astype(F32) * spread
        pulled_ref[which, :] = pulled.astype(BF16)
        for index in range(per):
            at = block * per + index
            first = index * columns
            west_ref[at : at + 1, :] = pulled[first : first + 1, :]
            east_ref[at : at + 1, :] = pulled[first + columns - 1 : first + columns, :]


def departures_kernel(slot_ref, box_ref, out_ref):
    slots = box_ref.shape[0]
    count = slot_ref.shape[1]
    turned = jnp.broadcast_to(slot_ref[...].astype(F32), (128, count)).T
    lane = iota((count, 128), 1).astype(F32)
    parts = [(lane + float(first) == turned).astype(F32).astype(BF16) for first in range(0, slots, 128)]
    out_ref[...] = dot_nn(jnp.concatenate(parts, axis=1), box_ref[...])


def halo(west, east, top, bottom):
    lon, lat = lax.axis_size("lon"), lax.axis_size("lat")
    onward = [(i, (i + 1) % lon) for i in range(lon)]
    left = lax.ppermute(east, "lon", onward)
    right = lax.ppermute(west, "lon", [(target, source) for source, target in onward])
    down = [(i, i + 1) for i in range(lat - 1)]
    up = [(target, source) for source, target in down]
    filler = jnp.zeros((14, top.shape[1]), top.dtype)
    north = lax.ppermute(jnp.concatenate([bottom, left[-1:], right[-1:], filler]), "lat", down)
    south = lax.ppermute(jnp.concatenate([top, left[:1], right[:1], filler]), "lat", up)
    return left, right, north, south


def body(
    model_state,
    tangent_slope,
    conv_weight,
    weight_in,
    bias_in,
    weight_mid,
    bias_mid,
    weight_out,
    bias_out,
    obs_tile,
    obs_cell,
    obs_frac,
    radiance,
    inv_error,
):
    rows, columns, channels = model_state.shape
    cells = rows * columns
    devices = lax.axis_size("lat") * lax.axis_size("lon")
    count, bands = radiance.shape
    capacity = 2 * count // devices
    slots = devices * capacity
    hidden = weight_in.shape[1]
    sds = jax.ShapeDtypeStruct

    def exchange(box):
        return lax.all_to_all(
            box.reshape(devices, capacity, -1), ("lat", "lon"), split_axis=0, concat_axis=0, tiled=True
        ).reshape(slots, -1)

    box, slot = kernel_call(
        functools.partial(dispatch_kernel, capacity),
        (sds((slots, bands + META), BF16), sds((1, count), jnp.int32)),
        flops=2 * slots * count * (bands + META),
        moved=2 * slots * (bands + META),
        name="dispatch",
    )(obs_tile.reshape(1, count), obs_cell.reshape(1, count), obs_frac.T, radiance)
    arrived = exchange(box)

    conv_flops = 2 * 9 * cells * channels * channels
    shifted = pltpu.VMEM((3, (rows + 2) * columns, channels), BF16)
    beside = halo(model_state[:, 0], model_state[:, -1], model_state[0], model_state[-1])
    forecast = kernel_call(
        forecast_kernel,
        sds((cells, channels), BF16),
        (shifted,),
        flops=conv_flops,
        moved=6 * cells * channels,
        name="forecast",
    )(model_state, tangent_slope, *beside, conv_weight)

    network_flops = 2 * slots * (channels * hidden + hidden * hidden + hidden * bands)
    departures_box, scaled, slope_first, slope_second = kernel_call(
        functools.partial(sample_kernel, columns),
        (
            sds((slots, bands), BF16),
            sds((slots, bands), BF16),
            sds((slots, hidden), F32),
            sds((slots, hidden), F32),
        ),
        (pltpu.VMEM((slots, channels), F32),),
        flops=network_flops + 2 * slots * cells * channels,
        moved=2 * cells * channels + 8 * slots * hidden,
        name="sample",
    )(
        arrived,
        forecast,
        weight_in,
        bias_in.reshape(1, -1),
        weight_mid,
        bias_mid.reshape(1, -1),
        weight_out,
        bias_out.reshape(1, -1),
        inv_error.reshape(1, -1),
    )
    returned = exchange(departures_box)

    spread, pulled, west, east = kernel_call(
        functools.partial(spread_kernel, columns),
        (
            sds((cells, channels), F32),
            sds((cells, channels), BF16),
            sds((rows, channels), F32),
            sds((rows, channels), F32),
        ),
        (pltpu.VMEM((slots, channels), BF16),),
        flops=network_flops + 2 * slots * cells * channels,
        moved=8 * cells * channels + 8 * slots * hidden,
        name="spread",
    )(
        arrived,
        scaled,
        slope_first,
        slope_second,
        weight_in,
        weight_mid,
        weight_out,
        tangent_slope.reshape(cells, channels),
    )
    beside = halo(
        west.astype(BF16), east.astype(BF16), pulled[:columns], pulled[cells - columns :]
    )
    gradient = kernel_call(
        gradient_kernel,
        sds((cells, channels), F32),
        (shifted,),
        flops=conv_flops,
        moved=10 * cells * channels,
        name="gradient",
    )(pulled.reshape(rows, columns, channels), spread, *beside, conv_weight)

    departures = kernel_call(
        departures_kernel,
        sds((count, bands), F32),
        flops=2 * slots * count * bands,
        moved=4 * count * bands,
        name="departures",
    )(slot, returned)
    return departures, gradient.reshape(rows, columns, channels)


def solution(mesh):
    in_specs = (
        P("lat", "lon", None),
        P("lat", "lon", None),
        P(),
        P(),
        P(),
        P(),
        P(),
        P(),
        P(),
        P(("lat", "lon"), None),
        P(("lat", "lon")),
        P(("lat", "lon"), None),
        P(("lat", "lon"), None),
        P(),
    )
    out_specs = (P(("lat", "lon"), None), P("lat", "lon", None))
    return jax.shard_map(body, mesh=mesh, in_specs=in_specs, out_specs=out_specs, check_vma=False)
```

```python
import functools

import jax
import jax.numpy as jnp
from jax import lax
from jax.experimental import pallas as pl
from jax.experimental.pallas import tpu as pltpu
from jax.sharding import PartitionSpec as P

F32 = jnp.float32
BF16 = jnp.bfloat16
META = 128
FIELDS = 6


def dot_nt(left, right):
    return lax.dot_general(left, right, (((1,), (1,)), ((), ())), preferred_element_type=F32)


def dot_nn(left, right):
    return jnp.dot(left, right, preferred_element_type=F32)


def iota(shape, dim):
    return lax.broadcasted_iota(jnp.int32, shape, dim)


def kernel_call(body, outs, out_spaces, in_spaces, scratch=(), flops=0, moved=0, limit=24, name=None):
    return pl.pallas_call(
        body,
        out_shape=outs,
        in_specs=[pl.BlockSpec(memory_space=space) for space in in_spaces],
        out_specs=[pl.BlockSpec(memory_space=space) for space in out_spaces],
        scratch_shapes=list(scratch),
        name=name,
        compiler_params=pltpu.CompilerParams(vmem_limit_bytes=limit * 1024 * 1024),
        cost_estimate=pl.CostEstimate(flops=flops, bytes_accessed=moved, transcendentals=0),
    )


HBM = pltpu.HBM
VMEM = pltpu.VMEM


def copies(semaphores, *pairs):
    started = []
    for index, (source, target) in enumerate(pairs):
        copy = pltpu.make_async_copy(source, target, semaphores.at[index])
        copy.start()
        started.append(copy)
    return started


def dispatch_kernel(
    capacity,
    tile_hbm,
    cell_hbm,
    frac_hbm,
    radiance_hbm,
    box_ref,
    slot_ref,
    tile_ref,
    cell_ref,
    frac_ref,
    radiance_ref,
    semaphores,
):
    waiting = copies(
        semaphores,
        (tile_hbm, tile_ref),
        (cell_hbm, cell_ref),
        (frac_hbm, frac_ref),
        (radiance_hbm, radiance_ref),
    )
    slots, width = box_ref.shape
    devices = slots // capacity
    count = tile_ref.shape[1]
    channels = width - META
    earlier = (iota((count, count), 0) < iota((count, count), 1)).astype(F32).astype(BF16)
    for copy in waiting[:3]:
        copy.wait()
    tile = tile_ref[...]
    match = (iota((devices, count), 0) == tile).astype(F32)
    before = dot_nn(match.astype(BF16), earlier)
    position = jnp.sum(before * match, axis=0, keepdims=True)
    slot = tile * capacity + position.astype(jnp.int32)
    slot_ref[...] = slot
    place = (iota((slots, count), 0) == slot).astype(F32).astype(BF16)
    cell = cell_ref[...]
    low, side = frac_ref[0:1, :], frac_ref[1:2, :]
    fields = (
        (cell >> 7).astype(F32),
        (cell & 127).astype(F32),
        (1.0 - low) * (1.0 - side),
        (1.0 - low) * side,
        low * (1.0 - side),
        low * side,
    )
    number = iota((META, count), 0)
    meta = jnp.zeros((META, count), F32)
    for index, field in enumerate(fields):
        meta = jnp.where(number == index, field, meta)
    box_ref[:, channels:] = dot_nt(place, meta.astype(BF16)).astype(BF16)
    waiting[3].wait()
    box_ref[:, :channels] = dot_nn(place, radiance_ref[...]).astype(BF16)


CHUNK = 512


def fill_row(shifted, row, center, left, right):
    columns = center.shape[0]
    place = iota(center.shape, 0)
    where = pl.ds(row * columns, columns)
    shifted[1, where, :] = center.astype(BF16)
    shifted[0, where, :] = jnp.where(place == 0, left, pltpu.roll(center, 1, 0)).astype(BF16)
    shifted[2, where, :] = jnp.where(
        place == columns - 1, right, pltpu.roll(center, columns - 1, 0)
    ).astype(BF16)


def fill(shifted, field_ref, left_ref, right_ref, north_ref, south_ref):
    rows, columns, _ = field_ref.shape
    left = left_ref[...].astype(F32)
    right = right_ref[...].astype(F32)
    for row in range(rows):
        fill_row(
            shifted,
            row + 1,
            field_ref[row].astype(F32),
            left[row : row + 1],
            right[row : row + 1],
        )
    for row, edge_ref, at in ((0, north_ref, 15), (rows + 1, south_ref, 0)):
        corners = edge_ref[columns:, :].astype(F32)
        fill_row(
            shifted,
            row,
            edge_ref[:columns, :].astype(F32),
            corners[at : at + 1],
            corners[16 + at : 17 + at],
        )


def convolve_rows(shifted, weight_ref, start, count, columns):
    total = None
    for row_step in range(3):
        for col_step in range(3):
            window = shifted[
                col_step, pl.ds(pl.multiple_of(start + row_step * columns, columns), count), :
            ]
            term = dot_nn(window, weight_ref[row_step, col_step])
            total = term if total is None else total + term
    return total


def forecast_kernel(
    state_hbm,
    slope_hbm,
    weight_hbm,
    left_ref,
    right_ref,
    north_ref,
    south_ref,
    out_hbm,
    mirrored_ref,
    sides_ref,
    state_ref,
    slope_ref,
    weight_ref,
    out_ref,
    shifted,
    semaphores,
    out_semaphores,
):
    waiting = copies(
        semaphores, (state_hbm, state_ref), (weight_hbm, weight_ref), (slope_hbm, slope_ref)
    )
    rows, columns, channels = state_ref.shape
    waiting[0].wait()
    fill(shifted, state_ref, left_ref, right_ref, north_ref, south_ref)
    waiting[1].wait()
    waiting[2].wait()
    per = CHUNK // columns

    def out_copy(index):
        which = pl.ds(pl.multiple_of(index * CHUNK, CHUNK), CHUNK)
        return pltpu.make_async_copy(
            out_ref.at[which, :], out_hbm.at[which, :], out_semaphores.at[index]
        )

    def step(index, carry):
        start = index * CHUNK
        response = convolve_rows(shifted, weight_ref, start, CHUNK, columns)
        which = pl.ds(index * per, per)
        state = state_ref[which].reshape(CHUNK, channels).astype(F32)
        slope = slope_ref[which].reshape(CHUNK, channels).astype(F32)
        out_ref[pl.ds(pl.multiple_of(start, CHUNK), CHUNK), :] = (
            state + slope * response
        ).astype(BF16)
        out_copy(index).start()
        return carry

    steps = rows * columns // CHUNK
    lax.fori_loop(0, steps, step, 0)
    for row_step in range(3):
        for col_step in range(3):
            mirrored_ref[row_step, col_step] = (
                weight_ref[2 - row_step, 2 - col_step].astype(F32).T.astype(BF16)
            )
    for row in range(rows):
        sides_ref[0, row : row + 1, :] = slope_ref[row, 0:16, :].astype(F32)[0:1]
        sides_ref[1, row : row + 1, :] = slope_ref[row, columns - 16 : columns, :].astype(F32)[15:16]
    for index in range(steps):
        out_copy(index).wait()


def gradient_kernel(
    pulled_ref,
    spread_ref,
    weight_hbm,
    left_ref,
    right_ref,
    north_ref,
    south_ref,
    out_hbm,
    weight_ref,
    out_ref,
    shifted,
    semaphores,
    out_semaphores,
):
    waiting = copies(semaphores, (weight_hbm, weight_ref))
    rows, columns, channels = pulled_ref.shape
    fill(shifted, pulled_ref, left_ref, right_ref, north_ref, south_ref)
    waiting[0].wait()

    def out_copy(index):
        which = pl.ds(pl.multiple_of(index * CHUNK, CHUNK), CHUNK)
        return pltpu.make_async_copy(
            out_ref.at[which, :], out_hbm.at[which, :], out_semaphores.at[index]
        )

    def step(index, carry):
        start = index * CHUNK
        response = convolve_rows(shifted, weight_ref, start, CHUNK, columns)
        which = pl.ds(pl.multiple_of(start, CHUNK), CHUNK)
        out_ref[which, :] = spread_ref[which, :] + response
        out_copy(index).start()
        return carry

    steps = rows * columns // CHUNK
    lax.fori_loop(0, steps, step, 0)
    for index in range(steps):
        out_copy(index).wait()


def sigmoid(value):
    return 0.5 + 0.5 * jnp.tanh(0.5 * value)


def blend(row_low, row_high, upper, lower, at):
    at = jnp.asarray(at, BF16)
    zero = jnp.zeros(upper.shape, BF16)
    return jnp.where(row_low == at, upper, jnp.where(row_high == at, lower, zero))


def turned_weights(fields, columns):
    slots = fields.shape[1]
    row, column, w00, w01, w10, w11 = (fields[index : index + 1, :] for index in range(FIELDS))
    place = iota((columns, slots), 0).astype(F32)
    here, beside = place == column, place == column + 1.0
    upper = (jnp.where(here, w00, 0.0) + jnp.where(beside, w01, 0.0)).astype(BF16)
    lower = (jnp.where(here, w10, 0.0) + jnp.where(beside, w11, 0.0)).astype(BF16)
    row_low = jnp.broadcast_to(row, (columns, slots)).astype(BF16)
    row_high = jnp.broadcast_to(row + 1.0, (columns, slots)).astype(BF16)
    return row_low, row_high, upper, lower


def observe_kernel(
    columns,
    box_ref,
    grid_hbm,
    weight_in_hbm,
    weight_mid_hbm,
    weight_out_hbm,
    vectors_hbm,
    slope_hbm,
    sides_hbm,
    departures_hbm,
    adjoint_hbm,
    fields_hbm,
    west_ref,
    east_ref,
    top_ref,
    bottom_ref,
    grid_ref,
    weight_in_ref,
    weight_mid_ref,
    weight_out_ref,
    vectors_ref,
    ends_ref,
    sides_ref,
    sampled,
    departures_ref,
    adjoint,
    fields_ref,
    semaphores,
    out_semaphores,
):
    slots, width = box_ref.shape
    cells, grid_channels = grid_ref.shape
    channels = width - META
    hidden = weight_in_ref.shape[1]
    rows = cells // columns
    waiting = copies(
        semaphores,
        (grid_hbm, grid_ref),
        (weight_in_hbm, weight_in_ref),
        (vectors_hbm, vectors_ref),
        (weight_mid_hbm, weight_mid_ref),
        (weight_out_hbm, weight_out_ref),
        (slope_hbm.at[pl.ds(0, columns), :], ends_ref.at[0]),
        (slope_hbm.at[pl.ds(cells - columns, columns), :], ends_ref.at[1]),
        (sides_hbm, sides_ref),
    )
    pick = (iota((16, META), 0) == iota((16, META), 1)).astype(F32).astype(BF16)
    fields_ref[...] = dot_nt(pick, box_ref[:, channels:])
    fields_out = pltpu.make_async_copy(fields_ref, fields_hbm, out_semaphores.at[0])
    fields_out.start()
    pick = iota((META, FIELDS * columns), 0) == iota((META, FIELDS * columns), 1) // columns
    wide = dot_nn(box_ref[:, channels:], pick.astype(F32).astype(BF16))
    row, column, w00, w01, w10, w11 = (
        wide[:, index * columns : (index + 1) * columns] for index in range(FIELDS)
    )
    lane = iota((slots, columns), 1).astype(F32)
    here, beside = lane == column, lane == column + 1.0
    upper = (jnp.where(here, w00, 0.0) + jnp.where(beside, w01, 0.0)).astype(BF16)
    lower = (jnp.where(here, w10, 0.0) + jnp.where(beside, w11, 0.0)).astype(BF16)
    row_low = row.astype(BF16)
    row_high = (row + 1.0).astype(BF16)
    per = 8
    waiting[0].wait()
    for block in range(rows // per):
        parts = [
            blend(row_low, row_high, upper, lower, block * per + index) for index in range(per)
        ]
        first = block * per * columns
        term = dot_nn(jnp.concatenate(parts, axis=1), grid_ref[first : first + per * columns, :])
        if block == 0:
            sampled[...] = term
        else:
            sampled[...] += term
    for copy in waiting[1:]:
        copy.wait()
    bias_in = vectors_ref[:, :hidden]
    bias_mid = vectors_ref[:, hidden : 2 * hidden]
    bias_out = vectors_ref[:, 2 * hidden : 2 * hidden + channels]
    inv_error = vectors_ref[:, 2 * hidden + channels :]
    step = 256
    for start in range(0, slots, step):
        part = slice(start, start + step)
        pre = dot_nn(sampled[part, :].astype(BF16), weight_in_ref[...]) + bias_in
        gate = sigmoid(pre)
        act = pre * gate
        slope_first = gate + act * (1.0 - gate)
        pre = dot_nn(act.astype(BF16), weight_mid_ref[...]) + bias_mid
        gate = sigmoid(pre)
        act = pre * gate
        slope_second = gate + act * (1.0 - gate)
        evolved = dot_nn(act.astype(BF16), weight_out_ref[...]) + bias_out
        departures = (evolved - box_ref[part, :channels].astype(F32)) * inv_error
        departures_ref[part, :] = departures.astype(BF16)
        back = (departures * inv_error).astype(BF16)
        back = (dot_nt(back, weight_out_ref[...]) * slope_second).astype(BF16)
        back = (dot_nt(back, weight_mid_ref[...]) * slope_first).astype(BF16)
        adjoint[part, :] = dot_nt(back, weight_in_ref[...]).astype(BF16)
    results = [
        pltpu.make_async_copy(departures_ref, departures_hbm, out_semaphores.at[1]),
        pltpu.make_async_copy(adjoint, adjoint_hbm, out_semaphores.at[2]),
    ]
    for copy in results:
        copy.start()
    fields = fields_ref[...]
    around = turned_weights(fields, columns)
    for at, index, edge_ref in ((0, 0, top_ref), (rows - 1, 1, bottom_ref)):
        spread = dot_nn(blend(*around, at), adjoint[...])
        edge_ref[...] = (ends_ref[index].astype(F32) * spread).astype(BF16)
    row, column, w00, w01, w10, w11 = (fields[index : index + 1, :] for index in range(FIELDS))
    place = iota((rows, slots), 0).astype(F32)
    here, below = place == row, place == row + 1.0
    zero = jnp.zeros((rows, slots), F32)
    for at, index, edge_ref, high, low in (
        (0.0, 0, west_ref, w00, w10),
        (columns - 2.0, 1, east_ref, w01, w11),
    ):
        chosen = column == at
        weights = jnp.where(
            here & chosen, high, jnp.where(below & chosen, low, zero)
        ).astype(BF16)
        edge_ref[...] = (sides_ref[index] * dot_nn(weights, adjoint[...])).astype(BF16)
    fields_out.wait()
    for copy in results:
        copy.wait()


def spread_kernel(
    columns,
    adjoint_hbm,
    fields_hbm,
    slope_hbm,
    spread_ref,
    pulled_ref,
    adjoint,
    fields_ref,
    slope_ref,
    semaphores,
):
    waiting = copies(
        semaphores, (fields_hbm, fields_ref), (adjoint_hbm, adjoint), (slope_hbm, slope_ref)
    )
    cells = spread_ref.shape[0]
    waiting[0].wait()
    around = turned_weights(fields_ref[...], columns)
    waiting[1].wait()
    waiting[2].wait()
    per = 4
    for block in range(cells // columns // per):
        parts = [blend(*around, block * per + index) for index in range(per)]
        first = block * per * columns
        which = slice(first, first + per * columns)
        spread = dot_nn(jnp.concatenate(parts, axis=0), adjoint[...])
        spread_ref[which, :] = spread
        pulled_ref[which, :] = (slope_ref[which, :].astype(F32) * spread).astype(BF16)


def departures_kernel(slot_ref, box_ref, out_ref):
    slots = box_ref.shape[0]
    count = slot_ref.shape[1]
    turned = jnp.broadcast_to(slot_ref[...].astype(F32), (128, count)).T
    lane = iota((count, 128), 1).astype(F32)
    parts = [(lane + float(first) == turned).astype(F32).astype(BF16) for first in range(0, slots, 128)]
    out_ref[...] = dot_nn(jnp.concatenate(parts, axis=1), box_ref[...])


def halo(west, east, top, bottom):
    lon, lat = lax.axis_size("lon"), lax.axis_size("lat")
    onward = [(i, (i + 1) % lon) for i in range(lon)]
    left = lax.ppermute(east, "lon", onward)
    right = lax.ppermute(west, "lon", [(target, source) for source, target in onward])
    down = [(i, i + 1) for i in range(lat - 1)]
    up = [(target, source) for source, target in down]
    north = lax.ppermute(jnp.concatenate([bottom, left[-16:], right[-16:]]), "lat", down)
    south = lax.ppermute(jnp.concatenate([top, left[:16], right[:16]]), "lat", up)
    return left, right, north, south


def body(
    model_state,
    tangent_slope,
    conv_weight,
    weight_in,
    bias_in,
    weight_mid,
    bias_mid,
    weight_out,
    bias_out,
    obs_tile,
    obs_cell,
    obs_frac,
    radiance,
    inv_error,
):
    rows, columns, channels = model_state.shape
    cells = rows * columns
    devices = lax.axis_size("lat") * lax.axis_size("lon")
    count, bands = radiance.shape
    capacity = 2 * count // devices
    slots = devices * capacity
    hidden = weight_in.shape[1]
    sds = jax.ShapeDtypeStruct
    dma = pltpu.SemaphoreType.DMA

    def exchange(box):
        return lax.all_to_all(
            box.reshape(devices, capacity, -1), ("lat", "lon"), split_axis=0, concat_axis=0, tiled=True
        ).reshape(slots, -1)

    box, slot = kernel_call(
        functools.partial(dispatch_kernel, capacity),
        (sds((slots, bands + META), BF16), sds((1, count), jnp.int32)),
        (VMEM, VMEM),
        (HBM,) * 4,
        (
            pltpu.VMEM((1, count), jnp.int32),
            pltpu.VMEM((1, count), jnp.int32),
            pltpu.VMEM((2, count), F32),
            pltpu.VMEM((count, bands), BF16),
            dma((4,)),
        ),
        flops=2 * slots * count * (bands + META),
        moved=2 * slots * (bands + META),
        name="dispatch",
    )(obs_tile.reshape(1, count), obs_cell.reshape(1, count), obs_frac.T, radiance)
    box, model_state = lax.optimization_barrier((box, model_state))
    arrived = exchange(box)

    conv_flops = 2 * 9 * cells * channels * channels
    conv_scratch = (
        pltpu.VMEM((3, (rows + 2) * columns, channels), BF16),
    )
    steps = cells // CHUNK
    beside = halo(model_state[:, 0], model_state[:, -1], model_state[0], model_state[-1])
    forecast, mirrored, sides = kernel_call(
        forecast_kernel,
        (
            sds((cells, channels), BF16),
            sds(conv_weight.shape, BF16),
            sds((2, rows, channels), F32),
        ),
        (HBM, VMEM, VMEM),
        (HBM,) * 3 + (VMEM,) * 4,
        (
            pltpu.VMEM((rows, columns, channels), BF16),
            pltpu.VMEM((rows, columns, channels), BF16),
            pltpu.VMEM(conv_weight.shape, BF16),
            pltpu.VMEM((cells, channels), BF16),
            *conv_scratch,
            dma((3,)),
            dma((steps,)),
        ),
        flops=conv_flops,
        moved=6 * cells * channels,
        name="forecast",
    )(model_state, tangent_slope, conv_weight, *beside)

    flat_slope = tangent_slope.reshape(cells, channels)
    vectors = jnp.concatenate([bias_in, bias_mid, bias_out, inv_error]).reshape(1, -1)
    network_flops = 2 * slots * (channels * hidden + hidden * hidden + hidden * bands)
    departures_box, adjoint, fields, west, east, top, bottom = kernel_call(
        functools.partial(observe_kernel, columns),
        (
            sds((slots, bands), BF16),
            sds((slots, channels), BF16),
            sds((16, slots), F32),
            sds((rows, channels), BF16),
            sds((rows, channels), BF16),
            sds((columns, channels), BF16),
            sds((columns, channels), BF16),
        ),
        (HBM,) * 3 + (VMEM,) * 4,
        (VMEM,) + (HBM,) * 7,
        (
            pltpu.VMEM((cells, channels), BF16),
            pltpu.VMEM(weight_in.shape, BF16),
            pltpu.VMEM(weight_mid.shape, BF16),
            pltpu.VMEM(weight_out.shape, BF16),
            pltpu.VMEM(vectors.shape, F32),
            pltpu.VMEM((2, columns, channels), BF16),
            pltpu.VMEM((2, rows, channels), F32),
            pltpu.VMEM((slots, channels), F32),
            pltpu.VMEM((slots, bands), BF16),
            pltpu.VMEM((slots, channels), BF16),
            pltpu.VMEM((16, slots), F32),
            dma((8,)),
            dma((3,)),
        ),
        flops=2 * network_flops + 2 * slots * cells * channels,
        moved=2 * cells * channels,
        limit=32,
        name="observe",
    )(arrived, forecast, weight_in, weight_mid, weight_out, vectors, flat_slope, sides)
    returned = exchange(departures_box)

    beside = halo(west, east, top, bottom)
    spread, pulled = kernel_call(
        functools.partial(spread_kernel, columns),
        (sds((cells, channels), F32), sds((cells, channels), BF16)),
        (VMEM, VMEM),
        (HBM,) * 3,
        (
            pltpu.VMEM((slots, channels), BF16),
            pltpu.VMEM((16, slots), F32),
            pltpu.VMEM((cells, channels), BF16),
            dma((3,)),
        ),
        flops=2 * slots * cells * channels,
        moved=2 * cells * channels,
        name="spread",
    )(adjoint, fields, flat_slope)
    gradient, = kernel_call(
        gradient_kernel,
        (sds((cells, channels), F32),),
        (HBM,),
        (VMEM, VMEM, HBM) + (VMEM,) * 4,
        (
            pltpu.VMEM(conv_weight.shape, BF16),
            pltpu.VMEM((cells, channels), F32),
            *conv_scratch,
            dma((1,)),
            dma((steps,)),
        ),
        flops=conv_flops,
        moved=4 * cells * channels,
        name="gradient",
    )(pulled.reshape(rows, columns, channels), spread, mirrored, *beside)

    departures, = kernel_call(
        departures_kernel,
        (sds((count, bands), F32),),
        (VMEM,),
        (VMEM, VMEM),
        flops=2 * slots * count * bands,
        moved=4 * count * bands,
        name="departures",
    )(slot, returned)
    return departures, gradient.reshape(rows, columns, channels)


def solution(mesh):
    in_specs = (
        P("lat", "lon", None),
        P("lat", "lon", None),
        P(),
        P(),
        P(),
        P(),
        P(),
        P(),
        P(),
        P(("lat", "lon"), None),
        P(("lat", "lon")),
        P(("lat", "lon"), None),
        P(("lat", "lon"), None),
        P(),
    )
    out_specs = (P(("lat", "lon"), None), P("lat", "lon", None))
    return jax.shard_map(body, mesh=mesh, in_specs=in_specs, out_specs=out_specs, check_vma=False)
```

```python
import functools

import jax
import jax.numpy as jnp
from jax import lax
from jax.experimental import pallas as pl
from jax.experimental.pallas import tpu as pltpu
from jax.sharding import PartitionSpec as P

F32 = jnp.float32
BF16 = jnp.bfloat16
META = 128
FIELDS = 6
VMEM_KIB = 60 * 1024 + 512


def dot_nt(left, right):
    return lax.dot_general(left, right, (((1,), (1,)), ((), ())), preferred_element_type=F32)


def dot_nn(left, right):
    return jnp.dot(left, right, preferred_element_type=F32)


def iota(shape, dim):
    return lax.broadcasted_iota(jnp.int32, shape, dim)


def kernel_call(body, outs, out_spaces, in_spaces, scratch=(), flops=0, moved=0, room=0, aliases=None, name=None):
    return pl.pallas_call(
        body,
        out_shape=outs,
        in_specs=[pl.BlockSpec(memory_space=space) for space in in_spaces],
        out_specs=[pl.BlockSpec(memory_space=space) for space in out_spaces],
        scratch_shapes=list(scratch),
        input_output_aliases=aliases or {},
        name=name,
        compiler_params=pltpu.CompilerParams(vmem_limit_bytes=(VMEM_KIB - room) * 1024),
        cost_estimate=pl.CostEstimate(flops=flops, bytes_accessed=moved, transcendentals=0),
    )


HBM = pltpu.HBM
VMEM = pltpu.VMEM


def copies(semaphores, *pairs):
    started = []
    for index, (source, target) in enumerate(pairs):
        copy = pltpu.make_async_copy(source, target, semaphores.at[index])
        copy.start()
        started.append(copy)
    return started


CORNER_LANE = 32
CORNER_WIDTH = 32


def corner_slots(lat, lon, capacity, shape, dim):
    lats, lons = lax.axis_size("lat"), lax.axis_size("lon")
    number = iota(shape, dim)
    result = jnp.full(shape, -1, jnp.int32)
    for index, (down, right) in enumerate(((-1, -1), (-1, 1), (1, -1), (1, 1))):
        row, column = lat + down, lax.rem(lon + right + lons, lons)
        inside = (row >= 0) & (row < lats)
        first = jnp.where(inside, (row * lons + column) * capacity, -4096)
        mine = (number >= index * 8) & (number < index * 8 + 8)
        result = jnp.where(mine, first + number - index * 8, result)
    return result


def corner_fold(shape, lane_dim):
    value, lane = iota(shape, 1 - lane_dim), iota(shape, lane_dim)
    chosen = (value % CORNER_WIDTH == lane - CORNER_LANE) & (lane >= CORNER_LANE)
    return (chosen & (lane < CORNER_LANE + CORNER_WIDTH)).astype(F32).astype(BF16)


def corner_mask(shape):
    return iota(shape, 1) // CORNER_WIDTH == iota(shape, 0) % 8


def corners_out(cells, lat, lon, capacity, first, count):
    channels = cells[0].shape[1]
    spread = jnp.concatenate([jnp.broadcast_to(cell, (8, channels)) for cell in cells], axis=0)
    kept = jnp.where(corner_mask(spread.shape), spread, 0.0).astype(BF16)
    folded = dot_nn(kept, corner_fold((channels, META), 1)).astype(BF16)
    target = corner_slots(lat, lon, capacity, (count, 32), 1)
    place = (iota((count, 32), 0) + first == target).astype(F32).astype(BF16)
    return dot_nn(place, folded)


def corners_in(lanes, lat, lon, capacity, channels):
    slots = lanes.shape[0]
    source = corner_slots(lat, lon, capacity, (32, slots), 0)
    place = (iota((32, slots), 1) == source).astype(F32).astype(BF16)
    folded = dot_nn(place, lanes).astype(BF16)
    spread = dot_nn(folded, corner_fold((META, channels), 0))
    kept = jnp.where(corner_mask(spread.shape), spread, 0.0)
    return [jnp.sum(kept[8 * index : 8 * index + 8], axis=0, keepdims=True) for index in range(4)]


def dispatch_kernel(
    capacity,
    tile_hbm,
    cell_hbm,
    frac_hbm,
    radiance_hbm,
    state_hbm,
    box_hbm,
    slot_hbm,
    west_hbm,
    east_hbm,
    top_hbm,
    bottom_hbm,
    tile_ref,
    cell_ref,
    frac_ref,
    radiance_ref,
    first_ref,
    last_ref,
    box_ref,
    slot_ref,
    west_ref,
    east_ref,
    semaphores,
    out_semaphores,
):
    rows, columns, _ = state_hbm.shape
    lat, lon = lax.axis_index("lat"), lax.axis_index("lon")
    waiting = copies(
        semaphores,
        (tile_hbm, tile_ref),
        (cell_hbm, cell_ref),
        (frac_hbm, frac_ref),
        (radiance_hbm, radiance_ref),
        (state_hbm.at[:, pl.ds(0, 16), :], first_ref),
        (state_hbm.at[:, pl.ds(columns - 16, 16), :], last_ref),
        (state_hbm.at[0], top_hbm),
        (state_hbm.at[rows - 1], bottom_hbm),
    )
    slots, width = box_ref.shape
    devices = slots // capacity
    count = tile_ref.shape[1]
    channels = width - META
    earlier = (iota((count, count), 0) < iota((count, count), 1)).astype(F32).astype(BF16)
    for copy in waiting[:3]:
        copy.wait()
    tile = tile_ref[...]
    match = (iota((devices, count), 0) == tile).astype(F32)
    before = dot_nn(match.astype(BF16), earlier)
    position = jnp.sum(before * match, axis=0, keepdims=True)
    slot = tile * capacity + position.astype(jnp.int32)
    slot_ref[...] = slot
    leaving = [pltpu.make_async_copy(slot_ref, slot_hbm, out_semaphores.at[0])]
    leaving[0].start()
    cell = cell_ref[...]
    low, side = frac_ref[0:1, :], frac_ref[1:2, :]
    fields = (
        (cell >> 7).astype(F32),
        (cell & 127).astype(F32),
        (1.0 - low) * (1.0 - side),
        (1.0 - low) * side,
        low * (1.0 - side),
        low * side,
    )
    number = iota((META, count), 0)
    meta = jnp.zeros((META, count), F32)
    for index, field in enumerate(fields):
        meta = jnp.where(number == index, field, meta)
    meta = meta.astype(BF16)
    waiting[3].wait()
    waiting[4].wait()
    waiting[5].wait()
    cells = []
    for block_ref, at, side_ref, side_hbm in (
        (first_ref, 0, west_ref, west_hbm),
        (last_ref, 15, east_ref, east_hbm),
    ):
        lines = [block_ref[row].astype(F32)[at : at + 1] for row in range(rows)]
        cells += [lines[0], lines[-1]]
        side_ref[...] = jnp.concatenate(lines, axis=0).astype(BF16)
        leaving.append(
            pltpu.make_async_copy(side_ref, side_hbm, out_semaphores.at[len(leaving)])
        )
        leaving[-1].start()
    cells = (cells[0], cells[2], cells[1], cells[3])
    step = slots // 4
    for index in range(4):
        part = slice(index * step, (index + 1) * step)
        place = (iota((step, count), 0) + index * step == slot).astype(F32).astype(BF16)
        corners = corners_out(cells, lat, lon, capacity, index * step, step)
        box_ref[part, channels:] = (dot_nt(place, meta) + corners).astype(BF16)
        box_ref[part, :channels] = dot_nn(place, radiance_ref[...]).astype(BF16)
        leaving.append(
            pltpu.make_async_copy(
                box_ref.at[part, :], box_hbm.at[part, :], out_semaphores.at[len(leaving)]
            )
        )
        leaving[-1].start()
    for copy in leaving + waiting[6:]:
        copy.wait()


CHUNK = 512


def fill_row(shifted, row, center, left, right):
    columns = center.shape[0]
    place = iota(center.shape, 0)
    where = pl.ds(row * columns, columns)
    shifted[1, where, :] = center.astype(BF16)
    shifted[0, where, :] = jnp.where(place == 0, left, pltpu.roll(center, 1, 0)).astype(BF16)
    shifted[2, where, :] = jnp.where(
        place == columns - 1, right, pltpu.roll(center, columns - 1, 0)
    ).astype(BF16)


def no_halo_rows(shifted, rows, columns):
    zero = jnp.zeros((3, columns, shifted.shape[2]), BF16)
    shifted[:, :columns, :] = zero
    shifted[:, (rows + 1) * columns :, :] = zero


def halo_terms(left, right, north, south, corners, weight_ref):
    rows, columns = left.shape[0], north.shape[0]

    def along_row(center, first, last, row_step):
        place = iota(center.shape, 0)
        west = jnp.where(place == 0, first, pltpu.roll(center, 1, 0))
        east = jnp.where(place == columns - 1, last, pltpu.roll(center, columns - 1, 0))
        return sum(
            dot_nn(window.astype(BF16), weight_ref[row_step, col_step])
            for col_step, window in enumerate((west, center, east))
        )

    def along_column(side, col_step):
        place = iota(side.shape, 0)
        up = jnp.where(place == 0, 0.0, pltpu.roll(side, 1, 0))
        down = jnp.where(place == rows - 1, 0.0, pltpu.roll(side, rows - 1, 0))
        return sum(
            dot_nn(window.astype(BF16), weight_ref[row_step, col_step])
            for row_step, window in enumerate((up, side, down))
        )

    top = along_row(north, corners[0], corners[1], 0)
    bottom = along_row(south, corners[2], corners[3], 2)
    west, east = along_column(left, 0), along_column(right, 2)
    return top, bottom, west, east


def with_ends(term, first, last):
    place = iota(term.shape, 0)
    ends = jnp.where(place == 0, first, jnp.where(place == term.shape[0] - 1, last, 0.0))
    return term + ends


def convolve_rows(shifted, weight_ref, start, count, columns):
    total = None
    for row_step in range(3):
        for col_step in range(3):
            first = start + row_step * columns
            term = dot_nn(
                shifted[col_step, first : first + count, :], weight_ref[row_step, col_step]
            )
            total = term if total is None else total + term
    return total


BORDERS = 4


def forecast_kernel(
    columns,
    state_hbm,
    slope_hbm,
    weight_hbm,
    out_hbm,
    mirrored_hbm,
    borders_hbm,
    state_ref,
    slope_ref,
    weight_ref,
    out_ref,
    mirrored_ref,
    borders_ref,
    shifted,
    semaphores,
    out_semaphores,
):
    cells, channels = state_ref.shape
    rows = cells // columns
    waiting = copies(
        semaphores, (state_hbm, state_ref), (weight_hbm, weight_ref), (slope_hbm, slope_ref)
    )
    no_halo_rows(shifted, rows, columns)
    for copy in waiting:
        copy.wait()
    zero = jnp.zeros((1, channels), F32)
    per = CHUNK // columns
    steps = cells // CHUNK
    leaving = []
    for index in range(steps + 1):
        if index < steps:
            for row in range(index * per, (index + 1) * per):
                center = state_ref[row * columns : (row + 1) * columns, :].astype(F32)
                fill_row(shifted, row + 1, center, zero, zero)
        if index > 0:
            start = (index - 1) * CHUNK
            part = slice(start, start + CHUNK)
            response = convolve_rows(shifted, weight_ref, start, CHUNK, columns)
            slope = slope_ref[part, :].astype(F32)
            total = state_ref[part, :].astype(F32) + slope * response
            out_ref[part, :] = total.astype(BF16)
            leaving.append(
                pltpu.make_async_copy(
                    out_ref.at[part, :], out_hbm.at[part, :], out_semaphores.at[index - 1]
                )
            )
            leaving[-1].start()
            for inner in range(per):
                row = (index - 1) * per + inner
                first, last = inner * columns, (inner + 1) * columns - 1
                for number, line in enumerate(
                    (slope[first : first + 1], slope[last : last + 1])
                    + (total[first : first + 1], total[last : last + 1])
                ):
                    at = number * rows + row
                    borders_ref[at : at + 1, :] = line
            if index == 1:
                borders_ref[BORDERS * rows : BORDERS * rows + columns, :] = total[:columns]
            if index == steps:
                borders_ref[BORDERS * rows + columns :, :] = total[CHUNK - columns :]
    for row_step in range(3):
        for col_step in range(3):
            mirrored_ref[row_step, col_step] = (
                weight_ref[2 - row_step, 2 - col_step].astype(F32).T.astype(BF16)
            )
    leaving += [
        pltpu.make_async_copy(mirrored_ref, mirrored_hbm, out_semaphores.at[steps]),
        pltpu.make_async_copy(borders_ref, borders_hbm, out_semaphores.at[steps + 1]),
    ]
    leaving[-2].start()
    leaving[-1].start()
    for copy in leaving:
        copy.wait()


def gradient_kernel(
    columns,
    adjoint_hbm,
    fields_hbm,
    slope_hbm,
    weight_hbm,
    out_hbm,
    adjoint,
    fields_ref,
    slope_ref,
    weight_ref,
    out_ref,
    shifted,
    semaphores,
    out_semaphores,
):
    waiting = copies(
        semaphores,
        (fields_hbm, fields_ref),
        (adjoint_hbm, adjoint),
        (slope_hbm, slope_ref),
        (weight_hbm, weight_ref),
    )
    cells, channels = slope_ref.shape
    rows = cells // columns
    no_halo_rows(shifted, rows, columns)
    waiting[0].wait()
    around = turned_weights(fields_ref[...], columns)
    for copy in waiting[1:]:
        copy.wait()
    zero = jnp.zeros((1, channels), F32)
    per = CHUNK // columns
    steps = cells // CHUNK
    leaving = []
    for index in range(steps + 1):
        if index < steps:
            part = slice(index * CHUNK, (index + 1) * CHUNK)
            weights = [blend(*around, index * per + row) for row in range(per)]
            spread = dot_nn(jnp.concatenate(weights, axis=0), adjoint[...])
            out_ref[part, :] = spread
            pulled = slope_ref[part, :].astype(F32) * spread
            for inner in range(per):
                center = pulled[inner * columns : (inner + 1) * columns, :]
                fill_row(shifted, index * per + inner + 1, center, zero, zero)
        if index > 0:
            start = (index - 1) * CHUNK
            part = slice(start, start + CHUNK)
            out_ref[part, :] += convolve_rows(shifted, weight_ref, start, CHUNK, columns)
            leaving.append(
                pltpu.make_async_copy(
                    out_ref.at[part, :], out_hbm.at[part, :], out_semaphores.at[index - 1]
                )
            )
            leaving[-1].start()
    for copy in leaving:
        copy.wait()


def finish_kernel(
    capacity,
    gradient_hbm,
    slot_hbm,
    box_hbm,
    weight_hbm,
    left_hbm,
    right_hbm,
    north_hbm,
    south_hbm,
    out_hbm,
    departures_hbm,
    slot_ref,
    box_ref,
    weight_ref,
    left_ref,
    right_ref,
    north_ref,
    south_ref,
    lines_ref,
    sides_ref,
    departures_ref,
    semaphores,
    out_semaphores,
):
    del gradient_hbm
    lat, lon = lax.axis_index("lat"), lax.axis_index("lon")
    rows, columns, cell_channels = out_hbm.shape
    inner = pl.ds(8, columns - 16)
    places = (
        (lines_ref.at[0], out_hbm.at[0, inner, :]),
        (lines_ref.at[1], out_hbm.at[rows - 1, inner, :]),
        (sides_ref.at[0], out_hbm.at[:, pl.ds(0, 8), :]),
        (sides_ref.at[1], out_hbm.at[:, pl.ds(columns - 8, 8), :]),
    )
    waiting = copies(
        semaphores,
        (slot_hbm, slot_ref),
        (box_hbm, box_ref),
        (weight_hbm, weight_ref),
        (left_hbm, left_ref),
        (right_hbm, right_ref),
        (north_hbm, north_ref),
        (south_hbm, south_ref),
        *((there, here) for here, there in places),
    )
    slots = box_ref.shape[0]
    count = slot_ref.shape[1]
    channels = box_ref.shape[1] - META
    waiting[0].wait()
    turned = jnp.broadcast_to(slot_ref[...].astype(F32), (128, count)).T
    lane = iota((count, 128), 1).astype(F32)
    parts = [
        (lane + float(first) == turned).astype(F32).astype(BF16) for first in range(0, slots, 128)
    ]
    place = jnp.concatenate(parts, axis=1)
    waiting[1].wait()
    step = count // 2
    leaving = []
    for index in range(2):
        part = slice(index * step, (index + 1) * step)
        departures_ref[part, :] = dot_nn(place[part, :], box_ref[:, :channels])
        leaving.append(
            pltpu.make_async_copy(
                departures_ref.at[part, :], departures_hbm.at[part, :], out_semaphores.at[4 + index]
            )
        )
        leaving[-1].start()
    for copy in waiting[2:]:
        copy.wait()
    top, bottom, west, east = halo_terms(
        left_ref[...].astype(F32),
        right_ref[...].astype(F32),
        north_ref[...].astype(F32),
        south_ref[...].astype(F32),
        corners_in(box_ref[:, channels:], lat, lon, capacity, cell_channels),
        weight_ref,
    )
    lines_ref[0] += top[8 : columns - 8]
    lines_ref[1] += bottom[8 : columns - 8]
    leaving += copies(out_semaphores, *places[:2])
    place = iota((8, cell_channels), 0)
    for number, side, at in ((0, west, 0), (1, east, 7)):
        ends = (top[:8], bottom[:8]) if number == 0 else (top[-8:], bottom[-8:])
        for row in range(rows):
            term = jnp.where(place == at, side[row : row + 1], 0.0)
            if row == 0:
                term = term + ends[0]
            if row == rows - 1:
                term = term + ends[1]
            sides_ref[number, row] += term
        leaving.append(pltpu.make_async_copy(*places[2 + number], out_semaphores.at[2 + number]))
        leaving[-1].start()
    for copy in leaving:
        copy.wait()


def sigmoid(value):
    return 0.5 + 0.5 * jnp.tanh(0.5 * value)


def blend(row_low, row_high, upper, lower, at):
    at = jnp.asarray(at, BF16)
    zero = jnp.zeros(upper.shape, BF16)
    return jnp.where(row_low == at, upper, jnp.where(row_high == at, lower, zero))


def turned_weights(fields, columns):
    slots = fields.shape[1]
    row, column, w00, w01, w10, w11 = (fields[index : index + 1, :] for index in range(FIELDS))
    place = iota((columns, slots), 0).astype(F32)
    here, beside = place == column, place == column + 1.0
    upper = (jnp.where(here, w00, 0.0) + jnp.where(beside, w01, 0.0)).astype(BF16)
    lower = (jnp.where(here, w10, 0.0) + jnp.where(beside, w11, 0.0)).astype(BF16)
    row_low = jnp.broadcast_to(row, (columns, slots)).astype(BF16)
    row_high = jnp.broadcast_to(row + 1.0, (columns, slots)).astype(BF16)
    return row_low, row_high, upper, lower


def observe_kernel(
    columns,
    capacity,
    box_hbm,
    grid_hbm,
    weight_in_hbm,
    weight_mid_hbm,
    weight_out_hbm,
    vectors_hbm,
    slope_hbm,
    borders_hbm,
    conv_hbm,
    left_hbm,
    right_hbm,
    north_hbm,
    south_hbm,
    departures_hbm,
    adjoint_hbm,
    fields_hbm,
    west_ref,
    east_ref,
    top_ref,
    bottom_ref,
    box_ref,
    grid_ref,
    weight_in_ref,
    weight_mid_ref,
    weight_out_ref,
    vectors_ref,
    ends_ref,
    borders_ref,
    conv_ref,
    left_ref,
    right_ref,
    north_ref,
    south_ref,
    sampled,
    departures_ref,
    adjoint,
    fields_ref,
    semaphores,
    out_semaphores,
):
    lat, lon = lax.axis_index("lat"), lax.axis_index("lon")
    slots, width = box_ref.shape
    cells, grid_channels = grid_ref.shape
    channels = width - META
    hidden = weight_in_ref.shape[1]
    rows = cells // columns
    waiting = copies(
        semaphores,
        (box_hbm, box_ref),
        (left_hbm, left_ref),
        (right_hbm, right_ref),
        (north_hbm, north_ref),
        (south_hbm, south_ref),
        (conv_hbm, conv_ref),
        (slope_hbm.at[pl.ds(0, columns), :], ends_ref.at[0]),
        (slope_hbm.at[pl.ds(cells - columns, columns), :], ends_ref.at[1]),
        (borders_hbm, borders_ref),
        (grid_hbm, grid_ref),
        (weight_in_hbm, weight_in_ref),
        (vectors_hbm, vectors_ref),
        (weight_mid_hbm, weight_mid_ref),
        (weight_out_hbm, weight_out_ref),
    )
    waiting[0].wait()
    pick = (iota((16, META), 0) == iota((16, META), 1)).astype(F32).astype(BF16)
    fields_ref[...] = dot_nt(pick, box_ref[:, channels:])
    fields_out = pltpu.make_async_copy(fields_ref, fields_hbm, out_semaphores.at[0])
    fields_out.start()
    pick = iota((META, FIELDS * columns), 0) == iota((META, FIELDS * columns), 1) // columns
    wide = dot_nn(box_ref[:, channels:], pick.astype(F32).astype(BF16))
    row, column, w00, w01, w10, w11 = (
        wide[:, index * columns : (index + 1) * columns] for index in range(FIELDS)
    )
    lane = iota((slots, columns), 1).astype(F32)
    here, beside = lane == column, lane == column + 1.0
    upper = (jnp.where(here, w00, 0.0) + jnp.where(beside, w01, 0.0)).astype(BF16)
    lower = (jnp.where(here, w10, 0.0) + jnp.where(beside, w11, 0.0)).astype(BF16)
    row_low = row.astype(BF16)
    row_high = (row + 1.0).astype(BF16)
    for copy in waiting[1:10]:
        copy.wait()
    top, bottom, west, east = halo_terms(
        left_ref[...].astype(F32),
        right_ref[...].astype(F32),
        north_ref[...].astype(F32),
        south_ref[...].astype(F32),
        corners_in(box_ref[:, channels:], lat, lon, capacity, grid_channels),
        conv_ref,
    )
    place = iota((16, grid_channels), 0)
    for number, side, others, at, first in (
        (0, west, (top[:1], bottom[:1]), 0, 0),
        (1, east, (top[-1:], bottom[-1:]), 15, columns - 16),
    ):
        slope = borders_ref[number * rows : (number + 1) * rows, :]
        value = borders_ref[(number + 2) * rows : (number + 3) * rows, :]
        value = value + slope * with_ends(side, *others)
        for row in range(rows):
            part = slice(row * columns + first, row * columns + first + 16)
            grid_ref[part, :] = jnp.where(
                place == at, value[row : row + 1], grid_ref[part, :].astype(F32)
            ).astype(BF16)
    for number, line, at in ((0, top, 0), (1, bottom, rows - 1)):
        first = BORDERS * rows + number * columns
        line = with_ends(line, west[at : at + 1], east[at : at + 1])
        grid_ref[at * columns : (at + 1) * columns, :] = (
            borders_ref[first : first + columns, :] + ends_ref[number].astype(F32) * line
        ).astype(BF16)
    per = 8
    for block in range(rows // per):
        parts = [
            blend(row_low, row_high, upper, lower, block * per + index) for index in range(per)
        ]
        first = block * per * columns
        term = dot_nn(jnp.concatenate(parts, axis=1), grid_ref[first : first + per * columns, :])
        if block == 0:
            sampled[...] = term
        else:
            sampled[...] += term
    for copy in waiting[10:]:
        copy.wait()
    bias_in = vectors_ref[:, :hidden]
    bias_mid = vectors_ref[:, hidden : 2 * hidden]
    bias_out = vectors_ref[:, 2 * hidden : 2 * hidden + channels]
    inv_error = vectors_ref[:, 2 * hidden + channels :]
    step = 256
    for start in range(0, slots, step):
        part = slice(start, start + step)
        pre = dot_nn(sampled[part, :].astype(BF16), weight_in_ref[...]) + bias_in
        gate = sigmoid(pre)
        act = pre * gate
        slope_first = gate + act * (1.0 - gate)
        pre = dot_nn(act.astype(BF16), weight_mid_ref[...]) + bias_mid
        gate = sigmoid(pre)
        act = pre * gate
        slope_second = gate + act * (1.0 - gate)
        evolved = dot_nn(act.astype(BF16), weight_out_ref[...]) + bias_out
        departures = (evolved - box_ref[part, :channels].astype(F32)) * inv_error
        departures_ref[part, :channels] = departures.astype(BF16)
        back = (departures * inv_error).astype(BF16)
        back = (dot_nt(back, weight_out_ref[...]) * slope_second).astype(BF16)
        back = (dot_nt(back, weight_mid_ref[...]) * slope_first).astype(BF16)
        adjoint[part, :] = dot_nt(back, weight_in_ref[...]).astype(BF16)
    results = copies(out_semaphores.at[pl.ds(2, 1)], (adjoint, adjoint_hbm))
    fields = fields_ref[...]
    around = turned_weights(fields, columns)
    cells_out = []
    for at, index, edge_ref in ((0, 0, top_ref), (rows - 1, 1, bottom_ref)):
        spread = dot_nn(blend(*around, at), adjoint[...])
        pulled = ends_ref[index].astype(F32) * spread
        edge_ref[...] = pulled.astype(BF16)
        cells_out += [pulled[:1], pulled[columns - 1 :]]
    departures_ref[:, channels:] = corners_out(cells_out, lat, lon, capacity, 0, slots).astype(BF16)
    results += copies(out_semaphores.at[pl.ds(1, 1)], (departures_ref, departures_hbm))
    row, column, w00, w01, w10, w11 = (fields[index : index + 1, :] for index in range(FIELDS))
    place = iota((rows, slots), 0).astype(F32)
    here, below = place == row, place == row + 1.0
    zero = jnp.zeros((rows, slots), F32)
    for at, index, edge_ref, high, low in (
        (0.0, 0, west_ref, w00, w10),
        (columns - 2.0, 1, east_ref, w01, w11),
    ):
        chosen = column == at
        weights = jnp.where(
            here & chosen, high, jnp.where(below & chosen, low, zero)
        ).astype(BF16)
        slope = borders_ref[index * rows : (index + 1) * rows, :]
        edge_ref[...] = (slope * dot_nn(weights, adjoint[...])).astype(BF16)
    fields_out.wait()
    for copy in results:
        copy.wait()


def beside(west, east):
    count = lax.axis_size("lon")
    onward = [(i, (i + 1) % count) for i in range(count)]
    left = lax.ppermute(east, "lon", onward)
    right = lax.ppermute(west, "lon", [(target, source) for source, target in onward])
    return left, right


def over(top, bottom):
    down = [(i, i + 1) for i in range(lax.axis_size("lat") - 1)]
    north = lax.ppermute(bottom, "lat", down)
    south = lax.ppermute(top, "lat", [(target, source) for source, target in down])
    return north, south


def body(
    model_state,
    tangent_slope,
    conv_weight,
    weight_in,
    bias_in,
    weight_mid,
    bias_mid,
    weight_out,
    bias_out,
    obs_tile,
    obs_cell,
    obs_frac,
    radiance,
    inv_error,
):
    rows, columns, channels = model_state.shape
    cells = rows * columns
    devices = lax.axis_size("lat") * lax.axis_size("lon")
    count, bands = radiance.shape
    capacity = 2 * count // devices
    slots = devices * capacity
    hidden = weight_in.shape[1]
    sds = jax.ShapeDtypeStruct
    dma = pltpu.SemaphoreType.DMA

    def exchange(box):
        return lax.all_to_all(
            box.reshape(devices, capacity, -1), ("lat", "lon"), split_axis=0, concat_axis=0, tiled=True
        ).reshape(slots, -1)

    box, slot, west, east, top, bottom = kernel_call(
        functools.partial(dispatch_kernel, capacity),
        (
            sds((slots, bands + META), BF16),
            sds((1, count), jnp.int32),
            sds((rows, channels), BF16),
            sds((rows, channels), BF16),
            sds((columns, channels), BF16),
            sds((columns, channels), BF16),
        ),
        (HBM,) * 6,
        (HBM,) * 5,
        (
            pltpu.VMEM((1, count), jnp.int32),
            pltpu.VMEM((1, count), jnp.int32),
            pltpu.VMEM((2, count), F32),
            pltpu.VMEM((count, bands), BF16),
            pltpu.VMEM((rows, 16, channels), BF16),
            pltpu.VMEM((rows, 16, channels), BF16),
            pltpu.VMEM((slots, bands + META), BF16),
            pltpu.VMEM((1, count), jnp.int32),
            pltpu.VMEM((rows, channels), BF16),
            pltpu.VMEM((rows, channels), BF16),
            dma((8,)),
            dma((7,)),
        ),
        flops=2 * slots * count * (bands + META),
        moved=2 * slots * (bands + META),
        name="dispatch",
    )(obs_tile.reshape(1, count), obs_cell.reshape(1, count), obs_frac.T, radiance, model_state)
    arrived = exchange(box)

    conv_flops = 2 * 9 * cells * channels * channels
    steps = cells // CHUNK
    halo_scratch = (
        pltpu.VMEM((rows, channels), BF16),
        pltpu.VMEM((rows, channels), BF16),
        pltpu.VMEM((columns, channels), BF16),
        pltpu.VMEM((columns, channels), BF16),
    )
    shifted = pltpu.VMEM((3, (rows + 2) * columns, channels), BF16)
    borders_shape = (BORDERS * rows + 2 * columns, channels)
    flat_slope = tangent_slope.reshape(cells, channels)
    halo = beside(west, east) + over(top, bottom)
    forecast, mirrored, borders = kernel_call(
        functools.partial(forecast_kernel, columns),
        (sds((cells, channels), BF16), sds(conv_weight.shape, BF16), sds(borders_shape, F32)),
        (HBM,) * 3,
        (HBM,) * 3,
        (
            pltpu.VMEM((cells, channels), BF16),
            pltpu.VMEM((cells, channels), BF16),
            pltpu.VMEM(conv_weight.shape, BF16),
            pltpu.VMEM((cells, channels), BF16),
            pltpu.VMEM(conv_weight.shape, BF16),
            pltpu.VMEM(borders_shape, F32),
            shifted,
            dma((3,)),
            dma((steps + 2,)),
        ),
        flops=conv_flops,
        moved=6 * cells * channels,
        room=512,
        name="forecast",
    )(model_state.reshape(cells, channels), flat_slope, conv_weight)

    vectors = jnp.concatenate([bias_in, bias_mid, bias_out, inv_error]).reshape(1, -1)
    network_flops = 2 * slots * (channels * hidden + hidden * hidden + hidden * bands)
    departures_box, adjoint, fields, west, east, top, bottom = kernel_call(
        functools.partial(observe_kernel, columns, capacity),
        (
            sds((slots, bands + META), BF16),
            sds((slots, channels), BF16),
            sds((16, slots), F32),
            sds((rows, channels), BF16),
            sds((rows, channels), BF16),
            sds((columns, channels), BF16),
            sds((columns, channels), BF16),
        ),
        (HBM,) * 3 + (VMEM,) * 4,
        (HBM,) * 13,
        (
            pltpu.VMEM((slots, bands + META), BF16),
            pltpu.VMEM((cells, channels), BF16),
            pltpu.VMEM(weight_in.shape, BF16),
            pltpu.VMEM(weight_mid.shape, BF16),
            pltpu.VMEM(weight_out.shape, BF16),
            pltpu.VMEM(vectors.shape, F32),
            pltpu.VMEM((2, columns, channels), BF16),
            pltpu.VMEM(borders_shape, F32),
            pltpu.VMEM(conv_weight.shape, BF16),
            *halo_scratch,
            pltpu.VMEM((slots, channels), F32),
            pltpu.VMEM((slots, bands + META), BF16),
            pltpu.VMEM((slots, channels), BF16),
            pltpu.VMEM((16, slots), F32),
            dma((14,)),
            dma((3,)),
        ),
        flops=2 * network_flops + 2 * slots * cells * channels,
        moved=2 * cells * channels,
        room=1024 + 256,
        name="observe",
    )(
        arrived,
        forecast,
        weight_in,
        weight_mid,
        weight_out,
        vectors,
        flat_slope,
        borders,
        conv_weight,
        *halo,
    )

    returned = exchange(departures_box)
    halo = beside(west, east) + over(top, bottom)
    gradient, = kernel_call(
        functools.partial(gradient_kernel, columns),
        (sds((cells, channels), F32),),
        (HBM,),
        (HBM,) * 4,
        (
            pltpu.VMEM((slots, channels), BF16),
            pltpu.VMEM((16, slots), F32),
            pltpu.VMEM((cells, channels), BF16),
            pltpu.VMEM(conv_weight.shape, BF16),
            pltpu.VMEM((cells, channels), F32),
            shifted,
            dma((4,)),
            dma((steps,)),
        ),
        flops=conv_flops + 2 * slots * cells * channels,
        moved=4 * cells * channels,
        room=400,
        name="gradient",
    )(adjoint, fields, flat_slope, mirrored)
    gradient, departures = kernel_call(
        functools.partial(finish_kernel, capacity),
        (sds((rows, columns, channels), F32), sds((count, bands), F32)),
        (HBM, HBM),
        (HBM,) * 8,
        (
            pltpu.VMEM((1, count), jnp.int32),
            pltpu.VMEM((slots, bands + META), BF16),
            pltpu.VMEM(conv_weight.shape, BF16),
            *halo_scratch,
            pltpu.VMEM((2, columns - 16, channels), F32),
            pltpu.VMEM((2, rows, 8, channels), F32),
            pltpu.VMEM((count, bands), F32),
            dma((11,)),
            dma((6,)),
        ),
        flops=2 * slots * count * bands,
        moved=4 * count * bands,
        aliases={0: 0},
        room=1024 + 192,
        name="finish",
    )(gradient.reshape(rows, columns, channels), slot, returned, mirrored, *halo)
    return departures, gradient


def solution(mesh):
    in_specs = (
        P("lat", "lon", None),
        P("lat", "lon", None),
        P(),
        P(),
        P(),
        P(),
        P(),
        P(),
        P(),
        P(("lat", "lon"), None),
        P(("lat", "lon")),
        P(("lat", "lon"), None),
        P(("lat", "lon"), None),
        P(),
    )
    out_specs = (P(("lat", "lon"), None), P("lat", "lon", None))
    return jax.shard_map(body, mesh=mesh, in_specs=in_specs, out_specs=out_specs, check_vma=False)
```

```python
import functools

import jax
import jax.numpy as jnp
from jax import lax
from jax.experimental import pallas as pl
from jax.experimental.pallas import tpu as pltpu
from jax.sharding import PartitionSpec as P

F32 = jnp.float32
BF16 = jnp.bfloat16
META = 128
FIELDS = 6
VMEM_KIB = 60 * 1024 + 512
ROOM = 1024 + 256


def dot_nt(left, right):
    return lax.dot_general(left, right, (((1,), (1,)), ((), ())), preferred_element_type=F32)


def dot_nn(left, right):
    return jnp.dot(left, right, preferred_element_type=F32)


def iota(shape, dim):
    return lax.broadcasted_iota(jnp.int32, shape, dim)


def kernel_call(body, outs, out_spaces, in_spaces, scratch=(), flops=0, moved=0, room=0, aliases=None, name=None):
    return pl.pallas_call(
        body,
        out_shape=outs,
        in_specs=[pl.BlockSpec(memory_space=space) for space in in_spaces],
        out_specs=[pl.BlockSpec(memory_space=space) for space in out_spaces],
        scratch_shapes=list(scratch),
        input_output_aliases=aliases or {},
        name=name,
        compiler_params=pltpu.CompilerParams(vmem_limit_bytes=(VMEM_KIB - room) * 1024),
        cost_estimate=pl.CostEstimate(flops=flops, bytes_accessed=moved, transcendentals=0),
    )


HBM = pltpu.HBM
VMEM = pltpu.VMEM


def copies(semaphores, *pairs):
    started = []
    for index, (source, target) in enumerate(pairs):
        copy = pltpu.make_async_copy(source, target, semaphores.at[index])
        copy.start()
        started.append(copy)
    return started


CORNER_LANE = 32
CORNER_WIDTH = 32


def diagonal_blocks(lat, lon, capacity):
    lats, lons = lax.axis_size("lat"), lax.axis_size("lon")
    blocks = []
    for down, right in ((-1, -1), (-1, 1), (1, -1), (1, 1)):
        row, column = lat + down, lax.rem(lon + right + lons, lons)
        inside = (row >= 0) & (row < lats)
        first = jnp.where(inside, row * lons + column, 0) * capacity
        aligned = pl.multiple_of((first // 16) * 16, 16)
        blocks.append((inside, aligned, lax.rem(first, 16)))
    return blocks


def corner_fold(shape, lane_dim):
    value, lane = iota(shape, 1 - lane_dim), iota(shape, lane_dim)
    chosen = (value % CORNER_WIDTH == lane - CORNER_LANE) & (lane >= CORNER_LANE)
    return (chosen & (lane < CORNER_LANE + CORNER_WIDTH)).astype(F32).astype(BF16)


def corner_mask(shape):
    return iota(shape, 1) // CORNER_WIDTH == iota(shape, 0) % 8


def corners_out(cells, lat, lon, capacity, box_ref, channels):
    width = cells[0].shape[1]
    spread = jnp.concatenate([jnp.broadcast_to(cell, (8, width)) for cell in cells], axis=0)
    kept = jnp.where(corner_mask(spread.shape), spread, 0.0).astype(BF16)
    folded = dot_nn(kept, corner_fold((width, META), 1))
    half = (iota((16, META), 0) // 8) * 8
    for index, (inside, first, own) in enumerate(diagonal_blocks(lat, lon, capacity)):
        lines = folded[8 * index : 8 * index + 8]
        lines = jnp.where(half == own, jnp.concatenate([lines, lines], axis=0), 0.0)

        @pl.when(inside)
        def _():
            which = pl.ds(first, 16)
            box_ref[which, channels:] = (box_ref[which, channels:].astype(F32) + lines).astype(BF16)


def corners_in(box_ref, lat, lon, capacity, channels, width):
    lines = []
    for inside, first, own in diagonal_blocks(lat, lon, capacity):
        block = box_ref[pl.ds(first, 16), channels:].astype(F32)
        mine = jnp.where(own == 0, block[:8], block[8:])
        lines.append(jnp.where(inside, mine, 0.0))
    folded = jnp.concatenate(lines, axis=0).astype(BF16)
    spread = dot_nn(folded, corner_fold((META, width), 0))
    kept = jnp.where(corner_mask(spread.shape), spread, 0.0)
    return [jnp.sum(kept[8 * index : 8 * index + 8], axis=0, keepdims=True) for index in range(4)]


def dispatch_kernel(
    capacity,
    tile_hbm,
    cell_hbm,
    frac_hbm,
    radiance_hbm,
    state_hbm,
    box_hbm,
    slot_hbm,
    west_hbm,
    east_hbm,
    top_hbm,
    bottom_hbm,
    tile_ref,
    cell_ref,
    frac_ref,
    radiance_ref,
    first_ref,
    last_ref,
    box_ref,
    slot_ref,
    west_ref,
    east_ref,
    lines_ref,
    semaphores,
    out_semaphores,
):
    rows, columns, _ = state_hbm.shape
    lat, lon = lax.axis_index("lat"), lax.axis_index("lon")
    waiting = copies(
        semaphores,
        (tile_hbm, tile_ref),
        (cell_hbm, cell_ref),
        (frac_hbm, frac_ref),
        (radiance_hbm, radiance_ref),
        (state_hbm.at[:, pl.ds(0, 16), :], first_ref),
        (state_hbm.at[:, pl.ds(columns - 16, 16), :], last_ref),
        (state_hbm.at[0], lines_ref.at[0]),
        (state_hbm.at[rows - 1], lines_ref.at[1]),
    )
    slots, width = box_ref.shape
    devices = slots // capacity
    count = tile_ref.shape[1]
    channels = width - META
    earlier = (iota((count, count), 0) < iota((count, count), 1)).astype(F32).astype(BF16)
    for copy in waiting[:3]:
        copy.wait()
    tile = tile_ref[...]
    match = (iota((devices, count), 0) == tile).astype(F32)
    before = dot_nn(match.astype(BF16), earlier)
    position = jnp.sum(before * match, axis=0, keepdims=True)
    slot = tile * capacity + position.astype(jnp.int32)
    slot_ref[...] = slot
    leaving = [pltpu.make_async_copy(slot_ref, slot_hbm, out_semaphores.at[0])]
    leaving[0].start()
    cell = cell_ref[...]
    low, side = frac_ref[0:1, :], frac_ref[1:2, :]
    fields = (
        (cell >> 7).astype(F32),
        (cell & 127).astype(F32),
        (1.0 - low) * (1.0 - side),
        (1.0 - low) * side,
        low * (1.0 - side),
        low * side,
    )
    number = iota((META, count), 0)
    meta = jnp.zeros((META, count), F32)
    for index, field in enumerate(fields):
        meta = jnp.where(number == index, field, meta)
    meta = meta.astype(BF16)
    waiting[3].wait()
    for copy in waiting[4:]:
        copy.wait()
    for index, line_hbm in enumerate((top_hbm, bottom_hbm)):
        leaving.append(
            pltpu.make_async_copy(lines_ref.at[index], line_hbm, out_semaphores.at[len(leaving)])
        )
        leaving[-1].start()
    cells = []
    for block_ref, at, side_ref, side_hbm in (
        (first_ref, 0, west_ref, west_hbm),
        (last_ref, 15, east_ref, east_hbm),
    ):
        lines = [block_ref[row].astype(F32)[at : at + 1] for row in range(rows)]
        cells += [lines[0], lines[-1]]
        side_ref[...] = jnp.concatenate(lines, axis=0).astype(BF16)
        leaving.append(
            pltpu.make_async_copy(side_ref, side_hbm, out_semaphores.at[len(leaving)])
        )
        leaving[-1].start()
    cells = (cells[0], cells[2], cells[1], cells[3])
    step = slots // 4
    for index in range(4):
        part = slice(index * step, (index + 1) * step)
        place = (iota((step, count), 0) + index * step == slot).astype(F32).astype(BF16)
        box_ref[part, channels:] = dot_nt(place, meta).astype(BF16)
        box_ref[part, :channels] = dot_nn(place, radiance_ref[...]).astype(BF16)
    corners_out(cells, lat, lon, capacity, box_ref, channels)
    leaving.append(pltpu.make_async_copy(box_ref, box_hbm, out_semaphores.at[len(leaving)]))
    leaving[-1].start()
    for copy in leaving:
        copy.wait()


CHUNK = 512
FORECAST_GROUPS = (0, 2, 6, 8)
GRADIENT_GROUPS = (0, 4, 8)


def fill_row(shifted, row, center, left, right):
    columns = center.shape[0]
    place = iota(center.shape, 0)
    where = pl.ds(row * columns, columns)
    shifted[1, where, :] = center.astype(BF16)
    shifted[0, where, :] = jnp.where(place == 0, left, pltpu.roll(center, 1, 0)).astype(BF16)
    shifted[2, where, :] = jnp.where(
        place == columns - 1, right, pltpu.roll(center, columns - 1, 0)
    ).astype(BF16)


def no_halo_rows(shifted, rows, columns):
    zero = jnp.zeros((3, columns, shifted.shape[2]), BF16)
    shifted[:, :columns, :] = zero
    shifted[:, (rows + 1) * columns :, :] = zero


def halo_terms(left, right, north, south, corners, weight_ref, mirror):
    rows, columns = left.shape[0], north.shape[0]
    product, weight_of = taps(weight_ref, mirror)

    def row_windows(center, first, last):
        place = iota(center.shape, 0)
        west = jnp.where(place == 0, first, pltpu.roll(center, 1, 0))
        east = jnp.where(place == columns - 1, last, pltpu.roll(center, columns - 1, 0))
        return west, center, east

    def column_windows(side):
        place = iota(side.shape, 0)
        up = jnp.where(place == 0, 0.0, pltpu.roll(side, 1, 0))
        down = jnp.where(place == rows - 1, 0.0, pltpu.roll(side, rows - 1, 0))
        return up, side, down

    lines = {0: row_windows(north, *corners[:2]), 2: row_windows(south, *corners[2:])}
    sides = {0: column_windows(left), 2: column_windows(right)}
    line_terms, side_terms = {0: 0.0, 2: 0.0}, {0: 0.0, 2: 0.0}
    for row_step in range(3):
        for col_step in range(3):
            windows = []
            if row_step != 1:
                windows.append(lines[row_step][col_step])
            if col_step != 1:
                windows.append(sides[col_step][row_step])
            if not windows:
                continue
            term = product(
                jnp.concatenate(windows, axis=0).astype(BF16), weight_of(row_step, col_step)
            )
            if row_step != 1:
                line_terms[row_step] += term[:columns]
            if col_step != 1:
                side_terms[col_step] += term[-rows:]
    top, bottom, west, east = line_terms[0], line_terms[2], side_terms[0], side_terms[2]
    return top, bottom, west, east


def with_ends(term, first, last):
    place = iota(term.shape, 0)
    ends = jnp.where(place == 0, first, jnp.where(place == term.shape[0] - 1, last, 0.0))
    return term + ends


def taps(weight_ref, mirror):
    if mirror:
        return dot_nt, lambda row_step, col_step: weight_ref[2 - row_step, 2 - col_step]
    return dot_nn, lambda row_step, col_step: weight_ref[row_step, col_step]


def convolve_rows(shifted, weight_ref, start, count, columns, mirror):
    product, weight_of = taps(weight_ref, mirror)
    total = None
    for row_step in range(3):
        for col_step in range(3):
            first = start + row_step * columns
            term = product(shifted[col_step, first : first + count, :], weight_of(row_step, col_step))
            total = term if total is None else total + term
    return total


def span_copy(source, target, semaphore, first, last):
    which = pl.ds(first * CHUNK, (last - first) * CHUNK)
    return pltpu.make_async_copy(source.at[which, :], target.at[which, :], semaphore)


BORDERS = 4


def forecast_kernel(
    columns,
    state_hbm,
    slope_hbm,
    weight_hbm,
    out_hbm,
    borders_hbm,
    state_ref,
    slope_ref,
    weight_ref,
    out_ref,
    borders_ref,
    shifted,
    weight_semaphore,
    state_semaphores,
    slope_semaphores,
    out_semaphores,
):
    cells, channels = state_ref.shape
    rows = cells // columns
    per = CHUNK // columns
    steps = cells // CHUNK
    zero = jnp.zeros((1, channels), F32)
    groups = list(zip(FORECAST_GROUPS[:-1], FORECAST_GROUPS[1:]))

    def copies_in(number):
        first, last = groups[number]
        ahead = (first + 1 if number else 0), min(last + 1, steps)
        found = [
            span_copy(slope_hbm, slope_ref, slope_semaphores.at[number], first, last)
        ]
        if ahead[0] < ahead[1]:
            found.append(span_copy(state_hbm, state_ref, state_semaphores.at[number], *ahead))
        if number == 0:
            found.append(pltpu.make_async_copy(weight_hbm, weight_ref, weight_semaphore.at[0]))
        return found[::-1]

    def fill(index):
        for row in range(index * per, (index + 1) * per):
            center = state_ref[row * columns : (row + 1) * columns, :].astype(F32)
            fill_row(shifted, row + 1, center, zero, zero)

    coming = copies_in(0)
    for copy in coming:
        copy.start()
    no_halo_rows(shifted, rows, columns)
    out = []
    for number, (low, high) in enumerate(groups):
        for copy in coming:
            copy.wait()
        if number + 1 < len(groups):
            coming = copies_in(number + 1)
            for copy in coming:
                copy.start()
        if number == 0:
            fill(0)
        for index in range(low, high):
            if index + 1 < steps:
                fill(index + 1)
            part = slice(index * CHUNK, (index + 1) * CHUNK)
            response = convolve_rows(shifted, weight_ref, part.start, CHUNK, columns, False)
            slope = slope_ref[part, :].astype(F32)
            total = state_ref[part, :].astype(F32) + slope * response
            out_ref[part, :] = total.astype(BF16)
            for inner in range(per):
                row = index * per + inner
                first, last = inner * columns, (inner + 1) * columns - 1
                for kind, line in enumerate(
                    (slope[first : first + 1], slope[last : last + 1])
                    + (total[first : first + 1], total[last : last + 1])
                ):
                    at = kind * rows + row
                    borders_ref[at : at + 1, :] = line
            if index == 0:
                borders_ref[BORDERS * rows : BORDERS * rows + columns, :] = total[:columns]
            if index == steps - 1:
                borders_ref[BORDERS * rows + columns :, :] = total[CHUNK - columns :]
        out.append(span_copy(out_ref, out_hbm, out_semaphores.at[number], low, high))
        out[-1].start()
    out.append(pltpu.make_async_copy(borders_ref, borders_hbm, out_semaphores.at[steps]))
    out[-1].start()
    for copy in out:
        copy.wait()


def gradient_kernel(
    columns,
    adjoint_hbm,
    fields_hbm,
    slope_hbm,
    weight_hbm,
    out_hbm,
    adjoint,
    fields_ref,
    slope_ref,
    weight_ref,
    out_ref,
    shifted,
    semaphores,
    slope_semaphores,
    out_semaphores,
):
    cells, channels = slope_ref.shape
    rows = cells // columns
    per = CHUNK // columns
    steps = cells // CHUNK
    waiting = copies(semaphores, (fields_hbm, fields_ref), (adjoint_hbm, adjoint))
    zero = jnp.zeros((1, channels), F32)
    groups = list(zip(GRADIENT_GROUPS[:-1], GRADIENT_GROUPS[1:]))

    def copies_in(number):
        first, last = groups[number]
        ahead = (first + 1 if number else 0), min(last + 1, steps)
        if ahead[0] == ahead[1]:
            return []
        return [span_copy(slope_hbm, slope_ref, slope_semaphores.at[number], *ahead)]

    coming = copies_in(0) + [pltpu.make_async_copy(weight_hbm, weight_ref, semaphores.at[2])]
    for copy in coming:
        copy.start()
    no_halo_rows(shifted, rows, columns)
    waiting[0].wait()
    around = turned_weights(fields_ref[...], columns)
    waiting[1].wait()

    def spread(index):
        weights = [blend(*around, index * per + row) for row in range(per)]
        out_ref[index * CHUNK : (index + 1) * CHUNK, :] = dot_nn(
            jnp.concatenate(weights, axis=0), adjoint[...]
        )

    def fill(index):
        part = slice(index * CHUNK, (index + 1) * CHUNK)
        pulled = slope_ref[part, :].astype(F32) * out_ref[part, :]
        for inner in range(per):
            center = pulled[inner * columns : (inner + 1) * columns, :]
            fill_row(shifted, index * per + inner + 1, center, zero, zero)

    for index in range(steps):
        spread(index)
    out = []
    for number, (low, high) in enumerate(groups):
        for copy in coming:
            copy.wait()
        if number + 1 < len(groups):
            coming = copies_in(number + 1)
            for copy in coming:
                copy.start()
        if number == 0:
            fill(0)
        for index in range(low, high):
            if index + 1 < steps:
                fill(index + 1)
            part = slice(index * CHUNK, (index + 1) * CHUNK)
            out_ref[part, :] += convolve_rows(shifted, weight_ref, part.start, CHUNK, columns, True)
        out.append(span_copy(out_ref, out_hbm, out_semaphores.at[number], low, high))
        out[-1].start()
    for copy in out:
        copy.wait()


def finish_kernel(
    capacity,
    gradient_hbm,
    slot_hbm,
    box_hbm,
    weight_hbm,
    left_hbm,
    right_hbm,
    north_hbm,
    south_hbm,
    out_hbm,
    departures_hbm,
    slot_ref,
    box_ref,
    weight_ref,
    left_ref,
    right_ref,
    north_ref,
    south_ref,
    lines_ref,
    sides_ref,
    departures_ref,
    semaphores,
    out_semaphores,
):
    del gradient_hbm
    lat, lon = lax.axis_index("lat"), lax.axis_index("lon")
    rows, columns, cell_channels = out_hbm.shape
    inner = pl.ds(8, columns - 16)
    places = (
        (lines_ref.at[0], out_hbm.at[0, inner, :]),
        (lines_ref.at[1], out_hbm.at[rows - 1, inner, :]),
        (sides_ref.at[0], out_hbm.at[:, pl.ds(0, 8), :]),
        (sides_ref.at[1], out_hbm.at[:, pl.ds(columns - 8, 8), :]),
    )
    waiting = copies(
        semaphores,
        (slot_hbm, slot_ref),
        (box_hbm, box_ref),
        (weight_hbm, weight_ref),
        (left_hbm, left_ref),
        (right_hbm, right_ref),
        (north_hbm, north_ref),
        (south_hbm, south_ref),
        *((there, here) for here, there in places),
    )
    slots = box_ref.shape[0]
    count = slot_ref.shape[1]
    channels = box_ref.shape[1] - META
    waiting[0].wait()
    turned = jnp.broadcast_to(slot_ref[...].astype(F32), (128, count)).T
    lane = iota((count, 128), 1).astype(F32)
    parts = [
        (lane + float(first) == turned).astype(F32).astype(BF16) for first in range(0, slots, 128)
    ]
    place = jnp.concatenate(parts, axis=1)
    waiting[1].wait()
    step = count // 2
    leaving = []
    for index in range(2):
        part = slice(index * step, (index + 1) * step)
        departures_ref[part, :] = dot_nn(place[part, :], box_ref[:, :channels])
        leaving.append(
            pltpu.make_async_copy(
                departures_ref.at[part, :], departures_hbm.at[part, :], out_semaphores.at[4 + index]
            )
        )
        leaving[-1].start()
    for copy in waiting[2:]:
        copy.wait()
    top, bottom, west, east = halo_terms(
        left_ref[...].astype(F32),
        right_ref[...].astype(F32),
        north_ref[...].astype(F32),
        south_ref[...].astype(F32),
        corners_in(box_ref, lat, lon, capacity, channels, cell_channels),
        weight_ref,
        True,
    )
    lines_ref[0] += top[8 : columns - 8]
    lines_ref[1] += bottom[8 : columns - 8]
    leaving += copies(out_semaphores, *places[:2])
    place = iota((8, cell_channels), 0)
    for number, side, at in ((0, west, 0), (1, east, 7)):
        ends = (top[:8], bottom[:8]) if number == 0 else (top[-8:], bottom[-8:])
        for row in range(rows):
            term = jnp.where(place == at, side[row : row + 1], 0.0)
            if row == 0:
                term = term + ends[0]
            if row == rows - 1:
                term = term + ends[1]
            sides_ref[number, row] += term
        leaving.append(pltpu.make_async_copy(*places[2 + number], out_semaphores.at[2 + number]))
        leaving[-1].start()
    for copy in leaving:
        copy.wait()


def sigmoid(value):
    return 0.5 + 0.5 * jnp.tanh(0.5 * value)


def blend(row_low, row_high, upper, lower, at):
    at = jnp.asarray(at, BF16)
    zero = jnp.zeros(upper.shape, BF16)
    return jnp.where(row_low == at, upper, jnp.where(row_high == at, lower, zero))


def turned_weights(fields, columns):
    slots = fields.shape[1]
    row, column, w00, w01, w10, w11 = (fields[index : index + 1, :] for index in range(FIELDS))
    place = iota((columns, slots), 0).astype(F32)
    here, beside = place == column, place == column + 1.0
    upper = (jnp.where(here, w00, 0.0) + jnp.where(beside, w01, 0.0)).astype(BF16)
    lower = (jnp.where(here, w10, 0.0) + jnp.where(beside, w11, 0.0)).astype(BF16)
    row_low = jnp.broadcast_to(row, (columns, slots)).astype(BF16)
    row_high = jnp.broadcast_to(row + 1.0, (columns, slots)).astype(BF16)
    return row_low, row_high, upper, lower


def observe_kernel(
    columns,
    capacity,
    box_hbm,
    grid_hbm,
    weight_in_hbm,
    weight_mid_hbm,
    weight_out_hbm,
    bias_in_hbm,
    bias_mid_hbm,
    bias_out_hbm,
    inv_error_hbm,
    slope_hbm,
    borders_hbm,
    conv_hbm,
    left_hbm,
    right_hbm,
    north_hbm,
    south_hbm,
    departures_hbm,
    adjoint_hbm,
    fields_hbm,
    west_ref,
    east_ref,
    top_ref,
    bottom_ref,
    box_ref,
    grid_ref,
    weight_in_ref,
    weight_mid_ref,
    weight_out_ref,
    bias_in_ref,
    bias_mid_ref,
    bias_out_ref,
    inv_error_ref,
    ends_ref,
    borders_ref,
    conv_ref,
    left_ref,
    right_ref,
    north_ref,
    south_ref,
    sampled,
    departures_ref,
    adjoint,
    fields_ref,
    semaphores,
    out_semaphores,
):
    lat, lon = lax.axis_index("lat"), lax.axis_index("lon")
    slots, width = box_ref.shape
    cells, grid_channels = grid_ref.shape
    channels = width - META
    hidden = weight_in_ref.shape[1]
    rows = cells // columns
    lanes, spare = pl.ds(0, channels), pl.ds(channels, META)
    waiting = copies(
        semaphores,
        (box_hbm.at[:, spare], box_ref.at[:, spare]),
        (left_hbm, left_ref),
        (right_hbm, right_ref),
        (north_hbm, north_ref),
        (south_hbm, south_ref),
        (conv_hbm, conv_ref),
        (grid_hbm, grid_ref),
        (slope_hbm.at[pl.ds(0, columns), :], ends_ref.at[0]),
        (slope_hbm.at[pl.ds(cells - columns, columns), :], ends_ref.at[1]),
        (borders_hbm, borders_ref),
        (weight_in_hbm, weight_in_ref),
        (bias_in_hbm, bias_in_ref),
        (bias_mid_hbm, bias_mid_ref),
        (bias_out_hbm, bias_out_ref),
        (inv_error_hbm, inv_error_ref),
        (weight_mid_hbm, weight_mid_ref),
        (weight_out_hbm, weight_out_ref),
        (box_hbm.at[:, lanes], box_ref.at[:, lanes]),
    )
    waiting[0].wait()
    pick = (iota((16, META), 0) == iota((16, META), 1)).astype(F32).astype(BF16)
    fields_ref[...] = dot_nt(pick, box_ref[:, channels:])
    fields_out = pltpu.make_async_copy(fields_ref, fields_hbm, out_semaphores.at[0])
    fields_out.start()
    pick = iota((META, FIELDS * columns), 0) == iota((META, FIELDS * columns), 1) // columns
    wide = dot_nn(box_ref[:, channels:], pick.astype(F32).astype(BF16))
    row, column, w00, w01, w10, w11 = (
        wide[:, index * columns : (index + 1) * columns] for index in range(FIELDS)
    )
    lane = iota((slots, columns), 1).astype(F32)
    here, beside = lane == column, lane == column + 1.0
    upper = (jnp.where(here, w00, 0.0) + jnp.where(beside, w01, 0.0)).astype(BF16)
    lower = (jnp.where(here, w10, 0.0) + jnp.where(beside, w11, 0.0)).astype(BF16)
    row_low = row.astype(BF16)
    row_high = (row + 1.0).astype(BF16)
    for copy in waiting[1:6]:
        copy.wait()
    top, bottom, west, east = halo_terms(
        left_ref[...].astype(F32),
        right_ref[...].astype(F32),
        north_ref[...].astype(F32),
        south_ref[...].astype(F32),
        corners_in(box_ref, lat, lon, capacity, channels, grid_channels),
        conv_ref,
        False,
    )
    for copy in waiting[6:10]:
        copy.wait()
    place = iota((16, grid_channels), 0)
    for number, side, others, at, first in (
        (0, west, (top[:1], bottom[:1]), 0, 0),
        (1, east, (top[-1:], bottom[-1:]), 15, columns - 16),
    ):
        slope = borders_ref[number * rows : (number + 1) * rows, :]
        value = borders_ref[(number + 2) * rows : (number + 3) * rows, :]
        value = value + slope * with_ends(side, *others)
        for row in range(rows):
            part = slice(row * columns + first, row * columns + first + 16)
            grid_ref[part, :] = jnp.where(
                place == at, value[row : row + 1], grid_ref[part, :].astype(F32)
            ).astype(BF16)
    for number, line, at in ((0, top, 0), (1, bottom, rows - 1)):
        first = BORDERS * rows + number * columns
        line = with_ends(line, west[at : at + 1], east[at : at + 1])
        grid_ref[at * columns : (at + 1) * columns, :] = (
            borders_ref[first : first + columns, :] + ends_ref[number].astype(F32) * line
        ).astype(BF16)
    strip = 256
    for start in range(0, slots, strip):
        part = slice(start, start + strip)
        parts = [blend(row_low[part], row_high[part], upper[part], lower[part], at) for at in range(rows)]
        sampled[part, :] = dot_nn(jnp.concatenate(parts, axis=1), grid_ref[...])
    for copy in waiting[10:]:
        copy.wait()
    bias_in, bias_mid, bias_out, inv_error = (
        ref[...].reshape(1, -1) for ref in (bias_in_ref, bias_mid_ref, bias_out_ref, inv_error_ref)
    )
    step = 512
    results = []
    for start in range(0, slots, step):
        part = slice(start, start + step)
        pre = dot_nn(sampled[part, :].astype(BF16), weight_in_ref[...]) + bias_in
        gate = sigmoid(pre)
        act = pre * gate
        slope_first = gate + act * (1.0 - gate)
        pre = dot_nn(act.astype(BF16), weight_mid_ref[...]) + bias_mid
        gate = sigmoid(pre)
        act = pre * gate
        slope_second = gate + act * (1.0 - gate)
        evolved = dot_nn(act.astype(BF16), weight_out_ref[...]) + bias_out
        departures = (evolved - box_ref[part, :channels].astype(F32)) * inv_error
        departures_ref[part, :channels] = departures.astype(BF16)
        back = (departures * inv_error).astype(BF16)
        back = (dot_nt(back, weight_out_ref[...]) * slope_second).astype(BF16)
        back = (dot_nt(back, weight_mid_ref[...]) * slope_first).astype(BF16)
        adjoint[part, :] = dot_nt(back, weight_in_ref[...]).astype(BF16)
        which = pl.ds(start, step)
        results += copies(
            out_semaphores.at[pl.ds(1 + len(results), 2)],
            (departures_ref.at[which, lanes], departures_hbm.at[which, lanes]),
            (adjoint.at[which, :], adjoint_hbm.at[which, :]),
        )
    fields = fields_ref[...]
    around = turned_weights(fields, columns)
    row, column, w00, w01, w10, w11 = (fields[index : index + 1, :] for index in range(FIELDS))
    place = iota((rows, slots), 0).astype(F32)
    here, below = place == row, place == row + 1.0
    zero = jnp.zeros((rows, slots), F32)
    weights = [blend(*around, 0), blend(*around, rows - 1)]
    for at, high, low in ((0.0, w00, w10), (columns - 2.0, w01, w11)):
        chosen = column == at
        weights.append(
            jnp.where(here & chosen, high, jnp.where(below & chosen, low, zero)).astype(BF16)
        )
    spread = dot_nn(jnp.concatenate(weights, axis=0), adjoint[...])
    cells_out = []
    for index, edge_ref in enumerate((top_ref, bottom_ref)):
        first = index * columns
        pulled = ends_ref[index].astype(F32) * spread[first : first + columns]
        edge_ref[...] = pulled.astype(BF16)
        cells_out += [pulled[:1], pulled[columns - 1 :]]
    for index, edge_ref in enumerate((west_ref, east_ref)):
        first = 2 * columns + index * rows
        slope = borders_ref[index * rows : (index + 1) * rows, :]
        edge_ref[...] = (slope * spread[first : first + rows]).astype(BF16)
    departures_ref[:, channels:] = jnp.zeros((slots, META), BF16)
    corners_out(cells_out, lat, lon, capacity, departures_ref, channels)
    results += copies(
        out_semaphores.at[pl.ds(1 + len(results), 1)],
        (departures_ref.at[:, spare], departures_hbm.at[:, spare]),
    )
    fields_out.wait()
    for copy in results:
        copy.wait()


def beside(west, east):
    count = lax.axis_size("lon")
    onward = [(i, (i + 1) % count) for i in range(count)]
    left = lax.ppermute(east, "lon", onward)
    right = lax.ppermute(west, "lon", [(target, source) for source, target in onward])
    return left, right


def over(top, bottom):
    down = [(i, i + 1) for i in range(lax.axis_size("lat") - 1)]
    north = lax.ppermute(bottom, "lat", down)
    south = lax.ppermute(top, "lat", [(target, source) for source, target in down])
    return north, south


def body(
    model_state,
    tangent_slope,
    conv_weight,
    weight_in,
    bias_in,
    weight_mid,
    bias_mid,
    weight_out,
    bias_out,
    obs_tile,
    obs_cell,
    obs_frac,
    radiance,
    inv_error,
):
    rows, columns, channels = model_state.shape
    cells = rows * columns
    devices = lax.axis_size("lat") * lax.axis_size("lon")
    count, bands = radiance.shape
    capacity = 2 * count // devices
    slots = devices * capacity
    hidden = weight_in.shape[1]
    sds = jax.ShapeDtypeStruct
    dma = pltpu.SemaphoreType.DMA

    def exchange(box):
        return lax.all_to_all(
            box.reshape(devices, capacity, -1), ("lat", "lon"), split_axis=0, concat_axis=0, tiled=True
        ).reshape(slots, -1)

    box, slot, west, east, top, bottom = kernel_call(
        functools.partial(dispatch_kernel, capacity),
        (
            sds((slots, bands + META), BF16),
            sds((1, count), jnp.int32),
            sds((rows, channels), BF16),
            sds((rows, channels), BF16),
            sds((columns, channels), BF16),
            sds((columns, channels), BF16),
        ),
        (HBM,) * 6,
        (HBM,) * 5,
        (
            pltpu.VMEM((1, count), jnp.int32),
            pltpu.VMEM((1, count), jnp.int32),
            pltpu.VMEM((2, count), F32),
            pltpu.VMEM((count, bands), BF16),
            pltpu.VMEM((rows, 16, channels), BF16),
            pltpu.VMEM((rows, 16, channels), BF16),
            pltpu.VMEM((slots, bands + META), BF16),
            pltpu.VMEM((1, count), jnp.int32),
            pltpu.VMEM((rows, channels), BF16),
            pltpu.VMEM((rows, channels), BF16),
            pltpu.VMEM((2, columns, channels), BF16),
            dma((8,)),
            dma((6,)),
        ),
        flops=2 * slots * count * (bands + META),
        moved=2 * slots * (bands + META),
        name="dispatch",
    )(obs_tile.reshape(1, count), obs_cell.reshape(1, count), obs_frac.T, radiance, model_state)
    arrived = exchange(box)

    conv_flops = 2 * 9 * cells * channels * channels
    steps = cells // CHUNK
    halo_scratch = (
        pltpu.VMEM((rows, channels), BF16),
        pltpu.VMEM((rows, channels), BF16),
        pltpu.VMEM((columns, channels), BF16),
        pltpu.VMEM((columns, channels), BF16),
    )
    shifted = pltpu.VMEM((3, (rows + 2) * columns, channels), BF16)
    borders_shape = (BORDERS * rows + 2 * columns, channels)
    flat_slope = tangent_slope.reshape(cells, channels)
    halo = beside(west, east) + over(top, bottom)
    forecast, borders = kernel_call(
        functools.partial(forecast_kernel, columns),
        (sds((cells, channels), BF16), sds(borders_shape, F32)),
        (HBM,) * 2,
        (HBM,) * 3,
        (
            pltpu.VMEM((cells, channels), BF16),
            pltpu.VMEM((cells, channels), BF16),
            pltpu.VMEM(conv_weight.shape, BF16),
            pltpu.VMEM((cells, channels), BF16),
            pltpu.VMEM(borders_shape, F32),
            shifted,
            dma((1,)),
            dma((steps,)),
            dma((steps,)),
            dma((steps + 1,)),
        ),
        flops=conv_flops,
        moved=6 * cells * channels,
        room=512,
        name="forecast",
    )(model_state.reshape(cells, channels), flat_slope, conv_weight)

    network_flops = 2 * slots * (channels * hidden + hidden * hidden + hidden * bands)
    departures_box, adjoint, fields, west, east, top, bottom = kernel_call(
        functools.partial(observe_kernel, columns, capacity),
        (
            sds((slots, bands + META), BF16),
            sds((slots, channels), BF16),
            sds((16, slots), F32),
            sds((rows, channels), BF16),
            sds((rows, channels), BF16),
            sds((columns, channels), BF16),
            sds((columns, channels), BF16),
        ),
        (HBM,) * 3 + (VMEM,) * 4,
        (HBM,) * 16,
        (
            pltpu.VMEM((slots, bands + META), BF16),
            pltpu.VMEM((cells, channels), BF16),
            pltpu.VMEM(weight_in.shape, BF16),
            pltpu.VMEM(weight_mid.shape, BF16),
            pltpu.VMEM(weight_out.shape, BF16),
            *(pltpu.VMEM(vector.shape, F32) for vector in (bias_in, bias_mid, bias_out, inv_error)),
            pltpu.VMEM((2, columns, channels), BF16),
            pltpu.VMEM(borders_shape, F32),
            pltpu.VMEM(conv_weight.shape, BF16),
            *halo_scratch,
            pltpu.VMEM((slots, channels), F32),
            pltpu.VMEM((slots, bands + META), BF16),
            pltpu.VMEM((slots, channels), BF16),
            pltpu.VMEM((16, slots), F32),
            dma((18,)),
            dma((6,)),
        ),
        flops=2 * network_flops + 2 * slots * cells * channels,
        moved=2 * cells * channels,
        room=ROOM,
        name="observe",
    )(
        arrived,
        forecast,
        weight_in,
        weight_mid,
        weight_out,
        bias_in,
        bias_mid,
        bias_out,
        inv_error,
        flat_slope,
        borders,
        conv_weight,
        *halo,
    )

    returned = exchange(departures_box)
    halo = beside(west, east) + over(top, bottom)
    gradient, = kernel_call(
        functools.partial(gradient_kernel, columns),
        (sds((cells, channels), F32),),
        (HBM,),
        (HBM,) * 4,
        (
            pltpu.VMEM((slots, channels), BF16),
            pltpu.VMEM((16, slots), F32),
            pltpu.VMEM((cells, channels), BF16),
            pltpu.VMEM(conv_weight.shape, BF16),
            pltpu.VMEM((cells, channels), F32),
            shifted,
            dma((3,)),
            dma((steps,)),
            dma((steps,)),
        ),
        flops=conv_flops + 2 * slots * cells * channels,
        moved=4 * cells * channels,
        room=400,
        name="gradient",
    )(adjoint, fields, flat_slope, conv_weight)
    gradient, departures = kernel_call(
        functools.partial(finish_kernel, capacity),
        (sds((rows, columns, channels), F32), sds((count, bands), F32)),
        (HBM, HBM),
        (HBM,) * 8,
        (
            pltpu.VMEM((1, count), jnp.int32),
            pltpu.VMEM((slots, bands + META), BF16),
            pltpu.VMEM(conv_weight.shape, BF16),
            *halo_scratch,
            pltpu.VMEM((2, columns - 16, channels), F32),
            pltpu.VMEM((2, rows, 8, channels), F32),
            pltpu.VMEM((count, bands), F32),
            dma((11,)),
            dma((6,)),
        ),
        flops=2 * slots * count * bands,
        moved=4 * count * bands,
        aliases={0: 0},
        room=1024 + 192,
        name="finish",
    )(gradient.reshape(rows, columns, channels), slot, returned, conv_weight, *halo)
    return departures, gradient


def solution(mesh):
    in_specs = (
        P("lat", "lon", None),
        P("lat", "lon", None),
        P(),
        P(),
        P(),
        P(),
        P(),
        P(),
        P(),
        P(("lat", "lon"), None),
        P(("lat", "lon")),
        P(("lat", "lon"), None),
        P(("lat", "lon"), None),
        P(),
    )
    out_specs = (P(("lat", "lon"), None), P("lat", "lon", None))
    return jax.shard_map(body, mesh=mesh, in_specs=in_specs, out_specs=out_specs, check_vma=False)
```

```python
import functools

import jax
import jax.numpy as jnp
from jax import lax
from jax.experimental import pallas as pl
from jax.experimental.pallas import tpu as pltpu
from jax.sharding import PartitionSpec as P

F32 = jnp.float32
BF16 = jnp.bfloat16
META = 128
FIELDS = 6
VMEM_KIB = 60 * 1024 + 512
ROOM = 1024 + 256


def dot_nt(left, right):
    return lax.dot_general(left, right, (((1,), (1,)), ((), ())), preferred_element_type=F32)


def dot_nn(left, right):
    return jnp.dot(left, right, preferred_element_type=F32)


def iota(shape, dim):
    return lax.broadcasted_iota(jnp.int32, shape, dim)


def kernel_call(body, outs, out_spaces, in_spaces, scratch=(), flops=0, moved=0, room=0, aliases=None, name=None):
    return pl.pallas_call(
        body,
        out_shape=outs,
        in_specs=[pl.BlockSpec(memory_space=space) for space in in_spaces],
        out_specs=[pl.BlockSpec(memory_space=space) for space in out_spaces],
        scratch_shapes=list(scratch),
        input_output_aliases=aliases or {},
        name=name,
        compiler_params=pltpu.CompilerParams(vmem_limit_bytes=(VMEM_KIB - room) * 1024),
        cost_estimate=pl.CostEstimate(flops=flops, bytes_accessed=moved, transcendentals=0),
    )


HBM = pltpu.HBM
VMEM = pltpu.VMEM


def copies(semaphores, *pairs):
    started = []
    for index, (source, target) in enumerate(pairs):
        copy = pltpu.make_async_copy(source, target, semaphores.at[index])
        copy.start()
        started.append(copy)
    return started


CORNER_LANE = 32
CORNER_WIDTH = 32


def diagonal_blocks(lat, lon, capacity):
    lats, lons = lax.axis_size("lat"), lax.axis_size("lon")
    blocks = []
    for down, right in ((-1, -1), (-1, 1), (1, -1), (1, 1)):
        row, column = lat + down, lax.rem(lon + right + lons, lons)
        inside = (row >= 0) & (row < lats)
        first = jnp.where(inside, row * lons + column, 0) * capacity
        aligned = pl.multiple_of((first // 16) * 16, 16)
        blocks.append((inside, aligned, lax.rem(first, 16)))
    return blocks


def corner_fold(shape, lane_dim):
    value, lane = iota(shape, 1 - lane_dim), iota(shape, lane_dim)
    chosen = (value % CORNER_WIDTH == lane - CORNER_LANE) & (lane >= CORNER_LANE)
    return (chosen & (lane < CORNER_LANE + CORNER_WIDTH)).astype(F32).astype(BF16)


def corner_mask(shape):
    return iota(shape, 1) // CORNER_WIDTH == iota(shape, 0) % 8


def corners_out(cells, lat, lon, capacity, box_ref, channels):
    width = cells[0].shape[1]
    spread = jnp.concatenate([jnp.broadcast_to(cell, (8, width)) for cell in cells], axis=0)
    kept = jnp.where(corner_mask(spread.shape), spread, 0.0).astype(BF16)
    folded = dot_nn(kept, corner_fold((width, META), 1))
    half = (iota((16, META), 0) // 8) * 8
    for index, (inside, first, own) in enumerate(diagonal_blocks(lat, lon, capacity)):
        lines = folded[8 * index : 8 * index + 8]
        lines = jnp.where(half == own, jnp.concatenate([lines, lines], axis=0), 0.0)

        @pl.when(inside)
        def _():
            which = pl.ds(first, 16)
            box_ref[which, channels:] = (box_ref[which, channels:].astype(F32) + lines).astype(BF16)


def corners_in(box_ref, lat, lon, capacity, channels, width):
    lines = []
    for inside, first, own in diagonal_blocks(lat, lon, capacity):
        block = box_ref[pl.ds(first, 16), channels:].astype(F32)
        mine = jnp.where(own == 0, block[:8], block[8:])
        lines.append(jnp.where(inside, mine, 0.0))
    folded = jnp.concatenate(lines, axis=0).astype(BF16)
    spread = dot_nn(folded, corner_fold((META, width), 0))
    kept = jnp.where(corner_mask(spread.shape), spread, 0.0)
    return [jnp.sum(kept[8 * index : 8 * index + 8], axis=0, keepdims=True) for index in range(4)]


def dispatch_kernel(
    capacity,
    tile_hbm,
    cell_hbm,
    frac_hbm,
    radiance_hbm,
    state_hbm,
    box_hbm,
    slot_hbm,
    west_hbm,
    east_hbm,
    top_hbm,
    bottom_hbm,
    tile_ref,
    cell_ref,
    frac_ref,
    radiance_ref,
    first_ref,
    last_ref,
    box_ref,
    slot_ref,
    west_ref,
    east_ref,
    lines_ref,
    semaphores,
    out_semaphores,
):
    rows, columns, _ = state_hbm.shape
    lat, lon = lax.axis_index("lat"), lax.axis_index("lon")
    waiting = copies(
        semaphores,
        (tile_hbm, tile_ref),
        (cell_hbm, cell_ref),
        (frac_hbm, frac_ref),
        (radiance_hbm, radiance_ref),
        (state_hbm.at[:, pl.ds(0, 16), :], first_ref),
        (state_hbm.at[:, pl.ds(columns - 16, 16), :], last_ref),
        (state_hbm.at[0], lines_ref.at[0]),
        (state_hbm.at[rows - 1], lines_ref.at[1]),
    )
    slots, width = box_ref.shape
    devices = slots // capacity
    count = tile_ref.shape[1]
    channels = width - META
    earlier = (iota((count, count), 0) < iota((count, count), 1)).astype(F32).astype(BF16)
    for copy in waiting[:3]:
        copy.wait()
    tile = tile_ref[...]
    match = (iota((devices, count), 0) == tile).astype(F32)
    before = dot_nn(match.astype(BF16), earlier)
    position = jnp.sum(before * match, axis=0, keepdims=True)
    slot = tile * capacity + position.astype(jnp.int32)
    slot_ref[...] = slot
    leaving = [pltpu.make_async_copy(slot_ref, slot_hbm, out_semaphores.at[0])]
    leaving[0].start()
    cell = cell_ref[...]
    low, side = frac_ref[0:1, :], frac_ref[1:2, :]
    fields = (
        (cell >> 7).astype(F32),
        (cell & 127).astype(F32),
        (1.0 - low) * (1.0 - side),
        (1.0 - low) * side,
        low * (1.0 - side),
        low * side,
    )
    number = iota((META, count), 0)
    meta = jnp.zeros((META, count), F32)
    for index, field in enumerate(fields):
        meta = jnp.where(number == index, field, meta)
    meta = meta.astype(BF16)
    for copy in waiting[4:]:
        copy.wait()
    for index, line_hbm in enumerate((top_hbm, bottom_hbm)):
        leaving.append(
            pltpu.make_async_copy(lines_ref.at[index], line_hbm, out_semaphores.at[len(leaving)])
        )
        leaving[-1].start()
    cells = []
    for block_ref, at, side_ref, side_hbm in (
        (first_ref, 0, west_ref, west_hbm),
        (last_ref, 15, east_ref, east_hbm),
    ):
        lines = [block_ref[row].astype(F32)[at : at + 1] for row in range(rows)]
        cells += [lines[0], lines[-1]]
        side_ref[...] = jnp.concatenate(lines, axis=0).astype(BF16)
        leaving.append(
            pltpu.make_async_copy(side_ref, side_hbm, out_semaphores.at[len(leaving)])
        )
        leaving[-1].start()
    cells = (cells[0], cells[2], cells[1], cells[3])
    places = []
    step = slots // 2
    for index in range(2):
        part = slice(index * step, (index + 1) * step)
        places.append((iota((step, count), 0) + index * step == slot).astype(F32).astype(BF16))
        box_ref[part, channels:] = dot_nt(places[index], meta).astype(BF16)
    corners_out(cells, lat, lon, capacity, box_ref, channels)
    waiting[3].wait()
    for index in range(2):
        part = slice(index * step, (index + 1) * step)
        box_ref[part, :channels] = dot_nn(places[index], radiance_ref[...]).astype(BF16)
        leaving.append(
            pltpu.make_async_copy(
                box_ref.at[part, :], box_hbm.at[part, :], out_semaphores.at[len(leaving)]
            )
        )
        leaving[-1].start()
    for copy in leaving:
        copy.wait()


CHUNK = 512
FORECAST_GROUPS = (0, 2, 6, 8)
GRADIENT_GROUPS = (0, 4, 8)


def fill_row(shifted, row, center, left, right):
    columns = center.shape[0]
    place = iota(center.shape, 0)
    where = pl.ds(row * columns, columns)
    shifted[1, where, :] = center.astype(BF16)
    shifted[0, where, :] = jnp.where(place == 0, left, pltpu.roll(center, 1, 0)).astype(BF16)
    shifted[2, where, :] = jnp.where(
        place == columns - 1, right, pltpu.roll(center, columns - 1, 0)
    ).astype(BF16)


def no_halo_rows(shifted, rows, columns):
    zero = jnp.zeros((3, columns, shifted.shape[2]), BF16)
    shifted[:, :columns, :] = zero
    shifted[:, (rows + 1) * columns :, :] = zero


def halo_terms(left, right, north, south, corners, weight_ref, mirror):
    rows, columns = left.shape[0], north.shape[0]
    lat = lax.axis_index("lat")
    north = jnp.where(lat > 0, north, 0.0)
    south = jnp.where(lat < lax.axis_size("lat") - 1, south, 0.0)
    product, weight_of = taps(weight_ref, mirror)

    def row_windows(center, first, last):
        place = iota(center.shape, 0)
        west = jnp.where(place == 0, first, pltpu.roll(center, 1, 0))
        east = jnp.where(place == columns - 1, last, pltpu.roll(center, columns - 1, 0))
        return west, center, east

    def column_windows(side):
        place = iota(side.shape, 0)
        up = jnp.where(place == 0, 0.0, pltpu.roll(side, 1, 0))
        down = jnp.where(place == rows - 1, 0.0, pltpu.roll(side, rows - 1, 0))
        return up, side, down

    lines = {0: row_windows(north, *corners[:2]), 2: row_windows(south, *corners[2:])}
    sides = {0: column_windows(left), 2: column_windows(right)}
    line_terms, side_terms = {0: 0.0, 2: 0.0}, {0: 0.0, 2: 0.0}
    for row_step in range(3):
        for col_step in range(3):
            windows = []
            if row_step != 1:
                windows.append(lines[row_step][col_step])
            if col_step != 1:
                windows.append(sides[col_step][row_step])
            if not windows:
                continue
            term = product(
                jnp.concatenate(windows, axis=0).astype(BF16), weight_of(row_step, col_step)
            )
            if row_step != 1:
                line_terms[row_step] += term[:columns]
            if col_step != 1:
                side_terms[col_step] += term[-rows:]
    top, bottom, west, east = line_terms[0], line_terms[2], side_terms[0], side_terms[2]
    return top, bottom, west, east


def with_ends(term, first, last):
    place = iota(term.shape, 0)
    ends = jnp.where(place == 0, first, jnp.where(place == term.shape[0] - 1, last, 0.0))
    return term + ends


def taps(weight_ref, mirror):
    if mirror:
        return dot_nt, lambda row_step, col_step: weight_ref[2 - row_step, 2 - col_step]
    return dot_nn, lambda row_step, col_step: weight_ref[row_step, col_step]


def convolve_rows(shifted, weight_ref, start, count, columns, mirror):
    product, weight_of = taps(weight_ref, mirror)
    total = None
    for row_step in range(3):
        for col_step in range(3):
            first = start + row_step * columns
            term = product(shifted[col_step, first : first + count, :], weight_of(row_step, col_step))
            total = term if total is None else total + term
    return total


def span_copy(source, target, semaphore, first, last):
    which = pl.ds(first * CHUNK, (last - first) * CHUNK)
    return pltpu.make_async_copy(source.at[which, :], target.at[which, :], semaphore)


BORDERS = 4


def forecast_kernel(
    columns,
    state_hbm,
    slope_hbm,
    weight_hbm,
    out_hbm,
    borders_hbm,
    state_ref,
    slope_ref,
    weight_ref,
    out_ref,
    borders_ref,
    shifted,
    weight_semaphore,
    state_semaphores,
    slope_semaphores,
    out_semaphores,
):
    cells, channels = state_ref.shape
    rows = cells // columns
    per = CHUNK // columns
    steps = cells // CHUNK
    zero = jnp.zeros((1, channels), F32)
    groups = list(zip(FORECAST_GROUPS[:-1], FORECAST_GROUPS[1:]))

    def copies_in(number):
        first, last = groups[number]
        ahead = (first + 1 if number else 0), min(last + 1, steps)
        found = [
            span_copy(slope_hbm, slope_ref, slope_semaphores.at[number], first, last)
        ]
        if ahead[0] < ahead[1]:
            found.append(span_copy(state_hbm, state_ref, state_semaphores.at[number], *ahead))
        if number == 0:
            found.append(pltpu.make_async_copy(weight_hbm, weight_ref, weight_semaphore.at[0]))
        return found[::-1]

    def fill(index):
        for row in range(index * per, (index + 1) * per):
            center = state_ref[row * columns : (row + 1) * columns, :].astype(F32)
            fill_row(shifted, row + 1, center, zero, zero)

    coming = copies_in(0)
    for copy in coming:
        copy.start()
    no_halo_rows(shifted, rows, columns)
    out = []
    for number, (low, high) in enumerate(groups):
        for copy in coming:
            copy.wait()
        if number + 1 < len(groups):
            coming = copies_in(number + 1)
            for copy in coming:
                copy.start()
        if number == 0:
            fill(0)
        for index in range(low, high):
            if index + 1 < steps:
                fill(index + 1)
            part = slice(index * CHUNK, (index + 1) * CHUNK)
            response = convolve_rows(shifted, weight_ref, part.start, CHUNK, columns, False)
            slope = slope_ref[part, :].astype(F32)
            total = state_ref[part, :].astype(F32) + slope * response
            out_ref[part, :] = total.astype(BF16)
            for inner in range(per):
                row = index * per + inner
                first, last = inner * columns, (inner + 1) * columns - 1
                for kind, line in enumerate(
                    (slope[first : first + 1], slope[last : last + 1])
                    + (total[first : first + 1], total[last : last + 1])
                ):
                    at = kind * rows + row
                    borders_ref[at : at + 1, :] = line
            if index == 0:
                borders_ref[BORDERS * rows : BORDERS * rows + columns, :] = total[:columns]
            if index == steps - 1:
                borders_ref[BORDERS * rows + columns :, :] = total[CHUNK - columns :]
        out.append(span_copy(out_ref, out_hbm, out_semaphores.at[number], low, high))
        out[-1].start()
    out.append(pltpu.make_async_copy(borders_ref, borders_hbm, out_semaphores.at[steps]))
    out[-1].start()
    for copy in out:
        copy.wait()


def gradient_kernel(
    columns,
    adjoint,
    fields_ref,
    slope_ref,
    weight_ref,
    out_hbm,
    out_ref,
    shifted,
    out_semaphores,
):
    cells, channels = slope_ref.shape
    rows = cells // columns
    per = CHUNK // columns
    steps = cells // CHUNK
    zero = jnp.zeros((1, channels), F32)
    groups = list(zip(GRADIENT_GROUPS[:-1], GRADIENT_GROUPS[1:]))

    no_halo_rows(shifted, rows, columns)
    around = turned_weights(fields_ref[...], columns)

    def spread(index):
        weights = [blend(*around, index * per + row) for row in range(per)]
        out_ref[index * CHUNK : (index + 1) * CHUNK, :] = dot_nn(
            jnp.concatenate(weights, axis=0), adjoint[...]
        )

    def fill(index):
        part = slice(index * CHUNK, (index + 1) * CHUNK)
        pulled = slope_ref[part, :].astype(F32) * out_ref[part, :]
        for inner in range(per):
            center = pulled[inner * columns : (inner + 1) * columns, :]
            fill_row(shifted, index * per + inner + 1, center, zero, zero)

    for index in range(steps):
        spread(index)
    out = []
    for number, (low, high) in enumerate(groups):
        if number == 0:
            fill(0)
        for index in range(low, high):
            if index + 1 < steps:
                fill(index + 1)
            part = slice(index * CHUNK, (index + 1) * CHUNK)
            out_ref[part, :] += convolve_rows(shifted, weight_ref, part.start, CHUNK, columns, True)
        out.append(span_copy(out_ref, out_hbm, out_semaphores.at[number], low, high))
        out[-1].start()
    for copy in out:
        copy.wait()


def finish_kernel(
    capacity,
    gradient_hbm,
    slot_hbm,
    box_ref,
    weight_hbm,
    left_hbm,
    right_hbm,
    north_hbm,
    south_hbm,
    out_hbm,
    departures_hbm,
    slot_ref,
    weight_ref,
    left_ref,
    right_ref,
    north_ref,
    south_ref,
    lines_ref,
    sides_ref,
    departures_ref,
    semaphores,
    out_semaphores,
):
    del gradient_hbm
    lat, lon = lax.axis_index("lat"), lax.axis_index("lon")
    rows, columns, cell_channels = out_hbm.shape
    inner = pl.ds(8, columns - 16)
    places = (
        (lines_ref.at[0], out_hbm.at[0, inner, :]),
        (lines_ref.at[1], out_hbm.at[rows - 1, inner, :]),
        (sides_ref.at[0], out_hbm.at[:, pl.ds(0, 8), :]),
        (sides_ref.at[1], out_hbm.at[:, pl.ds(columns - 8, 8), :]),
    )
    waiting = copies(
        semaphores,
        (slot_hbm, slot_ref),
        (weight_hbm, weight_ref),
        (left_hbm, left_ref),
        (right_hbm, right_ref),
        (north_hbm, north_ref),
        (south_hbm, south_ref),
        *((there, here) for here, there in places),
    )
    slots = box_ref.shape[0]
    count = slot_ref.shape[1]
    channels = box_ref.shape[1] - META
    waiting[0].wait()
    turned = jnp.broadcast_to(slot_ref[...].astype(F32), (128, count)).T
    lane = iota((count, 128), 1).astype(F32)
    parts = [
        (lane + float(first) == turned).astype(F32).astype(BF16) for first in range(0, slots, 128)
    ]
    place = jnp.concatenate(parts, axis=1)
    step = count // 2
    leaving = []
    for index in range(2):
        part = slice(index * step, (index + 1) * step)
        departures_ref[part, :] = dot_nn(place[part, :], box_ref[:, :channels])
        leaving.append(
            pltpu.make_async_copy(
                departures_ref.at[part, :], departures_hbm.at[part, :], out_semaphores.at[4 + index]
            )
        )
        leaving[-1].start()
    for copy in waiting[1:]:
        copy.wait()
    top, bottom, west, east = halo_terms(
        left_ref[...].astype(F32),
        right_ref[...].astype(F32),
        north_ref[...].astype(F32),
        south_ref[...].astype(F32),
        corners_in(box_ref, lat, lon, capacity, channels, cell_channels),
        weight_ref,
        True,
    )
    lines_ref[0] += top[8 : columns - 8]
    lines_ref[1] += bottom[8 : columns - 8]
    leaving += copies(out_semaphores, *places[:2])
    place = iota((8, cell_channels), 0)
    for number, side, at in ((0, west, 0), (1, east, 7)):
        ends = (top[:8], bottom[:8]) if number == 0 else (top[-8:], bottom[-8:])
        for row in range(rows):
            term = jnp.where(place == at, side[row : row + 1], 0.0)
            if row == 0:
                term = term + ends[0]
            if row == rows - 1:
                term = term + ends[1]
            sides_ref[number, row] += term
        leaving.append(pltpu.make_async_copy(*places[2 + number], out_semaphores.at[2 + number]))
        leaving[-1].start()
    for copy in leaving:
        copy.wait()


def sigmoid(value):
    return 0.5 + 0.5 * jnp.tanh(0.5 * value)


def blend(row_low, row_high, upper, lower, at):
    at = jnp.asarray(at, BF16)
    zero = jnp.zeros(upper.shape, BF16)
    return jnp.where(row_low == at, upper, jnp.where(row_high == at, lower, zero))


def turned_weights(fields, columns):
    slots = fields.shape[1]
    row, column, w00, w01, w10, w11 = (fields[index : index + 1, :] for index in range(FIELDS))
    place = iota((columns, slots), 0).astype(F32)
    here, beside = place == column, place == column + 1.0
    upper = (jnp.where(here, w00, 0.0) + jnp.where(beside, w01, 0.0)).astype(BF16)
    lower = (jnp.where(here, w10, 0.0) + jnp.where(beside, w11, 0.0)).astype(BF16)
    row_low = jnp.broadcast_to(row, (columns, slots)).astype(BF16)
    row_high = jnp.broadcast_to(row + 1.0, (columns, slots)).astype(BF16)
    return row_low, row_high, upper, lower


def observe_kernel(
    columns,
    capacity,
    box_hbm,
    grid_hbm,
    weight_in_hbm,
    weight_mid_hbm,
    weight_out_hbm,
    bias_in_hbm,
    bias_mid_hbm,
    bias_out_hbm,
    inv_error_hbm,
    slope_hbm,
    borders_hbm,
    conv_hbm,
    left_hbm,
    right_hbm,
    north_hbm,
    south_hbm,
    departures_hbm,
    adjoint_hbm,
    fields_hbm,
    west_ref,
    east_ref,
    top_ref,
    bottom_ref,
    box_ref,
    grid_ref,
    weight_in_ref,
    weight_mid_ref,
    weight_out_ref,
    bias_in_ref,
    bias_mid_ref,
    bias_out_ref,
    inv_error_ref,
    ends_ref,
    borders_ref,
    conv_ref,
    left_ref,
    right_ref,
    north_ref,
    south_ref,
    sampled,
    departures_ref,
    adjoint,
    fields_ref,
    semaphores,
    out_semaphores,
):
    lat, lon = lax.axis_index("lat"), lax.axis_index("lon")
    slots, width = box_ref.shape
    cells, grid_channels = grid_ref.shape
    channels = width - META
    hidden = weight_in_ref.shape[1]
    rows = cells // columns
    lanes, spare = pl.ds(0, channels), pl.ds(channels, META)
    waiting = copies(
        semaphores,
        (box_hbm.at[:, spare], box_ref.at[:, spare]),
        (left_hbm, left_ref),
        (right_hbm, right_ref),
        (north_hbm, north_ref),
        (south_hbm, south_ref),
        (conv_hbm, conv_ref),
        (grid_hbm, grid_ref),
        (slope_hbm.at[pl.ds(0, columns), :], ends_ref.at[0]),
        (slope_hbm.at[pl.ds(cells - columns, columns), :], ends_ref.at[1]),
        (borders_hbm, borders_ref),
        (weight_in_hbm, weight_in_ref),
        (bias_in_hbm, bias_in_ref),
        (bias_mid_hbm, bias_mid_ref),
        (bias_out_hbm, bias_out_ref),
        (inv_error_hbm, inv_error_ref),
        (weight_mid_hbm, weight_mid_ref),
        (weight_out_hbm, weight_out_ref),
        (box_hbm.at[:, lanes], box_ref.at[:, lanes]),
    )
    waiting[0].wait()
    pick = (iota((16, META), 0) == iota((16, META), 1)).astype(F32).astype(BF16)
    fields_ref[...] = dot_nt(pick, box_ref[:, channels:])
    fields_out = pltpu.make_async_copy(fields_ref, fields_hbm, out_semaphores.at[0])
    fields_out.start()
    pick = iota((META, FIELDS * columns), 0) == iota((META, FIELDS * columns), 1) // columns
    wide = dot_nn(box_ref[:, channels:], pick.astype(F32).astype(BF16))
    row, column, w00, w01, w10, w11 = (
        wide[:, index * columns : (index + 1) * columns] for index in range(FIELDS)
    )
    lane = iota((slots, columns), 1).astype(F32)
    here, beside = lane == column, lane == column + 1.0
    upper = (jnp.where(here, w00, 0.0) + jnp.where(beside, w01, 0.0)).astype(BF16)
    lower = (jnp.where(here, w10, 0.0) + jnp.where(beside, w11, 0.0)).astype(BF16)
    row_low = row.astype(BF16)
    row_high = (row + 1.0).astype(BF16)
    for copy in waiting[1:6]:
        copy.wait()
    top, bottom, west, east = halo_terms(
        left_ref[...].astype(F32),
        right_ref[...].astype(F32),
        north_ref[...].astype(F32),
        south_ref[...].astype(F32),
        corners_in(box_ref, lat, lon, capacity, channels, grid_channels),
        conv_ref,
        False,
    )
    for copy in waiting[6:10]:
        copy.wait()
    place = iota((16, grid_channels), 0)
    for number, side, others, at, first in (
        (0, west, (top[:1], bottom[:1]), 0, 0),
        (1, east, (top[-1:], bottom[-1:]), 15, columns - 16),
    ):
        slope = borders_ref[number * rows : (number + 1) * rows, :]
        value = borders_ref[(number + 2) * rows : (number + 3) * rows, :]
        value = value + slope * with_ends(side, *others)
        for row in range(rows):
            part = slice(row * columns + first, row * columns + first + 16)
            grid_ref[part, :] = jnp.where(
                place == at, value[row : row + 1], grid_ref[part, :].astype(F32)
            ).astype(BF16)
    for number, line, at in ((0, top, 0), (1, bottom, rows - 1)):
        first = BORDERS * rows + number * columns
        line = with_ends(line, west[at : at + 1], east[at : at + 1])
        grid_ref[at * columns : (at + 1) * columns, :] = (
            borders_ref[first : first + columns, :] + ends_ref[number].astype(F32) * line
        ).astype(BF16)
    strip = 256
    for start in range(0, slots, strip):
        part = slice(start, start + strip)
        parts = [blend(row_low[part], row_high[part], upper[part], lower[part], at) for at in range(rows)]
        sampled[part, :] = dot_nn(jnp.concatenate(parts, axis=1), grid_ref[...])
    for copy in waiting[10:]:
        copy.wait()
    bias_in, bias_mid, bias_out, inv_error = (
        ref[...].reshape(1, -1) for ref in (bias_in_ref, bias_mid_ref, bias_out_ref, inv_error_ref)
    )
    step = 512
    results = []
    for start in range(0, slots, step):
        part = slice(start, start + step)
        pre = dot_nn(sampled[part, :].astype(BF16), weight_in_ref[...]) + bias_in
        gate = sigmoid(pre)
        act = pre * gate
        slope_first = gate + act * (1.0 - gate)
        pre = dot_nn(act.astype(BF16), weight_mid_ref[...]) + bias_mid
        gate = sigmoid(pre)
        act = pre * gate
        slope_second = gate + act * (1.0 - gate)
        evolved = dot_nn(act.astype(BF16), weight_out_ref[...]) + bias_out
        departures = (evolved - box_ref[part, :channels].astype(F32)) * inv_error
        departures_ref[part, :channels] = departures.astype(BF16)
        back = (departures * inv_error).astype(BF16)
        back = (dot_nt(back, weight_out_ref[...]) * slope_second).astype(BF16)
        back = (dot_nt(back, weight_mid_ref[...]) * slope_first).astype(BF16)
        adjoint[part, :] = dot_nt(back, weight_in_ref[...]).astype(BF16)
        which = pl.ds(start, step)
        results += copies(
            out_semaphores.at[pl.ds(1 + len(results), 2)],
            (departures_ref.at[which, lanes], departures_hbm.at[which, lanes]),
            (adjoint.at[which, :], adjoint_hbm.at[which, :]),
        )
    fields = fields_ref[...]
    around = turned_weights(fields, columns)
    row, column, w00, w01, w10, w11 = (fields[index : index + 1, :] for index in range(FIELDS))
    place = iota((rows, slots), 0).astype(F32)
    here, below = place == row, place == row + 1.0
    zero = jnp.zeros((rows, slots), F32)
    weights = [blend(*around, 0), blend(*around, rows - 1)]
    for at, high, low in ((0.0, w00, w10), (columns - 2.0, w01, w11)):
        chosen = column == at
        weights.append(
            jnp.where(here & chosen, high, jnp.where(below & chosen, low, zero)).astype(BF16)
        )
    spread = dot_nn(jnp.concatenate(weights, axis=0), adjoint[...])
    cells_out = []
    for index, edge_ref in enumerate((top_ref, bottom_ref)):
        first = index * columns
        pulled = ends_ref[index].astype(F32) * spread[first : first + columns]
        edge_ref[...] = pulled.astype(BF16)
        cells_out += [pulled[:1], pulled[columns - 1 :]]
    for index, edge_ref in enumerate((west_ref, east_ref)):
        first = 2 * columns + index * rows
        slope = borders_ref[index * rows : (index + 1) * rows, :]
        edge_ref[...] = (slope * spread[first : first + rows]).astype(BF16)
    departures_ref[:, channels:] = jnp.zeros((slots, META), BF16)
    corners_out(cells_out, lat, lon, capacity, departures_ref, channels)
    results += copies(
        out_semaphores.at[pl.ds(1 + len(results), 1)],
        (departures_ref.at[:, spare], departures_hbm.at[:, spare]),
    )
    fields_out.wait()
    for copy in results:
        copy.wait()


def beside(west, east):
    count = lax.axis_size("lon")
    onward = [(i, (i + 1) % count) for i in range(count)]
    left = lax.ppermute(east, "lon", onward)
    right = lax.ppermute(west, "lon", [(target, source) for source, target in onward])
    return left, right


def over(top, bottom):
    count = lax.axis_size("lat")
    down = [(i, (i + 1) % count) for i in range(count)]
    north = lax.ppermute(bottom, "lat", down)
    south = lax.ppermute(top, "lat", [(target, source) for source, target in down])
    return north, south


def body(
    model_state,
    tangent_slope,
    conv_weight,
    weight_in,
    bias_in,
    weight_mid,
    bias_mid,
    weight_out,
    bias_out,
    obs_tile,
    obs_cell,
    obs_frac,
    radiance,
    inv_error,
):
    rows, columns, channels = model_state.shape
    cells = rows * columns
    devices = lax.axis_size("lat") * lax.axis_size("lon")
    count, bands = radiance.shape
    capacity = 2 * count // devices
    slots = devices * capacity
    hidden = weight_in.shape[1]
    sds = jax.ShapeDtypeStruct
    dma = pltpu.SemaphoreType.DMA

    def exchange(box):
        return lax.all_to_all(
            box.reshape(devices, capacity, -1), ("lat", "lon"), split_axis=0, concat_axis=0, tiled=True
        ).reshape(slots, -1)

    box, slot, west, east, top, bottom = kernel_call(
        functools.partial(dispatch_kernel, capacity),
        (
            sds((slots, bands + META), BF16),
            sds((1, count), jnp.int32),
            sds((rows, channels), BF16),
            sds((rows, channels), BF16),
            sds((columns, channels), BF16),
            sds((columns, channels), BF16),
        ),
        (HBM,) * 6,
        (HBM,) * 5,
        (
            pltpu.VMEM((1, count), jnp.int32),
            pltpu.VMEM((1, count), jnp.int32),
            pltpu.VMEM((2, count), F32),
            pltpu.VMEM((count, bands), BF16),
            pltpu.VMEM((rows, 16, channels), BF16),
            pltpu.VMEM((rows, 16, channels), BF16),
            pltpu.VMEM((slots, bands + META), BF16),
            pltpu.VMEM((1, count), jnp.int32),
            pltpu.VMEM((rows, channels), BF16),
            pltpu.VMEM((rows, channels), BF16),
            pltpu.VMEM((2, columns, channels), BF16),
            dma((8,)),
            dma((7,)),
        ),
        flops=2 * slots * count * (bands + META),
        moved=2 * slots * (bands + META),
        name="dispatch",
    )(obs_tile.reshape(1, count), obs_cell.reshape(1, count), obs_frac.T, radiance, model_state)
    arrived = exchange(box)

    conv_flops = 2 * 9 * cells * channels * channels
    steps = cells // CHUNK
    halo_scratch = (
        pltpu.VMEM((rows, channels), BF16),
        pltpu.VMEM((rows, channels), BF16),
        pltpu.VMEM((columns, channels), BF16),
        pltpu.VMEM((columns, channels), BF16),
    )
    shifted = pltpu.VMEM((3, (rows + 2) * columns, channels), BF16)
    borders_shape = (BORDERS * rows + 2 * columns, channels)
    flat_slope = tangent_slope.reshape(cells, channels)
    halo = beside(west, east) + over(top, bottom)
    forecast, borders = kernel_call(
        functools.partial(forecast_kernel, columns),
        (sds((cells, channels), BF16), sds(borders_shape, F32)),
        (HBM,) * 2,
        (HBM,) * 3,
        (
            pltpu.VMEM((cells, channels), BF16),
            pltpu.VMEM((cells, channels), BF16),
            pltpu.VMEM(conv_weight.shape, BF16),
            pltpu.VMEM((cells, channels), BF16),
            pltpu.VMEM(borders_shape, F32),
            shifted,
            dma((1,)),
            dma((steps,)),
            dma((steps,)),
            dma((steps + 1,)),
        ),
        flops=conv_flops,
        moved=6 * cells * channels,
        room=512,
        name="forecast",
    )(model_state.reshape(cells, channels), flat_slope, conv_weight)

    network_flops = 2 * slots * (channels * hidden + hidden * hidden + hidden * bands)
    departures_box, adjoint, fields, west, east, top, bottom = kernel_call(
        functools.partial(observe_kernel, columns, capacity),
        (
            sds((slots, bands + META), BF16),
            sds((slots, channels), BF16),
            sds((16, slots), F32),
            sds((rows, channels), BF16),
            sds((rows, channels), BF16),
            sds((columns, channels), BF16),
            sds((columns, channels), BF16),
        ),
        (HBM,) * 3 + (VMEM,) * 4,
        (HBM,) * 16,
        (
            pltpu.VMEM((slots, bands + META), BF16),
            pltpu.VMEM((cells, channels), BF16),
            pltpu.VMEM(weight_in.shape, BF16),
            pltpu.VMEM(weight_mid.shape, BF16),
            pltpu.VMEM(weight_out.shape, BF16),
            *(pltpu.VMEM(vector.shape, F32) for vector in (bias_in, bias_mid, bias_out, inv_error)),
            pltpu.VMEM((2, columns, channels), BF16),
            pltpu.VMEM(borders_shape, F32),
            pltpu.VMEM(conv_weight.shape, BF16),
            *halo_scratch,
            pltpu.VMEM((slots, channels), F32),
            pltpu.VMEM((slots, bands + META), BF16),
            pltpu.VMEM((slots, channels), BF16),
            pltpu.VMEM((16, slots), F32),
            dma((18,)),
            dma((6,)),
        ),
        flops=2 * network_flops + 2 * slots * cells * channels,
        moved=2 * cells * channels,
        room=ROOM,
        name="observe",
    )(
        arrived,
        forecast,
        weight_in,
        weight_mid,
        weight_out,
        bias_in,
        bias_mid,
        bias_out,
        inv_error,
        flat_slope,
        borders,
        conv_weight,
        *halo,
    )

    returned = exchange(departures_box)
    halo = beside(west, east) + over(top, bottom)
    gradient, = kernel_call(
        functools.partial(gradient_kernel, columns),
        (sds((cells, channels), F32),),
        (HBM,),
        (VMEM,) * 4,
        (
            pltpu.VMEM((cells, channels), F32),
            shifted,
            dma((steps,)),
        ),
        flops=conv_flops + 2 * slots * cells * channels,
        moved=4 * cells * channels,
        room=30720,
        name="gradient",
    )(adjoint, fields, flat_slope, conv_weight)
    gradient, departures = kernel_call(
        functools.partial(finish_kernel, capacity),
        (sds((rows, columns, channels), F32), sds((count, bands), F32)),
        (HBM, HBM),
        (HBM, HBM, VMEM) + (HBM,) * 5,
        (
            pltpu.VMEM((1, count), jnp.int32),
            pltpu.VMEM(conv_weight.shape, BF16),
            *halo_scratch,
            pltpu.VMEM((2, columns - 16, channels), F32),
            pltpu.VMEM((2, rows, 8, channels), F32),
            pltpu.VMEM((count, bands), F32),
            dma((11,)),
            dma((6,)),
        ),
        flops=2 * slots * count * bands,
        moved=4 * count * bands,
        aliases={0: 0},
        room=30720,
        name="finish",
    )(gradient.reshape(rows, columns, channels), slot, returned, conv_weight, *halo)
    return departures, gradient


def solution(mesh):
    in_specs = (
        P("lat", "lon", None),
        P("lat", "lon", None),
        P(),
        P(),
        P(),
        P(),
        P(),
        P(),
        P(),
        P(("lat", "lon"), None),
        P(("lat", "lon")),
        P(("lat", "lon"), None),
        P(("lat", "lon"), None),
        P(),
    )
    out_specs = (P(("lat", "lon"), None), P("lat", "lon", None))
    return jax.shard_map(body, mesh=mesh, in_specs=in_specs, out_specs=out_specs, check_vma=False)
```

```python
import functools

import jax
import jax.numpy as jnp
from jax import lax
from jax.experimental import pallas as pl
from jax.experimental.pallas import tpu as pltpu
from jax.sharding import PartitionSpec as P

F32 = jnp.float32
BF16 = jnp.bfloat16
META = 128
FIELDS = 6
VMEM_KIB = 60 * 1024 + 512
ROOM = 1024 + 256


def dot_nt(left, right):
    return lax.dot_general(left, right, (((1,), (1,)), ((), ())), preferred_element_type=F32)


def dot_nn(left, right):
    return jnp.dot(left, right, preferred_element_type=F32)


def iota(shape, dim):
    return lax.broadcasted_iota(jnp.int32, shape, dim)


def kernel_call(body, outs, out_spaces, in_spaces, scratch=(), flops=0, moved=0, room=0, aliases=None, name=None):
    return pl.pallas_call(
        body,
        out_shape=outs,
        in_specs=[pl.BlockSpec(memory_space=space) for space in in_spaces],
        out_specs=[pl.BlockSpec(memory_space=space) for space in out_spaces],
        scratch_shapes=list(scratch),
        input_output_aliases=aliases or {},
        name=name,
        compiler_params=pltpu.CompilerParams(vmem_limit_bytes=(VMEM_KIB - room) * 1024),
        cost_estimate=pl.CostEstimate(flops=flops, bytes_accessed=moved, transcendentals=0),
    )


HBM = pltpu.HBM
VMEM = pltpu.VMEM


def copies(semaphores, *pairs):
    started = []
    for index, (source, target) in enumerate(pairs):
        copy = pltpu.make_async_copy(source, target, semaphores.at[index])
        copy.start()
        started.append(copy)
    return started


CORNER_LANE = 32
CORNER_WIDTH = 32


def diagonal_blocks(lat, lon, capacity):
    lats, lons = lax.axis_size("lat"), lax.axis_size("lon")
    blocks = []
    for down, right in ((-1, -1), (-1, 1), (1, -1), (1, 1)):
        row, column = lat + down, lax.rem(lon + right + lons, lons)
        inside = (row >= 0) & (row < lats)
        first = jnp.where(inside, row * lons + column, 0) * capacity
        aligned = pl.multiple_of((first // 16) * 16, 16)
        blocks.append((inside, aligned, lax.rem(first, 16)))
    return blocks


def corner_fold(shape, lane_dim):
    value, lane = iota(shape, 1 - lane_dim), iota(shape, lane_dim)
    chosen = (value % CORNER_WIDTH == lane - CORNER_LANE) & (lane >= CORNER_LANE)
    return (chosen & (lane < CORNER_LANE + CORNER_WIDTH)).astype(F32).astype(BF16)


def corner_mask(shape):
    return iota(shape, 1) // CORNER_WIDTH == iota(shape, 0) % 8


def corners_out(cells, lat, lon, capacity, box_ref, channels):
    width = cells[0].shape[1]
    spread = jnp.concatenate([jnp.broadcast_to(cell, (8, width)) for cell in cells], axis=0)
    kept = jnp.where(corner_mask(spread.shape), spread, 0.0).astype(BF16)
    folded = dot_nn(kept, corner_fold((width, META), 1))
    half = (iota((16, META), 0) // 8) * 8
    for index, (inside, first, own) in enumerate(diagonal_blocks(lat, lon, capacity)):
        lines = folded[8 * index : 8 * index + 8]
        lines = jnp.where(half == own, jnp.concatenate([lines, lines], axis=0), 0.0)

        @pl.when(inside)
        def _():
            which = pl.ds(first, 16)
            box_ref[which, channels:] = (box_ref[which, channels:].astype(F32) + lines).astype(BF16)


def corners_in(box_ref, lat, lon, capacity, channels, width):
    lines = []
    for inside, first, own in diagonal_blocks(lat, lon, capacity):
        block = box_ref[pl.ds(first, 16), channels:].astype(F32)
        mine = jnp.where(own == 0, block[:8], block[8:])
        lines.append(jnp.where(inside, mine, 0.0))
    folded = jnp.concatenate(lines, axis=0).astype(BF16)
    spread = dot_nn(folded, corner_fold((META, width), 0))
    kept = jnp.where(corner_mask(spread.shape), spread, 0.0)
    return [jnp.sum(kept[8 * index : 8 * index + 8], axis=0, keepdims=True) for index in range(4)]


def dispatch_kernel(
    capacity,
    tile_hbm,
    cell_hbm,
    frac_hbm,
    radiance_hbm,
    state_hbm,
    box_hbm,
    slot_hbm,
    west_hbm,
    east_hbm,
    top_hbm,
    bottom_hbm,
    tile_ref,
    cell_ref,
    frac_ref,
    radiance_ref,
    first_ref,
    last_ref,
    box_ref,
    slot_ref,
    west_ref,
    east_ref,
    lines_ref,
    semaphores,
    out_semaphores,
):
    rows, columns, _ = state_hbm.shape
    lat, lon = lax.axis_index("lat"), lax.axis_index("lon")
    waiting = copies(
        semaphores,
        (tile_hbm, tile_ref),
        (cell_hbm, cell_ref),
        (frac_hbm, frac_ref),
        (radiance_hbm, radiance_ref),
        (state_hbm.at[:, pl.ds(0, 16), :], first_ref),
        (state_hbm.at[:, pl.ds(columns - 16, 16), :], last_ref),
        (state_hbm.at[0], lines_ref.at[0]),
        (state_hbm.at[rows - 1], lines_ref.at[1]),
    )
    slots, width = box_ref.shape
    devices = slots // capacity
    count = tile_ref.shape[1]
    channels = width - META
    earlier = (iota((count, count), 0) < iota((count, count), 1)).astype(F32).astype(BF16)
    for copy in waiting[:3]:
        copy.wait()
    tile = tile_ref[...]
    match = (iota((devices, count), 0) == tile).astype(F32)
    before = dot_nn(match.astype(BF16), earlier)
    position = jnp.sum(before * match, axis=0, keepdims=True)
    slot = tile * capacity + position.astype(jnp.int32)
    slot_ref[...] = slot
    leaving = [pltpu.make_async_copy(slot_ref, slot_hbm, out_semaphores.at[0])]
    leaving[0].start()
    cell = cell_ref[...]
    low, side = frac_ref[0:1, :], frac_ref[1:2, :]
    fields = (
        (cell >> 7).astype(F32),
        (cell & 127).astype(F32),
        (1.0 - low) * (1.0 - side),
        (1.0 - low) * side,
        low * (1.0 - side),
        low * side,
    )
    number = iota((META, count), 0)
    meta = jnp.zeros((META, count), F32)
    for index, field in enumerate(fields):
        meta = jnp.where(number == index, field, meta)
    meta = meta.astype(BF16)
    for copy in waiting[4:]:
        copy.wait()
    for index, line_hbm in enumerate((top_hbm, bottom_hbm)):
        leaving.append(
            pltpu.make_async_copy(lines_ref.at[index], line_hbm, out_semaphores.at[len(leaving)])
        )
        leaving[-1].start()
    cells = []
    for block_ref, at, side_ref, side_hbm in (
        (first_ref, 0, west_ref, west_hbm),
        (last_ref, 15, east_ref, east_hbm),
    ):
        lines = [block_ref[row].astype(F32)[at : at + 1] for row in range(rows)]
        cells += [lines[0], lines[-1]]
        side_ref[...] = jnp.concatenate(lines, axis=0).astype(BF16)
        leaving.append(
            pltpu.make_async_copy(side_ref, side_hbm, out_semaphores.at[len(leaving)])
        )
        leaving[-1].start()
    cells = (cells[0], cells[2], cells[1], cells[3])
    places = []
    step = slots // 2
    for index in range(2):
        part = slice(index * step, (index + 1) * step)
        places.append((iota((step, count), 0) + index * step == slot).astype(F32).astype(BF16))
        box_ref[part, channels:] = dot_nt(places[index], meta).astype(BF16)
    corners_out(cells, lat, lon, capacity, box_ref, channels)
    waiting[3].wait()
    for index in range(2):
        part = slice(index * step, (index + 1) * step)
        box_ref[part, :channels] = dot_nn(places[index], radiance_ref[...]).astype(BF16)
        leaving.append(
            pltpu.make_async_copy(
                box_ref.at[part, :], box_hbm.at[part, :], out_semaphores.at[len(leaving)]
            )
        )
        leaving[-1].start()
    for copy in leaving:
        copy.wait()


CHUNK = 512
FORECAST_GROUPS = (0, 2, 6, 8)
GRADIENT_GROUPS = (0, 4, 8)
SPREAD_AHEAD = 6


def fill_row(shifted, row, center, left, right):
    columns = center.shape[0]
    place = iota(center.shape, 0)
    where = pl.ds(row * columns, columns)
    shifted[1, where, :] = center.astype(BF16)
    shifted[0, where, :] = jnp.where(place == 0, left, pltpu.roll(center, 1, 0)).astype(BF16)
    shifted[2, where, :] = jnp.where(
        place == columns - 1, right, pltpu.roll(center, columns - 1, 0)
    ).astype(BF16)


def no_halo_rows(shifted, rows, columns):
    zero = jnp.zeros((3, columns, shifted.shape[2]), BF16)
    shifted[:, :columns, :] = zero
    shifted[:, (rows + 1) * columns :, :] = zero


def halo_terms(left, right, north, south, corners, weight_ref, mirror):
    rows, columns = left.shape[0], north.shape[0]
    lat = lax.axis_index("lat")
    north = jnp.where(lat > 0, north, 0.0)
    south = jnp.where(lat < lax.axis_size("lat") - 1, south, 0.0)
    product, weight_of = taps(weight_ref, mirror)

    def row_windows(center, first, last):
        place = iota(center.shape, 0)
        west = jnp.where(place == 0, first, pltpu.roll(center, 1, 0))
        east = jnp.where(place == columns - 1, last, pltpu.roll(center, columns - 1, 0))
        return west, center, east

    def column_windows(side):
        place = iota(side.shape, 0)
        up = jnp.where(place == 0, 0.0, pltpu.roll(side, 1, 0))
        down = jnp.where(place == rows - 1, 0.0, pltpu.roll(side, rows - 1, 0))
        return up, side, down

    lines = {0: row_windows(north, *corners[:2]), 2: row_windows(south, *corners[2:])}
    sides = {0: column_windows(left), 2: column_windows(right)}
    line_terms, side_terms = {0: 0.0, 2: 0.0}, {0: 0.0, 2: 0.0}
    for row_step in range(3):
        for col_step in range(3):
            windows = []
            if row_step != 1:
                windows.append(lines[row_step][col_step])
            if col_step != 1:
                windows.append(sides[col_step][row_step])
            if not windows:
                continue
            term = product(
                jnp.concatenate(windows, axis=0).astype(BF16), weight_of(row_step, col_step)
            )
            if row_step != 1:
                line_terms[row_step] += term[:columns]
            if col_step != 1:
                side_terms[col_step] += term[-rows:]
    top, bottom, west, east = line_terms[0], line_terms[2], side_terms[0], side_terms[2]
    return top, bottom, west, east


def with_ends(term, first, last):
    place = iota(term.shape, 0)
    ends = jnp.where(place == 0, first, jnp.where(place == term.shape[0] - 1, last, 0.0))
    return term + ends


def taps(weight_ref, mirror):
    if mirror:
        return dot_nt, lambda row_step, col_step: weight_ref[2 - row_step, 2 - col_step]
    return dot_nn, lambda row_step, col_step: weight_ref[row_step, col_step]


def convolve_rows(shifted, weight_ref, start, count, columns, mirror):
    product, weight_of = taps(weight_ref, mirror)
    total = None
    for row_step in range(3):
        for col_step in range(3):
            first = start + row_step * columns
            term = product(shifted[col_step, first : first + count, :], weight_of(row_step, col_step))
            total = term if total is None else total + term
    return total


def span_copy(source, target, semaphore, first, last):
    which = pl.ds(first * CHUNK, (last - first) * CHUNK)
    return pltpu.make_async_copy(source.at[which, :], target.at[which, :], semaphore)


BORDERS = 4


def forecast_kernel(
    columns,
    state_hbm,
    slope_hbm,
    weight_hbm,
    out_hbm,
    borders_hbm,
    state_ref,
    slope_ref,
    weight_ref,
    out_ref,
    borders_ref,
    shifted,
    weight_semaphore,
    state_semaphores,
    slope_semaphores,
    out_semaphores,
):
    cells, channels = state_ref.shape
    rows = cells // columns
    per = CHUNK // columns
    steps = cells // CHUNK
    zero = jnp.zeros((1, channels), F32)
    groups = list(zip(FORECAST_GROUPS[:-1], FORECAST_GROUPS[1:]))

    def copies_in(number):
        first, last = groups[number]
        ahead = (first + 1 if number else 0), min(last + 1, steps)
        found = [
            span_copy(slope_hbm, slope_ref, slope_semaphores.at[number], first, last)
        ]
        if ahead[0] < ahead[1]:
            found.append(span_copy(state_hbm, state_ref, state_semaphores.at[number], *ahead))
        if number == 0:
            found.append(pltpu.make_async_copy(weight_hbm, weight_ref, weight_semaphore.at[0]))
        return found[::-1]

    def fill(index):
        for row in range(index * per, (index + 1) * per):
            center = state_ref[row * columns : (row + 1) * columns, :].astype(F32)
            fill_row(shifted, row + 1, center, zero, zero)

    coming = copies_in(0)
    for copy in coming:
        copy.start()
    no_halo_rows(shifted, rows, columns)
    out = []
    for number, (low, high) in enumerate(groups):
        for copy in coming:
            copy.wait()
        if number + 1 < len(groups):
            coming = copies_in(number + 1)
            for copy in coming:
                copy.start()
        if number == 0:
            fill(0)
        for index in range(low, high):
            if index + 1 < steps:
                fill(index + 1)
            part = slice(index * CHUNK, (index + 1) * CHUNK)
            response = convolve_rows(shifted, weight_ref, part.start, CHUNK, columns, False)
            slope = slope_ref[part, :].astype(F32)
            total = state_ref[part, :].astype(F32) + slope * response
            out_ref[part, :] = total.astype(BF16)
            for inner in range(per):
                row = index * per + inner
                first, last = inner * columns, (inner + 1) * columns - 1
                for kind, line in enumerate(
                    (slope[first : first + 1], slope[last : last + 1])
                    + (total[first : first + 1], total[last : last + 1])
                ):
                    at = kind * rows + row
                    borders_ref[at : at + 1, :] = line
            if index == 0:
                borders_ref[BORDERS * rows : BORDERS * rows + columns, :] = total[:columns]
            if index == steps - 1:
                borders_ref[BORDERS * rows + columns :, :] = total[CHUNK - columns :]
        out.append(span_copy(out_ref, out_hbm, out_semaphores.at[number], low, high))
        out[-1].start()
    out.append(pltpu.make_async_copy(borders_ref, borders_hbm, out_semaphores.at[steps]))
    out[-1].start()
    for copy in out:
        copy.wait()


def gradient_kernel(
    columns,
    adjoint,
    fields_ref,
    slope_hbm,
    weight_ref,
    out_hbm,
    slope_ref,
    out_ref,
    shifted,
    slope_semaphore,
    out_semaphores,
):
    cells, channels = slope_ref.shape
    rows = cells // columns
    per = CHUNK // columns
    steps = cells // CHUNK
    zero = jnp.zeros((1, channels), F32)
    groups = list(zip(GRADIENT_GROUPS[:-1], GRADIENT_GROUPS[1:]))

    slope_in = copies(slope_semaphore, (slope_hbm, slope_ref))[0]
    no_halo_rows(shifted, rows, columns)
    around = turned_weights(fields_ref[...], columns)

    def spread(index):
        weights = [blend(*around, index * per + row) for row in range(per)]
        out_ref[index * CHUNK : (index + 1) * CHUNK, :] = dot_nn(
            jnp.concatenate(weights, axis=0), adjoint[...]
        )

    def fill(index):
        part = slice(index * CHUNK, (index + 1) * CHUNK)
        pulled = slope_ref[part, :].astype(F32) * out_ref[part, :]
        for inner in range(per):
            center = pulled[inner * columns : (inner + 1) * columns, :]
            fill_row(shifted, index * per + inner + 1, center, zero, zero)

    for index in range(SPREAD_AHEAD):
        spread(index)
    slope_in.wait()
    out = []
    for number, (low, high) in enumerate(groups):
        if number == 0:
            fill(0)
        for index in range(low, high):
            if index + 1 < steps:
                if index + 1 >= SPREAD_AHEAD:
                    spread(index + 1)
                fill(index + 1)
            part = slice(index * CHUNK, (index + 1) * CHUNK)
            out_ref[part, :] += convolve_rows(shifted, weight_ref, part.start, CHUNK, columns, True)
        out.append(span_copy(out_ref, out_hbm, out_semaphores.at[number], low, high))
        out[-1].start()
    for copy in out:
        copy.wait()


def finish_kernel(
    capacity,
    gradient_hbm,
    slot_hbm,
    box_ref,
    weight_hbm,
    left_hbm,
    right_hbm,
    north_hbm,
    south_hbm,
    out_hbm,
    departures_hbm,
    slot_ref,
    weight_ref,
    left_ref,
    right_ref,
    north_ref,
    south_ref,
    lines_ref,
    sides_ref,
    departures_ref,
    semaphores,
    out_semaphores,
):
    del gradient_hbm
    lat, lon = lax.axis_index("lat"), lax.axis_index("lon")
    rows, columns, cell_channels = out_hbm.shape
    inner = pl.ds(8, columns - 16)
    places = (
        (lines_ref.at[0], out_hbm.at[0, inner, :]),
        (lines_ref.at[1], out_hbm.at[rows - 1, inner, :]),
        (sides_ref.at[0], out_hbm.at[:, pl.ds(0, 8), :]),
        (sides_ref.at[1], out_hbm.at[:, pl.ds(columns - 8, 8), :]),
    )
    waiting = copies(
        semaphores,
        (slot_hbm, slot_ref),
        (weight_hbm, weight_ref),
        (left_hbm, left_ref),
        (right_hbm, right_ref),
        (north_hbm, north_ref),
        (south_hbm, south_ref),
        *((there, here) for here, there in places),
    )
    slots = box_ref.shape[0]
    count = slot_ref.shape[1]
    channels = box_ref.shape[1] - META
    waiting[0].wait()
    turned = jnp.broadcast_to(slot_ref[...].astype(F32), (128, count)).T
    lane = iota((count, 128), 1).astype(F32)
    parts = [
        (lane + float(first) == turned).astype(F32).astype(BF16) for first in range(0, slots, 128)
    ]
    place = jnp.concatenate(parts, axis=1)
    step = count // 2
    leaving = []
    for index in range(2):
        part = slice(index * step, (index + 1) * step)
        departures_ref[part, :] = dot_nn(place[part, :], box_ref[:, :channels])
        leaving.append(
            pltpu.make_async_copy(
                departures_ref.at[part, :], departures_hbm.at[part, :], out_semaphores.at[4 + index]
            )
        )
        leaving[-1].start()
    for copy in waiting[1:6]:
        copy.wait()
    top, bottom, west, east = halo_terms(
        left_ref[...].astype(F32),
        right_ref[...].astype(F32),
        north_ref[...].astype(F32),
        south_ref[...].astype(F32),
        corners_in(box_ref, lat, lon, capacity, channels, cell_channels),
        weight_ref,
        True,
    )
    for copy in waiting[6:]:
        copy.wait()
    lines_ref[0] += top[8 : columns - 8]
    lines_ref[1] += bottom[8 : columns - 8]
    leaving += copies(out_semaphores, *places[:2])
    place = iota((8, cell_channels), 0)
    for number, side, at in ((0, west, 0), (1, east, 7)):
        ends = (top[:8], bottom[:8]) if number == 0 else (top[-8:], bottom[-8:])
        for row in range(rows):
            term = jnp.where(place == at, side[row : row + 1], 0.0)
            if row == 0:
                term = term + ends[0]
            if row == rows - 1:
                term = term + ends[1]
            sides_ref[number, row] += term
        leaving.append(pltpu.make_async_copy(*places[2 + number], out_semaphores.at[2 + number]))
        leaving[-1].start()
    for copy in leaving:
        copy.wait()


def sigmoid(value):
    return 0.5 + 0.5 * jnp.tanh(0.5 * value)


def blend(row_low, row_high, upper, lower, at):
    at = jnp.asarray(at, BF16)
    zero = jnp.zeros(upper.shape, BF16)
    return jnp.where(row_low == at, upper, jnp.where(row_high == at, lower, zero))


def turned_weights(fields, columns):
    slots = fields.shape[1]
    row, column, w00, w01, w10, w11 = (fields[index : index + 1, :] for index in range(FIELDS))
    place = iota((columns, slots), 0).astype(F32)
    here, beside = place == column, place == column + 1.0
    upper = (jnp.where(here, w00, 0.0) + jnp.where(beside, w01, 0.0)).astype(BF16)
    lower = (jnp.where(here, w10, 0.0) + jnp.where(beside, w11, 0.0)).astype(BF16)
    row_low = jnp.broadcast_to(row, (columns, slots)).astype(BF16)
    row_high = jnp.broadcast_to(row + 1.0, (columns, slots)).astype(BF16)
    return row_low, row_high, upper, lower


def observe_kernel(
    columns,
    capacity,
    box_hbm,
    grid_hbm,
    weight_in_hbm,
    weight_mid_hbm,
    weight_out_hbm,
    bias_in_hbm,
    bias_mid_hbm,
    bias_out_hbm,
    inv_error_hbm,
    slope_hbm,
    borders_hbm,
    conv_hbm,
    left_hbm,
    right_hbm,
    north_hbm,
    south_hbm,
    departures_hbm,
    adjoint_hbm,
    fields_hbm,
    west_hbm,
    east_hbm,
    top_hbm,
    bottom_hbm,
    box_ref,
    grid_ref,
    weight_in_ref,
    weight_mid_ref,
    weight_out_ref,
    bias_in_ref,
    bias_mid_ref,
    bias_out_ref,
    inv_error_ref,
    ends_ref,
    borders_ref,
    conv_ref,
    left_ref,
    right_ref,
    north_ref,
    south_ref,
    sampled,
    departures_ref,
    adjoint,
    fields_ref,
    sides_ref,
    lines_ref,
    semaphores,
    out_semaphores,
):
    lat, lon = lax.axis_index("lat"), lax.axis_index("lon")
    slots, width = box_ref.shape
    cells, grid_channels = grid_ref.shape
    channels = width - META
    hidden = weight_in_ref.shape[1]
    rows = cells // columns
    lanes, spare = pl.ds(0, channels), pl.ds(channels, META)
    waiting = copies(
        semaphores,
        (box_hbm.at[:, spare], box_ref.at[:, spare]),
        (left_hbm, left_ref),
        (right_hbm, right_ref),
        (north_hbm, north_ref),
        (south_hbm, south_ref),
        (conv_hbm, conv_ref),
        (grid_hbm, grid_ref),
        (slope_hbm.at[pl.ds(0, columns), :], ends_ref.at[0]),
        (slope_hbm.at[pl.ds(cells - columns, columns), :], ends_ref.at[1]),
        (borders_hbm, borders_ref),
        (weight_in_hbm, weight_in_ref),
        (bias_in_hbm, bias_in_ref),
        (bias_mid_hbm, bias_mid_ref),
        (bias_out_hbm, bias_out_ref),
        (inv_error_hbm, inv_error_ref),
        (weight_mid_hbm, weight_mid_ref),
        (weight_out_hbm, weight_out_ref),
        (box_hbm.at[:, lanes], box_ref.at[:, lanes]),
    )
    waiting[0].wait()
    pick = (iota((16, META), 0) == iota((16, META), 1)).astype(F32).astype(BF16)
    fields_ref[...] = dot_nt(pick, box_ref[:, channels:])
    fields_out = pltpu.make_async_copy(fields_ref, fields_hbm, out_semaphores.at[0])
    fields_out.start()
    pick = iota((META, FIELDS * columns), 0) == iota((META, FIELDS * columns), 1) // columns
    wide = dot_nn(box_ref[:, channels:], pick.astype(F32).astype(BF16))
    row, column, w00, w01, w10, w11 = (
        wide[:, index * columns : (index + 1) * columns] for index in range(FIELDS)
    )
    lane = iota((slots, columns), 1).astype(F32)
    here, beside = lane == column, lane == column + 1.0
    upper = (jnp.where(here, w00, 0.0) + jnp.where(beside, w01, 0.0)).astype(BF16)
    lower = (jnp.where(here, w10, 0.0) + jnp.where(beside, w11, 0.0)).astype(BF16)
    row_low = row.astype(BF16)
    row_high = (row + 1.0).astype(BF16)
    for copy in waiting[1:6]:
        copy.wait()
    top, bottom, west, east = halo_terms(
        left_ref[...].astype(F32),
        right_ref[...].astype(F32),
        north_ref[...].astype(F32),
        south_ref[...].astype(F32),
        corners_in(box_ref, lat, lon, capacity, channels, grid_channels),
        conv_ref,
        False,
    )
    departures_ref[:, channels:] = jnp.zeros((slots, META), BF16)
    for copy in waiting[6:10]:
        copy.wait()
    place = iota((16, grid_channels), 0)
    for number, side, others, at, first in (
        (0, west, (top[:1], bottom[:1]), 0, 0),
        (1, east, (top[-1:], bottom[-1:]), 15, columns - 16),
    ):
        slope = borders_ref[number * rows : (number + 1) * rows, :]
        value = borders_ref[(number + 2) * rows : (number + 3) * rows, :]
        value = value + slope * with_ends(side, *others)
        for row in range(rows):
            part = slice(row * columns + first, row * columns + first + 16)
            grid_ref[part, :] = jnp.where(
                place == at, value[row : row + 1], grid_ref[part, :].astype(F32)
            ).astype(BF16)
    for number, line, at in ((0, top, 0), (1, bottom, rows - 1)):
        first = BORDERS * rows + number * columns
        line = with_ends(line, west[at : at + 1], east[at : at + 1])
        grid_ref[at * columns : (at + 1) * columns, :] = (
            borders_ref[first : first + columns, :] + ends_ref[number].astype(F32) * line
        ).astype(BF16)
    strip = 256
    for start in range(0, slots, strip):
        part = slice(start, start + strip)
        parts = [blend(row_low[part], row_high[part], upper[part], lower[part], at) for at in range(rows)]
        sampled[part, :] = dot_nn(jnp.concatenate(parts, axis=1), grid_ref[...])
    for copy in waiting[10:]:
        copy.wait()
    bias_in, bias_mid, bias_out, inv_error = (
        ref[...].reshape(1, -1) for ref in (bias_in_ref, bias_mid_ref, bias_out_ref, inv_error_ref)
    )
    step = 512
    results = []
    for start in range(0, slots, step):
        part = slice(start, start + step)
        pre = dot_nn(sampled[part, :].astype(BF16), weight_in_ref[...]) + bias_in
        gate = sigmoid(pre)
        act = pre * gate
        slope_first = gate + act * (1.0 - gate)
        pre = dot_nn(act.astype(BF16), weight_mid_ref[...]) + bias_mid
        gate = sigmoid(pre)
        act = pre * gate
        slope_second = gate + act * (1.0 - gate)
        evolved = dot_nn(act.astype(BF16), weight_out_ref[...]) + bias_out
        departures = (evolved - box_ref[part, :channels].astype(F32)) * inv_error
        departures_ref[part, :channels] = departures.astype(BF16)
        back = (departures * inv_error).astype(BF16)
        back = (dot_nt(back, weight_out_ref[...]) * slope_second).astype(BF16)
        back = (dot_nt(back, weight_mid_ref[...]) * slope_first).astype(BF16)
        adjoint[part, :] = dot_nt(back, weight_in_ref[...]).astype(BF16)
        which = pl.ds(start, step)
        results += copies(
            out_semaphores.at[pl.ds(1 + len(results), 2)],
            (departures_ref.at[which, lanes], departures_hbm.at[which, lanes]),
            (adjoint.at[which, :], adjoint_hbm.at[which, :]),
        )
    fields = fields_ref[...]
    around = turned_weights(fields, columns)
    row, column, w00, w01, w10, w11 = (fields[index : index + 1, :] for index in range(FIELDS))
    place = iota((rows, slots), 0).astype(F32)
    here, below = place == row, place == row + 1.0
    zero = jnp.zeros((rows, slots), F32)
    weights = [blend(*around, 0), blend(*around, rows - 1)]
    for at, high, low in ((0.0, w00, w10), (columns - 2.0, w01, w11)):
        chosen = column == at
        weights.append(
            jnp.where(here & chosen, high, jnp.where(below & chosen, low, zero)).astype(BF16)
        )
    spread = dot_nn(jnp.concatenate(weights, axis=0), adjoint[...])
    cells_out = []
    for index in range(2):
        first = index * columns
        pulled = ends_ref[index].astype(F32) * spread[first : first + columns]
        lines_ref[index] = pulled.astype(BF16)
        cells_out += [pulled[:1], pulled[columns - 1 :]]
    for index in range(2):
        first = 2 * columns + index * rows
        slope = borders_ref[index * rows : (index + 1) * rows, :]
        sides_ref[index] = (slope * spread[first : first + rows]).astype(BF16)
    results += copies(
        out_semaphores.at[pl.ds(1 + len(results), 4)],
        (sides_ref.at[0], west_hbm),
        (sides_ref.at[1], east_hbm),
        (lines_ref.at[0], top_hbm),
        (lines_ref.at[1], bottom_hbm),
    )
    corners_out(cells_out, lat, lon, capacity, departures_ref, channels)
    results += copies(
        out_semaphores.at[pl.ds(1 + len(results), 1)],
        (departures_ref.at[:, spare], departures_hbm.at[:, spare]),
    )
    fields_out.wait()
    for copy in results:
        copy.wait()


def beside(west, east):
    count = lax.axis_size("lon")
    onward = [(i, (i + 1) % count) for i in range(count)]
    left = lax.ppermute(east, "lon", onward)
    right = lax.ppermute(west, "lon", [(target, source) for source, target in onward])
    return left, right


def over(top, bottom):
    count = lax.axis_size("lat")
    down = [(i, (i + 1) % count) for i in range(count)]
    north = lax.ppermute(bottom, "lat", down)
    south = lax.ppermute(top, "lat", [(target, source) for source, target in down])
    return north, south


def body(
    model_state,
    tangent_slope,
    conv_weight,
    weight_in,
    bias_in,
    weight_mid,
    bias_mid,
    weight_out,
    bias_out,
    obs_tile,
    obs_cell,
    obs_frac,
    radiance,
    inv_error,
):
    rows, columns, channels = model_state.shape
    cells = rows * columns
    devices = lax.axis_size("lat") * lax.axis_size("lon")
    count, bands = radiance.shape
    capacity = 2 * count // devices
    slots = devices * capacity
    hidden = weight_in.shape[1]
    sds = jax.ShapeDtypeStruct
    dma = pltpu.SemaphoreType.DMA

    def exchange(box):
        return lax.all_to_all(
            box.reshape(devices, capacity, -1), ("lat", "lon"), split_axis=0, concat_axis=0, tiled=True
        ).reshape(slots, -1)

    box, slot, west, east, top, bottom = kernel_call(
        functools.partial(dispatch_kernel, capacity),
        (
            sds((slots, bands + META), BF16),
            sds((1, count), jnp.int32),
            sds((rows, channels), BF16),
            sds((rows, channels), BF16),
            sds((columns, channels), BF16),
            sds((columns, channels), BF16),
        ),
        (HBM,) * 6,
        (HBM,) * 5,
        (
            pltpu.VMEM((1, count), jnp.int32),
            pltpu.VMEM((1, count), jnp.int32),
            pltpu.VMEM((2, count), F32),
            pltpu.VMEM((count, bands), BF16),
            pltpu.VMEM((rows, 16, channels), BF16),
            pltpu.VMEM((rows, 16, channels), BF16),
            pltpu.VMEM((slots, bands + META), BF16),
            pltpu.VMEM((1, count), jnp.int32),
            pltpu.VMEM((rows, channels), BF16),
            pltpu.VMEM((rows, channels), BF16),
            pltpu.VMEM((2, columns, channels), BF16),
            dma((8,)),
            dma((7,)),
        ),
        flops=2 * slots * count * (bands + META),
        moved=2 * slots * (bands + META),
        name="dispatch",
    )(obs_tile.reshape(1, count), obs_cell.reshape(1, count), obs_frac.T, radiance, model_state)
    arrived = exchange(box)

    conv_flops = 2 * 9 * cells * channels * channels
    steps = cells // CHUNK
    halo_scratch = (
        pltpu.VMEM((rows, channels), BF16),
        pltpu.VMEM((rows, channels), BF16),
        pltpu.VMEM((columns, channels), BF16),
        pltpu.VMEM((columns, channels), BF16),
    )
    shifted = pltpu.VMEM((3, (rows + 2) * columns, channels), BF16)
    borders_shape = (BORDERS * rows + 2 * columns, channels)
    flat_slope = tangent_slope.reshape(cells, channels)
    halo = beside(west, east) + over(top, bottom)
    forecast, borders = kernel_call(
        functools.partial(forecast_kernel, columns),
        (sds((cells, channels), BF16), sds(borders_shape, F32)),
        (HBM,) * 2,
        (HBM,) * 3,
        (
            pltpu.VMEM((cells, channels), BF16),
            pltpu.VMEM((cells, channels), BF16),
            pltpu.VMEM(conv_weight.shape, BF16),
            pltpu.VMEM((cells, channels), BF16),
            pltpu.VMEM(borders_shape, F32),
            shifted,
            dma((1,)),
            dma((steps,)),
            dma((steps,)),
            dma((steps + 1,)),
        ),
        flops=conv_flops,
        moved=6 * cells * channels,
        room=512,
        name="forecast",
    )(model_state.reshape(cells, channels), flat_slope, conv_weight)

    network_flops = 2 * slots * (channels * hidden + hidden * hidden + hidden * bands)
    departures_box, adjoint, fields, west, east, top, bottom = kernel_call(
        functools.partial(observe_kernel, columns, capacity),
        (
            sds((slots, bands + META), BF16),
            sds((slots, channels), BF16),
            sds((16, slots), F32),
            sds((rows, channels), BF16),
            sds((rows, channels), BF16),
            sds((columns, channels), BF16),
            sds((columns, channels), BF16),
        ),
        (HBM,) * 7,
        (HBM,) * 16,
        (
            pltpu.VMEM((slots, bands + META), BF16),
            pltpu.VMEM((cells, channels), BF16),
            pltpu.VMEM(weight_in.shape, BF16),
            pltpu.VMEM(weight_mid.shape, BF16),
            pltpu.VMEM(weight_out.shape, BF16),
            *(pltpu.VMEM(vector.shape, F32) for vector in (bias_in, bias_mid, bias_out, inv_error)),
            pltpu.VMEM((2, columns, channels), BF16),
            pltpu.VMEM(borders_shape, F32),
            pltpu.VMEM(conv_weight.shape, BF16),
            *halo_scratch,
            pltpu.VMEM((slots, channels), F32),
            pltpu.VMEM((slots, bands + META), BF16),
            pltpu.VMEM((slots, channels), BF16),
            pltpu.VMEM((16, slots), F32),
            pltpu.VMEM((2, rows, channels), BF16),
            pltpu.VMEM((2, columns, channels), BF16),
            dma((18,)),
            dma((10,)),
        ),
        flops=2 * network_flops + 2 * slots * cells * channels,
        moved=2 * cells * channels,
        room=ROOM,
        name="observe",
    )(
        arrived,
        forecast,
        weight_in,
        weight_mid,
        weight_out,
        bias_in,
        bias_mid,
        bias_out,
        inv_error,
        flat_slope,
        borders,
        conv_weight,
        *halo,
    )

    returned = exchange(departures_box)
    halo = beside(west, east) + over(top, bottom)
    gradient, = kernel_call(
        functools.partial(gradient_kernel, columns),
        (sds((cells, channels), F32),),
        (HBM,),
        (VMEM, VMEM, HBM, VMEM),
        (
            pltpu.VMEM((cells, channels), BF16),
            pltpu.VMEM((cells, channels), F32),
            shifted,
            dma((1,)),
            dma((steps,)),
        ),
        flops=conv_flops + 2 * slots * cells * channels,
        moved=4 * cells * channels,
        room=9216,
        name="gradient",
    )(adjoint, fields, flat_slope, conv_weight)
    gradient, departures = kernel_call(
        functools.partial(finish_kernel, capacity),
        (sds((rows, columns, channels), F32), sds((count, bands), F32)),
        (HBM, HBM),
        (HBM, HBM, VMEM) + (HBM,) * 5,
        (
            pltpu.VMEM((1, count), jnp.int32),
            pltpu.VMEM(conv_weight.shape, BF16),
            *halo_scratch,
            pltpu.VMEM((2, columns - 16, channels), F32),
            pltpu.VMEM((2, rows, 8, channels), F32),
            pltpu.VMEM((count, bands), F32),
            dma((11,)),
            dma((6,)),
        ),
        flops=2 * slots * count * bands,
        moved=4 * count * bands,
        aliases={0: 0},
        room=30720,
        name="finish",
    )(gradient.reshape(rows, columns, channels), slot, returned, conv_weight, *halo)
    return departures, gradient


def solution(mesh):
    in_specs = (
        P("lat", "lon", None),
        P("lat", "lon", None),
        P(),
        P(),
        P(),
        P(),
        P(),
        P(),
        P(),
        P(("lat", "lon"), None),
        P(("lat", "lon")),
        P(("lat", "lon"), None),
        P(("lat", "lon"), None),
        P(),
    )
    out_specs = (P(("lat", "lon"), None), P("lat", "lon", None))
    return jax.shard_map(body, mesh=mesh, in_specs=in_specs, out_specs=out_specs, check_vma=False)
```

```python
import functools

import jax
import jax.numpy as jnp
from jax import lax
from jax.experimental import pallas as pl
from jax.experimental.pallas import tpu as pltpu
from jax.sharding import PartitionSpec as P

F32 = jnp.float32
BF16 = jnp.bfloat16
META = 128
FIELDS = 6
VMEM_KIB = 60 * 1024 + 512
ROOM = 1024 + 256


def dot_nt(left, right):
    return lax.dot_general(left, right, (((1,), (1,)), ((), ())), preferred_element_type=F32)


def dot_nn(left, right):
    return jnp.dot(left, right, preferred_element_type=F32)


def iota(shape, dim):
    return lax.broadcasted_iota(jnp.int32, shape, dim)


def kernel_call(body, outs, out_spaces, in_spaces, scratch=(), flops=0, moved=0, room=0, aliases=None, name=None):
    return pl.pallas_call(
        body,
        out_shape=outs,
        in_specs=[pl.BlockSpec(memory_space=space) for space in in_spaces],
        out_specs=[pl.BlockSpec(memory_space=space) for space in out_spaces],
        scratch_shapes=list(scratch),
        input_output_aliases=aliases or {},
        name=name,
        compiler_params=pltpu.CompilerParams(vmem_limit_bytes=(VMEM_KIB - room) * 1024),
        cost_estimate=pl.CostEstimate(flops=flops, bytes_accessed=moved, transcendentals=0),
    )


HBM = pltpu.HBM
VMEM = pltpu.VMEM


def copies(semaphores, *pairs):
    started = []
    for index, (source, target) in enumerate(pairs):
        copy = pltpu.make_async_copy(source, target, semaphores.at[index])
        copy.start()
        started.append(copy)
    return started


CORNER_LANE = 32
CORNER_WIDTH = 32


def diagonal_blocks(lat, lon, capacity):
    lats, lons = lax.axis_size("lat"), lax.axis_size("lon")
    blocks = []
    for down, right in ((-1, -1), (-1, 1), (1, -1), (1, 1)):
        row, column = lat + down, lax.rem(lon + right + lons, lons)
        inside = (row >= 0) & (row < lats)
        first = jnp.where(inside, row * lons + column, 0) * capacity
        aligned = pl.multiple_of((first // 16) * 16, 16)
        blocks.append((inside, aligned, lax.rem(first, 16)))
    return blocks


def corner_fold(shape, lane_dim):
    value, lane = iota(shape, 1 - lane_dim), iota(shape, lane_dim)
    chosen = (value % CORNER_WIDTH == lane - CORNER_LANE) & (lane >= CORNER_LANE)
    return (chosen & (lane < CORNER_LANE + CORNER_WIDTH)).astype(F32).astype(BF16)


def corner_mask(shape):
    return iota(shape, 1) // CORNER_WIDTH == iota(shape, 0) % 8


def corners_out(cells, lat, lon, capacity, box_ref, channels):
    width = cells[0].shape[1]
    spread = jnp.concatenate([jnp.broadcast_to(cell, (8, width)) for cell in cells], axis=0)
    kept = jnp.where(corner_mask(spread.shape), spread, 0.0).astype(BF16)
    folded = dot_nn(kept, corner_fold((width, META), 1))
    half = (iota((16, META), 0) // 8) * 8
    for index, (inside, first, own) in enumerate(diagonal_blocks(lat, lon, capacity)):
        lines = folded[8 * index : 8 * index + 8]
        lines = jnp.where((half == own) & inside, jnp.concatenate([lines, lines], axis=0), 0.0)
        which = pl.ds(first, 16)
        box_ref[which, channels:] = (box_ref[which, channels:].astype(F32) + lines).astype(BF16)


def corners_in(box_ref, lat, lon, capacity, channels, width):
    lines = []
    for inside, first, own in diagonal_blocks(lat, lon, capacity):
        block = box_ref[pl.ds(first, 16), channels:].astype(F32)
        mine = jnp.where(own == 0, block[:8], block[8:])
        lines.append(jnp.where(inside, mine, 0.0))
    folded = jnp.concatenate(lines, axis=0).astype(BF16)
    spread = dot_nn(folded, corner_fold((META, width), 0))
    kept = jnp.where(corner_mask(spread.shape), spread, 0.0)
    return [jnp.sum(kept[8 * index : 8 * index + 8], axis=0, keepdims=True) for index in range(4)]


def dispatch_kernel(
    capacity,
    tile_hbm,
    cell_hbm,
    frac_hbm,
    radiance_hbm,
    state_hbm,
    box_hbm,
    slot_hbm,
    west_hbm,
    east_hbm,
    top_hbm,
    bottom_hbm,
    tile_ref,
    cell_ref,
    frac_ref,
    radiance_ref,
    first_ref,
    last_ref,
    box_ref,
    slot_ref,
    west_ref,
    east_ref,
    lines_ref,
    semaphores,
    out_semaphores,
):
    rows, columns, _ = state_hbm.shape
    lat, lon = lax.axis_index("lat"), lax.axis_index("lon")
    waiting = copies(
        semaphores,
        (tile_hbm, tile_ref),
        (cell_hbm, cell_ref),
        (frac_hbm, frac_ref),
        (radiance_hbm, radiance_ref),
        (state_hbm.at[:, pl.ds(0, 16), :], first_ref),
        (state_hbm.at[:, pl.ds(columns - 16, 16), :], last_ref),
        (state_hbm.at[0], lines_ref.at[0]),
        (state_hbm.at[rows - 1], lines_ref.at[1]),
    )
    slots, width = box_ref.shape
    devices = slots // capacity
    count = tile_ref.shape[1]
    channels = width - META
    earlier = (iota((count, count), 0) < iota((count, count), 1)).astype(F32).astype(BF16)
    for copy in waiting[:3]:
        copy.wait()
    tile = tile_ref[...]
    match = (iota((devices, count), 0) == tile).astype(F32)
    before = dot_nn(match.astype(BF16), earlier)
    position = jnp.sum(before * match, axis=0, keepdims=True)
    slot = tile * capacity + position.astype(jnp.int32)
    slot_ref[...] = slot
    leaving = [pltpu.make_async_copy(slot_ref, slot_hbm, out_semaphores.at[0])]
    leaving[0].start()
    cell = cell_ref[...]
    low, side = frac_ref[0:1, :], frac_ref[1:2, :]
    fields = (
        (cell >> 7).astype(F32),
        (cell & 127).astype(F32),
        (1.0 - low) * (1.0 - side),
        (1.0 - low) * side,
        low * (1.0 - side),
        low * side,
    )
    number = iota((META, count), 0)
    meta = jnp.zeros((META, count), F32)
    for index, field in enumerate(fields):
        meta = jnp.where(number == index, field, meta)
    meta = meta.astype(BF16)
    for copy in waiting[4:]:
        copy.wait()
    for index, line_hbm in enumerate((top_hbm, bottom_hbm)):
        leaving.append(
            pltpu.make_async_copy(lines_ref.at[index], line_hbm, out_semaphores.at[len(leaving)])
        )
        leaving[-1].start()
    cells = []
    for block_ref, at, side_ref, side_hbm in (
        (first_ref, 0, west_ref, west_hbm),
        (last_ref, 15, east_ref, east_hbm),
    ):
        lines = [block_ref[row].astype(F32)[at : at + 1] for row in range(rows)]
        cells += [lines[0], lines[-1]]
        side_ref[...] = jnp.concatenate(lines, axis=0).astype(BF16)
        leaving.append(
            pltpu.make_async_copy(side_ref, side_hbm, out_semaphores.at[len(leaving)])
        )
        leaving[-1].start()
    cells = (cells[0], cells[2], cells[1], cells[3])
    places = []
    step = slots // 4
    for index in range(4):
        part = slice(index * step, (index + 1) * step)
        places.append((iota((step, count), 0) + index * step == slot).astype(F32).astype(BF16))
        box_ref[part, channels:] = dot_nt(places[index], meta).astype(BF16)
    corners_out(cells, lat, lon, capacity, box_ref, channels)
    waiting[3].wait()
    for index in range(4):
        part = slice(index * step, (index + 1) * step)
        box_ref[part, :channels] = dot_nn(places[index], radiance_ref[...]).astype(BF16)
        leaving.append(
            pltpu.make_async_copy(
                box_ref.at[part, :], box_hbm.at[part, :], out_semaphores.at[len(leaving)]
            )
        )
        leaving[-1].start()
    for copy in leaving:
        copy.wait()


CHUNK = 512
FORECAST_GROUPS = (0, 2, 6, 8)
GRADIENT_GROUPS = (0, 4, 8)
SPREAD_AHEAD = 6


def fill_row(shifted, row, center, left, right):
    columns = center.shape[0]
    place = iota(center.shape, 0)
    where = pl.ds(row * columns, columns)
    shifted[1, where, :] = center.astype(BF16)
    shifted[0, where, :] = jnp.where(place == 0, left, pltpu.roll(center, 1, 0)).astype(BF16)
    shifted[2, where, :] = jnp.where(
        place == columns - 1, right, pltpu.roll(center, columns - 1, 0)
    ).astype(BF16)


def no_halo_rows(shifted, rows, columns):
    zero = jnp.zeros((3, columns, shifted.shape[2]), BF16)
    shifted[:, :columns, :] = zero
    shifted[:, (rows + 1) * columns :, :] = zero


def halo_terms(left, right, north, south, corners, weight_ref, mirror):
    rows, columns = left.shape[0], north.shape[0]
    lat = lax.axis_index("lat")
    north = jnp.where(lat > 0, north, 0.0)
    south = jnp.where(lat < lax.axis_size("lat") - 1, south, 0.0)
    product, weight_of = taps(weight_ref, mirror)

    def row_windows(center, first, last):
        place = iota(center.shape, 0)
        west = jnp.where(place == 0, first, pltpu.roll(center, 1, 0))
        east = jnp.where(place == columns - 1, last, pltpu.roll(center, columns - 1, 0))
        return west, center, east

    def column_windows(side):
        place = iota(side.shape, 0)
        up = jnp.where(place == 0, 0.0, pltpu.roll(side, 1, 0))
        down = jnp.where(place == rows - 1, 0.0, pltpu.roll(side, rows - 1, 0))
        return up, side, down

    lines = {0: row_windows(north, *corners[:2]), 2: row_windows(south, *corners[2:])}
    sides = {0: column_windows(left), 2: column_windows(right)}
    line_terms, side_terms = {0: 0.0, 2: 0.0}, {0: 0.0, 2: 0.0}
    for row_step in range(3):
        for col_step in range(3):
            windows = []
            if row_step != 1:
                windows.append(lines[row_step][col_step])
            if col_step != 1:
                windows.append(sides[col_step][row_step])
            if not windows:
                continue
            term = product(
                jnp.concatenate(windows, axis=0).astype(BF16), weight_of(row_step, col_step)
            )
            if row_step != 1:
                line_terms[row_step] += term[:columns]
            if col_step != 1:
                side_terms[col_step] += term[-rows:]
    top, bottom, west, east = line_terms[0], line_terms[2], side_terms[0], side_terms[2]
    return top, bottom, west, east


def with_ends(term, first, last):
    place = iota(term.shape, 0)
    ends = jnp.where(place == 0, first, jnp.where(place == term.shape[0] - 1, last, 0.0))
    return term + ends


def taps(weight_ref, mirror):
    if mirror:
        return dot_nt, lambda row_step, col_step: weight_ref[2 - row_step, 2 - col_step]
    return dot_nn, lambda row_step, col_step: weight_ref[row_step, col_step]


def convolve_rows(shifted, weight_ref, start, count, columns, mirror):
    product, weight_of = taps(weight_ref, mirror)
    total = None
    for row_step in range(3):
        for col_step in range(3):
            first = start + row_step * columns
            term = product(shifted[col_step, first : first + count, :], weight_of(row_step, col_step))
            total = term if total is None else total + term
    return total


def span_copy(source, target, semaphore, first, last):
    which = pl.ds(first * CHUNK, (last - first) * CHUNK)
    return pltpu.make_async_copy(source.at[which, :], target.at[which, :], semaphore)


BORDERS = 4


def forecast_kernel(
    columns,
    state_hbm,
    slope_hbm,
    weight_hbm,
    out_hbm,
    borders_hbm,
    state_ref,
    slope_ref,
    weight_ref,
    out_ref,
    borders_ref,
    shifted,
    weight_semaphore,
    state_semaphores,
    slope_semaphores,
    out_semaphores,
):
    cells, channels = state_ref.shape
    rows = cells // columns
    per = CHUNK // columns
    steps = cells // CHUNK
    zero = jnp.zeros((1, channels), F32)
    groups = list(zip(FORECAST_GROUPS[:-1], FORECAST_GROUPS[1:]))

    def copies_in(number):
        first, last = groups[number]
        ahead = (first + 1 if number else 0), min(last + 1, steps)
        found = [
            span_copy(slope_hbm, slope_ref, slope_semaphores.at[number], first, last)
        ]
        if ahead[0] < ahead[1]:
            found.append(span_copy(state_hbm, state_ref, state_semaphores.at[number], *ahead))
        if number == 0:
            found.append(pltpu.make_async_copy(weight_hbm, weight_ref, weight_semaphore.at[0]))
        return found[::-1]

    def fill(index):
        for row in range(index * per, (index + 1) * per):
            center = state_ref[row * columns : (row + 1) * columns, :].astype(F32)
            fill_row(shifted, row + 1, center, zero, zero)

    coming = copies_in(0)
    for copy in coming:
        copy.start()
    no_halo_rows(shifted, rows, columns)
    out = []
    for number, (low, high) in enumerate(groups):
        for copy in coming:
            copy.wait()
        if number + 1 < len(groups):
            coming = copies_in(number + 1)
            for copy in coming:
                copy.start()
        if number == 0:
            fill(0)
        for index in range(low, high):
            if index + 1 < steps:
                fill(index + 1)
            part = slice(index * CHUNK, (index + 1) * CHUNK)
            response = convolve_rows(shifted, weight_ref, part.start, CHUNK, columns, False)
            slope = slope_ref[part, :].astype(F32)
            total = state_ref[part, :].astype(F32) + slope * response
            out_ref[part, :] = total.astype(BF16)
            for inner in range(per):
                row = index * per + inner
                first, last = inner * columns, (inner + 1) * columns - 1
                for kind, line in enumerate(
                    (slope[first : first + 1], slope[last : last + 1])
                    + (total[first : first + 1], total[last : last + 1])
                ):
                    at = kind * rows + row
                    borders_ref[at : at + 1, :] = line
            if index == 0:
                borders_ref[BORDERS * rows : BORDERS * rows + columns, :] = total[:columns]
            if index == steps - 1:
                borders_ref[BORDERS * rows + columns :, :] = total[CHUNK - columns :]
        out.append(span_copy(out_ref, out_hbm, out_semaphores.at[number], low, high))
        out[-1].start()
    out.append(pltpu.make_async_copy(borders_ref, borders_hbm, out_semaphores.at[steps]))
    out[-1].start()
    for copy in out:
        copy.wait()


def gradient_kernel(
    columns,
    adjoint,
    fields_ref,
    slope_hbm,
    weight_ref,
    out_hbm,
    slope_ref,
    out_ref,
    shifted,
    slope_semaphore,
    out_semaphores,
):
    cells, channels = slope_ref.shape
    rows = cells // columns
    per = CHUNK // columns
    steps = cells // CHUNK
    zero = jnp.zeros((1, channels), F32)
    groups = list(zip(GRADIENT_GROUPS[:-1], GRADIENT_GROUPS[1:]))

    slope_in = copies(slope_semaphore, (slope_hbm, slope_ref))[0]
    no_halo_rows(shifted, rows, columns)
    around = turned_weights(fields_ref[...], columns)

    def spread(index):
        weights = [blend(*around, index * per + row) for row in range(per)]
        out_ref[index * CHUNK : (index + 1) * CHUNK, :] = dot_nn(
            jnp.concatenate(weights, axis=0), adjoint[...]
        )

    def fill(index):
        part = slice(index * CHUNK, (index + 1) * CHUNK)
        pulled = slope_ref[part, :].astype(F32) * out_ref[part, :]
        for inner in range(per):
            center = pulled[inner * columns : (inner + 1) * columns, :]
            fill_row(shifted, index * per + inner + 1, center, zero, zero)

    for index in range(SPREAD_AHEAD):
        spread(index)
    slope_in.wait()
    out = []
    for number, (low, high) in enumerate(groups):
        if number == 0:
            fill(0)
        for index in range(low, high):
            if index + 1 < steps:
                if index + 1 >= SPREAD_AHEAD:
                    spread(index + 1)
                fill(index + 1)
            part = slice(index * CHUNK, (index + 1) * CHUNK)
            out_ref[part, :] += convolve_rows(shifted, weight_ref, part.start, CHUNK, columns, True)
        out.append(span_copy(out_ref, out_hbm, out_semaphores.at[number], low, high))
        out[-1].start()
    for copy in out:
        copy.wait()


def finish_kernel(
    capacity,
    gradient_hbm,
    slot_hbm,
    box_ref,
    weight_hbm,
    left_hbm,
    right_hbm,
    north_hbm,
    south_hbm,
    out_hbm,
    departures_hbm,
    slot_ref,
    weight_ref,
    left_ref,
    right_ref,
    north_ref,
    south_ref,
    lines_ref,
    sides_ref,
    departures_ref,
    semaphores,
    out_semaphores,
):
    del gradient_hbm
    lat, lon = lax.axis_index("lat"), lax.axis_index("lon")
    rows, columns, cell_channels = out_hbm.shape
    inner = pl.ds(8, columns - 16)
    places = (
        (lines_ref.at[0], out_hbm.at[0, inner, :]),
        (lines_ref.at[1], out_hbm.at[rows - 1, inner, :]),
        (sides_ref.at[0], out_hbm.at[:, pl.ds(0, 8), :]),
        (sides_ref.at[1], out_hbm.at[:, pl.ds(columns - 8, 8), :]),
    )
    waiting = copies(
        semaphores,
        (slot_hbm, slot_ref),
        (weight_hbm, weight_ref),
        (left_hbm, left_ref),
        (right_hbm, right_ref),
        (north_hbm, north_ref),
        (south_hbm, south_ref),
        *((there, here) for here, there in places),
    )
    slots = box_ref.shape[0]
    count = slot_ref.shape[1]
    channels = box_ref.shape[1] - META
    waiting[0].wait()
    turned = jnp.broadcast_to(slot_ref[...].astype(F32), (128, count)).T
    lane = iota((count, 128), 1).astype(F32)
    parts = [
        (lane + float(first) == turned).astype(F32).astype(BF16) for first in range(0, slots, 128)
    ]
    place = jnp.concatenate(parts, axis=1)
    step = count // 2
    leaving = []
    for index in range(2):
        part = slice(index * step, (index + 1) * step)
        departures_ref[part, :] = dot_nn(place[part, :], box_ref[:, :channels])
        leaving.append(
            pltpu.make_async_copy(
                departures_ref.at[part, :], departures_hbm.at[part, :], out_semaphores.at[4 + index]
            )
        )
        leaving[-1].start()
    for copy in waiting[1:6]:
        copy.wait()
    top, bottom, west, east = halo_terms(
        left_ref[...].astype(F32),
        right_ref[...].astype(F32),
        north_ref[...].astype(F32),
        south_ref[...].astype(F32),
        corners_in(box_ref, lat, lon, capacity, channels, cell_channels),
        weight_ref,
        True,
    )
    for copy in waiting[6:]:
        copy.wait()
    lines_ref[0] += top[8 : columns - 8]
    lines_ref[1] += bottom[8 : columns - 8]
    leaving += copies(out_semaphores, *places[:2])
    place = iota((8, cell_channels), 0)
    for number, side, at in ((0, west, 0), (1, east, 7)):
        ends = (top[:8], bottom[:8]) if number == 0 else (top[-8:], bottom[-8:])
        for row in range(rows):
            term = jnp.where(place == at, side[row : row + 1], 0.0)
            if row == 0:
                term = term + ends[0]
            if row == rows - 1:
                term = term + ends[1]
            sides_ref[number, row] += term
        leaving.append(pltpu.make_async_copy(*places[2 + number], out_semaphores.at[2 + number]))
        leaving[-1].start()
    for copy in leaving:
        copy.wait()


def sigmoid(value):
    return 0.5 + 0.5 * jnp.tanh(0.5 * value)


def blend(row_low, row_high, upper, lower, at):
    at = jnp.asarray(at, BF16)
    zero = jnp.zeros(upper.shape, BF16)
    return jnp.where(row_low == at, upper, jnp.where(row_high == at, lower, zero))


def turned_weights(fields, columns):
    slots = fields.shape[1]
    row, column, w00, w01, w10, w11 = (fields[index : index + 1, :] for index in range(FIELDS))
    place = iota((columns, slots), 0).astype(F32)
    here, beside = place == column, place == column + 1.0
    upper = (jnp.where(here, w00, 0.0) + jnp.where(beside, w01, 0.0)).astype(BF16)
    lower = (jnp.where(here, w10, 0.0) + jnp.where(beside, w11, 0.0)).astype(BF16)
    row_low = jnp.broadcast_to(row, (columns, slots)).astype(BF16)
    row_high = jnp.broadcast_to(row + 1.0, (columns, slots)).astype(BF16)
    return row_low, row_high, upper, lower


def observe_kernel(
    columns,
    capacity,
    box_hbm,
    grid_hbm,
    weight_in_hbm,
    weight_mid_hbm,
    weight_out_hbm,
    bias_in_hbm,
    bias_mid_hbm,
    bias_out_hbm,
    inv_error_hbm,
    slope_hbm,
    borders_hbm,
    conv_hbm,
    left_hbm,
    right_hbm,
    north_hbm,
    south_hbm,
    departures_hbm,
    adjoint_hbm,
    fields_hbm,
    west_hbm,
    east_hbm,
    top_hbm,
    bottom_hbm,
    box_ref,
    grid_ref,
    weight_in_ref,
    weight_mid_ref,
    weight_out_ref,
    bias_in_ref,
    bias_mid_ref,
    bias_out_ref,
    inv_error_ref,
    ends_ref,
    borders_ref,
    conv_ref,
    left_ref,
    right_ref,
    north_ref,
    south_ref,
    sampled,
    departures_ref,
    adjoint,
    fields_ref,
    sides_ref,
    lines_ref,
    semaphores,
    out_semaphores,
):
    lat, lon = lax.axis_index("lat"), lax.axis_index("lon")
    slots, width = box_ref.shape
    cells, grid_channels = grid_ref.shape
    channels = width - META
    hidden = weight_in_ref.shape[1]
    rows = cells // columns
    lanes, spare = pl.ds(0, channels), pl.ds(channels, META)
    waiting = copies(
        semaphores,
        (box_hbm.at[:, spare], box_ref.at[:, spare]),
        (left_hbm, left_ref),
        (right_hbm, right_ref),
        (north_hbm, north_ref),
        (south_hbm, south_ref),
        (conv_hbm, conv_ref),
        (grid_hbm, grid_ref),
        (slope_hbm.at[pl.ds(0, columns), :], ends_ref.at[0]),
        (slope_hbm.at[pl.ds(cells - columns, columns), :], ends_ref.at[1]),
        (borders_hbm, borders_ref),
        (weight_in_hbm, weight_in_ref),
        (bias_in_hbm, bias_in_ref),
        (bias_mid_hbm, bias_mid_ref),
        (bias_out_hbm, bias_out_ref),
        (inv_error_hbm, inv_error_ref),
        (weight_mid_hbm, weight_mid_ref),
        (weight_out_hbm, weight_out_ref),
        (box_hbm.at[:, lanes], box_ref.at[:, lanes]),
    )
    waiting[0].wait()
    pick = (iota((16, META), 0) == iota((16, META), 1)).astype(F32).astype(BF16)
    fields_ref[...] = dot_nt(pick, box_ref[:, channels:])
    fields_out = pltpu.make_async_copy(fields_ref, fields_hbm, out_semaphores.at[0])
    fields_out.start()
    pick = iota((META, FIELDS * columns), 0) == iota((META, FIELDS * columns), 1) // columns
    wide = dot_nn(box_ref[:, channels:], pick.astype(F32).astype(BF16))
    row, column, w00, w01, w10, w11 = (
        wide[:, index * columns : (index + 1) * columns] for index in range(FIELDS)
    )
    lane = iota((slots, columns), 1).astype(F32)
    here, beside = lane == column, lane == column + 1.0
    upper = (jnp.where(here, w00, 0.0) + jnp.where(beside, w01, 0.0)).astype(BF16)
    lower = (jnp.where(here, w10, 0.0) + jnp.where(beside, w11, 0.0)).astype(BF16)
    row_low = row.astype(BF16)
    row_high = (row + 1.0).astype(BF16)
    for copy in waiting[1:6]:
        copy.wait()
    top, bottom, west, east = halo_terms(
        left_ref[...].astype(F32),
        right_ref[...].astype(F32),
        north_ref[...].astype(F32),
        south_ref[...].astype(F32),
        corners_in(box_ref, lat, lon, capacity, channels, grid_channels),
        conv_ref,
        False,
    )
    departures_ref[:, channels:] = jnp.zeros((slots, META), BF16)
    for copy in waiting[6:10]:
        copy.wait()
    place = iota((16, grid_channels), 0)
    for number, side, others, at, first in (
        (0, west, (top[:1], bottom[:1]), 0, 0),
        (1, east, (top[-1:], bottom[-1:]), 15, columns - 16),
    ):
        slope = borders_ref[number * rows : (number + 1) * rows, :]
        value = borders_ref[(number + 2) * rows : (number + 3) * rows, :]
        value = value + slope * with_ends(side, *others)
        for row in range(rows):
            part = slice(row * columns + first, row * columns + first + 16)
            grid_ref[part, :] = jnp.where(
                place == at, value[row : row + 1], grid_ref[part, :].astype(F32)
            ).astype(BF16)
    for number, line, at in ((0, top, 0), (1, bottom, rows - 1)):
        first = BORDERS * rows + number * columns
        line = with_ends(line, west[at : at + 1], east[at : at + 1])
        grid_ref[at * columns : (at + 1) * columns, :] = (
            borders_ref[first : first + columns, :] + ends_ref[number].astype(F32) * line
        ).astype(BF16)
    strip = 256
    for start in range(0, slots, strip):
        part = slice(start, start + strip)
        parts = [blend(row_low[part], row_high[part], upper[part], lower[part], at) for at in range(rows)]
        sampled[part, :] = dot_nn(jnp.concatenate(parts, axis=1), grid_ref[...])
    for copy in waiting[10:]:
        copy.wait()
    bias_in, bias_mid, bias_out, inv_error = (
        ref[...].reshape(1, -1) for ref in (bias_in_ref, bias_mid_ref, bias_out_ref, inv_error_ref)
    )
    step = 512
    results = []
    for start in range(0, slots, step):
        part = slice(start, start + step)
        pre = dot_nn(sampled[part, :].astype(BF16), weight_in_ref[...]) + bias_in
        gate = sigmoid(pre)
        act = pre * gate
        slope_first = gate + act * (1.0 - gate)
        pre = dot_nn(act.astype(BF16), weight_mid_ref[...]) + bias_mid
        gate = sigmoid(pre)
        act = pre * gate
        slope_second = gate + act * (1.0 - gate)
        evolved = dot_nn(act.astype(BF16), weight_out_ref[...]) + bias_out
        departures = (evolved - box_ref[part, :channels].astype(F32)) * inv_error
        departures_ref[part, :channels] = departures.astype(BF16)
        back = (departures * inv_error).astype(BF16)
        back = (dot_nt(back, weight_out_ref[...]) * slope_second).astype(BF16)
        back = (dot_nt(back, weight_mid_ref[...]) * slope_first).astype(BF16)
        adjoint[part, :] = dot_nt(back, weight_in_ref[...]).astype(BF16)
        which = pl.ds(start, step)
        results += copies(
            out_semaphores.at[pl.ds(1 + len(results), 2)],
            (departures_ref.at[which, lanes], departures_hbm.at[which, lanes]),
            (adjoint.at[which, :], adjoint_hbm.at[which, :]),
        )
    fields = fields_ref[...]
    around = turned_weights(fields, columns)
    row, column, w00, w01, w10, w11 = (fields[index : index + 1, :] for index in range(FIELDS))
    place = iota((rows, slots), 0).astype(F32)
    here, below = place == row, place == row + 1.0
    zero = jnp.zeros((rows, slots), F32)
    weights = [blend(*around, 0), blend(*around, rows - 1)]
    for at, high, low in ((0.0, w00, w10), (columns - 2.0, w01, w11)):
        chosen = column == at
        weights.append(
            jnp.where(here & chosen, high, jnp.where(below & chosen, low, zero)).astype(BF16)
        )
    spread = dot_nn(jnp.concatenate(weights, axis=0), adjoint[...])
    cells_out = []
    for index in range(2):
        first = index * columns
        pulled = ends_ref[index].astype(F32) * spread[first : first + columns]
        lines_ref[index] = pulled.astype(BF16)
        cells_out += [pulled[:1], pulled[columns - 1 :]]
    for index in range(2):
        first = 2 * columns + index * rows
        slope = borders_ref[index * rows : (index + 1) * rows, :]
        sides_ref[index] = (slope * spread[first : first + rows]).astype(BF16)
    results += copies(
        out_semaphores.at[pl.ds(1 + len(results), 4)],
        (sides_ref.at[0], west_hbm),
        (sides_ref.at[1], east_hbm),
        (lines_ref.at[0], top_hbm),
        (lines_ref.at[1], bottom_hbm),
    )
    corners_out(cells_out, lat, lon, capacity, departures_ref, channels)
    results += copies(
        out_semaphores.at[pl.ds(1 + len(results), 1)],
        (departures_ref.at[:, spare], departures_hbm.at[:, spare]),
    )
    fields_out.wait()
    for copy in results:
        copy.wait()


def beside(west, east):
    count = lax.axis_size("lon")
    onward = [(i, (i + 1) % count) for i in range(count)]
    left = lax.ppermute(east, "lon", onward)
    right = lax.ppermute(west, "lon", [(target, source) for source, target in onward])
    return left, right


def over(top, bottom):
    count = lax.axis_size("lat")
    down = [(i, (i + 1) % count) for i in range(count)]
    north = lax.ppermute(bottom, "lat", down)
    south = lax.ppermute(top, "lat", [(target, source) for source, target in down])
    return north, south


def body(
    model_state,
    tangent_slope,
    conv_weight,
    weight_in,
    bias_in,
    weight_mid,
    bias_mid,
    weight_out,
    bias_out,
    obs_tile,
    obs_cell,
    obs_frac,
    radiance,
    inv_error,
):
    rows, columns, channels = model_state.shape
    cells = rows * columns
    devices = lax.axis_size("lat") * lax.axis_size("lon")
    count, bands = radiance.shape
    capacity = 2 * count // devices
    slots = devices * capacity
    hidden = weight_in.shape[1]
    sds = jax.ShapeDtypeStruct
    dma = pltpu.SemaphoreType.DMA

    def exchange(box):
        return lax.all_to_all(
            box.reshape(devices, capacity, -1), ("lat", "lon"), split_axis=0, concat_axis=0, tiled=True
        ).reshape(slots, -1)

    box, slot, west, east, top, bottom = kernel_call(
        functools.partial(dispatch_kernel, capacity),
        (
            sds((slots, bands + META), BF16),
            sds((1, count), jnp.int32),
            sds((rows, channels), BF16),
            sds((rows, channels), BF16),
            sds((columns, channels), BF16),
            sds((columns, channels), BF16),
        ),
        (HBM,) * 6,
        (HBM,) * 5,
        (
            pltpu.VMEM((1, count), jnp.int32),
            pltpu.VMEM((1, count), jnp.int32),
            pltpu.VMEM((2, count), F32),
            pltpu.VMEM((count, bands), BF16),
            pltpu.VMEM((rows, 16, channels), BF16),
            pltpu.VMEM((rows, 16, channels), BF16),
            pltpu.VMEM((slots, bands + META), BF16),
            pltpu.VMEM((1, count), jnp.int32),
            pltpu.VMEM((rows, channels), BF16),
            pltpu.VMEM((rows, channels), BF16),
            pltpu.VMEM((2, columns, channels), BF16),
            dma((8,)),
            dma((9,)),
        ),
        flops=2 * slots * count * (bands + META),
        moved=2 * slots * (bands + META),
        name="dispatch",
    )(obs_tile.reshape(1, count), obs_cell.reshape(1, count), obs_frac.T, radiance, model_state)
    arrived = exchange(box)

    conv_flops = 2 * 9 * cells * channels * channels
    steps = cells // CHUNK
    halo_scratch = (
        pltpu.VMEM((rows, channels), BF16),
        pltpu.VMEM((rows, channels), BF16),
        pltpu.VMEM((columns, channels), BF16),
        pltpu.VMEM((columns, channels), BF16),
    )
    shifted = pltpu.VMEM((3, (rows + 2) * columns, channels), BF16)
    borders_shape = (BORDERS * rows + 2 * columns, channels)
    flat_slope = tangent_slope.reshape(cells, channels)
    halo = beside(west, east) + over(top, bottom)
    forecast, borders = kernel_call(
        functools.partial(forecast_kernel, columns),
        (sds((cells, channels), BF16), sds(borders_shape, F32)),
        (HBM,) * 2,
        (HBM,) * 3,
        (
            pltpu.VMEM((cells, channels), BF16),
            pltpu.VMEM((cells, channels), BF16),
            pltpu.VMEM(conv_weight.shape, BF16),
            pltpu.VMEM((cells, channels), BF16),
            pltpu.VMEM(borders_shape, F32),
            shifted,
            dma((1,)),
            dma((steps,)),
            dma((steps,)),
            dma((steps + 1,)),
        ),
        flops=conv_flops,
        moved=6 * cells * channels,
        room=512,
        name="forecast",
    )(model_state.reshape(cells, channels), flat_slope, conv_weight)

    network_flops = 2 * slots * (channels * hidden + hidden * hidden + hidden * bands)
    departures_box, adjoint, fields, west, east, top, bottom = kernel_call(
        functools.partial(observe_kernel, columns, capacity),
        (
            sds((slots, bands + META), BF16),
            sds((slots, channels), BF16),
            sds((16, slots), F32),
            sds((rows, channels), BF16),
            sds((rows, channels), BF16),
            sds((columns, channels), BF16),
            sds((columns, channels), BF16),
        ),
        (HBM,) * 7,
        (HBM,) * 16,
        (
            pltpu.VMEM((slots, bands + META), BF16),
            pltpu.VMEM((cells, channels), BF16),
            pltpu.VMEM(weight_in.shape, BF16),
            pltpu.VMEM(weight_mid.shape, BF16),
            pltpu.VMEM(weight_out.shape, BF16),
            *(pltpu.VMEM(vector.shape, F32) for vector in (bias_in, bias_mid, bias_out, inv_error)),
            pltpu.VMEM((2, columns, channels), BF16),
            pltpu.VMEM(borders_shape, F32),
            pltpu.VMEM(conv_weight.shape, BF16),
            *halo_scratch,
            pltpu.VMEM((slots, channels), F32),
            pltpu.VMEM((slots, bands + META), BF16),
            pltpu.VMEM((slots, channels), BF16),
            pltpu.VMEM((16, slots), F32),
            pltpu.VMEM((2, rows, channels), BF16),
            pltpu.VMEM((2, columns, channels), BF16),
            dma((18,)),
            dma((10,)),
        ),
        flops=2 * network_flops + 2 * slots * cells * channels,
        moved=2 * cells * channels,
        room=ROOM,
        name="observe",
    )(
        arrived,
        forecast,
        weight_in,
        weight_mid,
        weight_out,
        bias_in,
        bias_mid,
        bias_out,
        inv_error,
        flat_slope,
        borders,
        conv_weight,
        *halo,
    )

    returned = exchange(departures_box)
    halo = beside(west, east) + over(top, bottom)
    gradient, = kernel_call(
        functools.partial(gradient_kernel, columns),
        (sds((cells, channels), F32),),
        (HBM,),
        (VMEM, VMEM, HBM, VMEM),
        (
            pltpu.VMEM((cells, channels), BF16),
            pltpu.VMEM((cells, channels), F32),
            shifted,
            dma((1,)),
            dma((steps,)),
        ),
        flops=conv_flops + 2 * slots * cells * channels,
        moved=4 * cells * channels,
        room=9216,
        name="gradient",
    )(adjoint, fields, flat_slope, conv_weight)
    gradient, departures = kernel_call(
        functools.partial(finish_kernel, capacity),
        (sds((rows, columns, channels), F32), sds((count, bands), F32)),
        (HBM, HBM),
        (HBM, HBM, VMEM) + (HBM,) * 5,
        (
            pltpu.VMEM((1, count), jnp.int32),
            pltpu.VMEM(conv_weight.shape, BF16),
            *halo_scratch,
            pltpu.VMEM((2, columns - 16, channels), F32),
            pltpu.VMEM((2, rows, 8, channels), F32),
            pltpu.VMEM((count, bands), F32),
            dma((11,)),
            dma((6,)),
        ),
        flops=2 * slots * count * bands,
        moved=4 * count * bands,
        aliases={0: 0},
        room=30720,
        name="finish",
    )(gradient.reshape(rows, columns, channels), slot, returned, conv_weight, *halo)
    return departures, gradient


def solution(mesh):
    in_specs = (
        P("lat", "lon", None),
        P("lat", "lon", None),
        P(),
        P(),
        P(),
        P(),
        P(),
        P(),
        P(),
        P(("lat", "lon"), None),
        P(("lat", "lon")),
        P(("lat", "lon"), None),
        P(("lat", "lon"), None),
        P(),
    )
    out_specs = (P(("lat", "lon"), None), P("lat", "lon", None))
    return jax.shard_map(body, mesh=mesh, in_specs=in_specs, out_specs=out_specs, check_vma=False)
```
